32 devices in a mesh: dp: 4 (over y, x), chan: 8 (over z, core).
Axes of the slice: x: 2, y: 2, z: 4, core: 2. Of those that a mesh axis runs over, the one named last changes fastest.
Arguments:
- x_in: bfloat16 [4, 48, 360, 800], P('dp', None, None, 'chan'), may hold values from -12 to 12
- cotangent: bfloat16 [4, 48, 360, 800], P('dp', None, None, 'chan'), may hold values from -9 to 9
- land: int32 [4, 48, 360], P('dp'), may hold values 0 or 1
- grid_res: int32 [4], P('dp'), may hold values from 0 to 1
- dw_kernel: bfloat16 [49, 800], replicated, may hold values from -0.875 to 0.875
- gain: float32 [800], replicated, may hold values from 0.5 to 1.5
- shift: float32 [800], replicated, may hold values from -1.75 to 1.75
- res_bias: float32 [2, 800], replicated, may hold values from -3 to 3
- w_in: bfloat16 [800, 3200], replicated, may hold values from -0.21875 to 0.21875
- b_in: float32 [3200], replicated, may hold values from -1.75 to 1.75
- w_out: bfloat16 [3200, 800], replicated, may hold values from -0.109375 to 0.109375
- b_out: float32 [800], replicated, may hold values from -1.75 to 1.75
Outputs:
- mixed: bfloat16 [4, 48, 360, 800], P('dp', None, None, 'chan')
- x_grad: bfloat16 [4, 48, 360, 800], P('dp', None, None, 'chan')
- g_kernel: float32 [49, 800], replicated
- g_gain: float32 [800], replicated
- g_shift: float32 [800], replicated
- g_res_bias: float32 [2, 800], replicated
- g_w_in: float32 [800, 3200], replicated
- g_b_in: float32 [3200], replicated
- g_w_out: float32 [3200, 800], replicated
- g_b_out: float32 [800], replicated
The draws below stay inside these ranges and needn't reach their ends.
All inputs are finite; a program needn't handle non-finite values. No bound on the sum of `land` on one device may be relied on, other than what follows from the above.
Results may differ from the reference program's by a relative error of at most 0.01.
Values may be sent and summed in bfloat16 or wider, within the bound.
No kernel may reach another device: no remote copies, remote signals or barrier semaphores. Data moves between devices by JAX's collectives and lax.ppermute only.
A program may use at most 320 MiB of HBM per device.

```python
import math
import jax
import jax.numpy as jnp
from jax import lax

C = 800
FF = 3200
KS = 7
W = 360
ROWS_DEV = 6
H = 48
SAMPLES = 4


def latitude_scale(key, low_end, high_end):
    places = jnp.arange(H, dtype=jnp.float32) / max(H - 1, 1)
    rough = jnp.exp(jax.random.uniform(key, (H,), jnp.float32, -0.35, 0.35))
    return low_end * (high_end / low_end) ** places * rough


def draw_x_in(key, part):
    key = jax.random.fold_in(key, 11)
    keys = jax.random.split(key, 3)
    rows_scale = latitude_scale(keys[0], 0.1, 1.0)
    chan_scale = jnp.exp(jax.random.uniform(keys[1], (C,), jnp.float32, math.log(0.5), math.log(2.0)))
    shape = (SAMPLES, H, W, C)
    base = jnp.clip(jax.random.normal(keys[2], shape, jnp.float32), -4.0, 4.0)
    return (base * rows_scale[None, :, None, None] * chan_scale).astype(jnp.bfloat16)


def draw_cotangent(key, part):
    key = jax.random.fold_in(key, 23)
    keys = jax.random.split(key, 2)
    rows_scale = latitude_scale(keys[0], 0.5, 1.5)
    shape = (SAMPLES, H, W, C)
    base = jnp.clip(jax.random.normal(keys[1], shape, jnp.float32), -4.0, 4.0)
    return (base * rows_scale[None, :, None, None]).astype(jnp.bfloat16)


def plant(values, key, least, high):
    longest = values.shape.index(max(values.shape))
    spots = []
    for shift in (0, 1):
        where = [jax.random.randint(jax.random.fold_in(key, axis), (), 0, length) for axis, length in enumerate(values.shape)]
        where[longest] = (where[longest] + shift) % values.shape[longest]
        spots.append(tuple(where))
    return values.at[spots[0]].set(least).at[spots[1]].set(high)


def gaussian(own_key, shape, width, limit, kind=jnp.bfloat16):
    result = jax.random.normal(own_key, shape, jnp.float32) * width
    return jnp.minimum(jnp.maximum(result, -limit), limit).astype(kind)


def setup_inputs(seed: int = 0) -> dict:
    splits = jax.random.split(jax.random.key(seed), 13)
    return {
        "x_in": draw_x_in(jax.random.fold_in(splits[12], 71), 0),
        "cotangent": draw_cotangent(jax.random.fold_in(splits[12], 71), 0),
        "land": plant((jax.random.randint(splits[2], (SAMPLES, H, W), 0, 3) < 2).astype(jnp.int32), jax.random.fold_in(splits[2], 1), 0, 1),
        "grid_res": plant(jax.random.randint(splits[3], (SAMPLES,), 0, 2), jax.random.fold_in(splits[3], 1), 0, 1).astype(jnp.int32),
        "dw_kernel": gaussian(splits[4], (KS * KS, C), (KS * KS) ** -0.5, 0.875),
        "gain": jnp.clip(1.0 + 0.1 * jax.random.normal(splits[5], (C,), jnp.float32), 0.5, 1.5),
        "shift": gaussian(splits[6], (C,), 0.3, 1.75, jnp.float32),
        "res_bias": gaussian(splits[7], (2, C), 0.5, 3.0, jnp.float32),
        "w_in": gaussian(splits[8], (C, FF), C ** -0.5, 0.21875),
        "b_in": gaussian(splits[9], (FF,), 0.3, 1.75, jnp.float32),
        "w_out": gaussian(splits[10], (FF, C), FF ** -0.5, 0.109375),
        "b_out": gaussian(splits[11], (C,), 0.3, 1.75, jnp.float32),
    }


@jax.custom_vjp
def low(v):
    return lax.optimization_barrier(v.astype(jnp.bfloat16)).astype(jnp.float32)

@jax.custom_vjp
def low_back(v):
    return v

def low_keep(v):
    return (low(v), None)

def low_pass(kept, grad):
    return (grad,)

def back_keep(v):
    return (v, None)

def back_low(kept, grad):
    return (low(grad),)
low.defvjp(low_keep, low_pass)
low_back.defvjp(back_keep, back_low)

def conv_sample(sample, kernel):
    margin = (KS - 1) // 2
    padded = jnp.pad(sample, ((margin, margin), (0, 0), (0, 0)))
    padded = jnp.concatenate([padded[:, -margin:], padded, padded[:, :margin]], axis=1)
    summed = jnp.zeros_like(sample)
    for row_off in range(KS):
        for col_off in range(KS):
            summed = summed + padded[row_off:row_off + H, col_off:col_off + W, :] * kernel[KS * row_off + col_off]
    return summed

def reference(x_in, cotangent, land, grid_res, dw_kernel, gain, shift, res_bias, w_in, b_in, w_out, b_out):
    highest = lax.Precision.HIGHEST
    land_mask = land.astype(jnp.float32)[..., None]
    chooser = (grid_res[:, None] == jnp.arange(2, dtype=jnp.int32)[None, :]).astype(jnp.float32)

    def forward(inputs, kernel, gains, shifts, rbias, weight_in, bias_in, weight_out, bias_out):
        inputs = low_back(inputs)

        def conv_one(sample):
            return conv_sample(sample, kernel)
        conv = lax.map(jax.checkpoint(conv_one), inputs)
        conv = low_back(conv)
        mean = lax.optimization_barrier(jnp.mean(conv, axis=(0, 1, 2)))
        var = lax.optimization_barrier(jnp.mean(conv * conv, axis=(0, 1, 2))) - mean * mean
        centred = (conv - mean) * lax.rsqrt(var + 1e-05)
        sample_bias = lax.optimization_barrier(jnp.sum(chooser[:, :, None] * rbias[None], axis=1))
        normed = low_back(low(gains * centred + shifts + sample_bias[:, None, None, :]))

        def perceptron(block):
            hidden = low_back(jnp.dot(block, weight_in, precision=highest) + bias_in)
            active = low(jax.nn.gelu(hidden, approximate=False))
            return low_back(jnp.dot(active, weight_out, precision=highest) + bias_out)
        blocks = normed.reshape(-1, ROWS_DEV * W, C)
        branch = lax.map(jax.checkpoint(perceptron), blocks).reshape(inputs.shape)
        return land_mask * (inputs + branch)
    mixed, pullback = jax.vjp(forward, x_in.astype(jnp.float32), dw_kernel.astype(jnp.float32), gain, shift, res_bias, w_in.astype(jnp.float32), b_in, w_out.astype(jnp.float32), b_out)
    grads = pullback(cotangent.astype(jnp.float32))
    return (mixed.astype(jnp.bfloat16), grads[0].astype(jnp.bfloat16), grads[1], grads[2], grads[3], grads[4], grads[5], grads[6], grads[7], grads[8])
```

```python
from functools import partial
import math

import jax
import jax.numpy as jnp
from jax import lax
from jax.experimental import pallas as pl
from jax.experimental.pallas import tpu as pltpu
from jax.sharding import PartitionSpec as P

LANES = 128
SUBL = 8
VMEM_LIMIT = 56 * 1024 * 1024
F32 = jnp.float32
BF16 = jnp.bfloat16


def round_up(value, step):
    return (value + step - 1) // step * step


def block_of(total, most):
    return max(size for size in range(1, most + 1) if total % size == 0)


class Sizes:
    def __init__(self, chan, height, width, bands, taps):
        self.chan, self.height, self.width, self.bands = chan, height, width, bands
        self.side = math.isqrt(taps)
        self.margin = self.side // 2
        self.rows = height // bands
        self.wide = round_up(width + 2 * self.margin, LANES)
        self.tiles = self.wide // LANES
        self.pad = round_up(chan, SUBL)
        self.packed_rows = bands * self.pad
        self.units = self.rows * self.tiles
        self.top = SUBL
        self.tall = height + 2 * SUBL

    def tall_scratch(self):
        return pltpu.VMEM((self.tiles, self.tall, LANES), F32)

    def pack_scratch(self):
        return pltpu.VMEM((self.units, self.packed_rows, LANES), F32)


def params(semantics=("arbitrary",)):
    return pltpu.CompilerParams(dimension_semantics=semantics, vmem_limit_bytes=VMEM_LIMIT)


def split_tiles(z, value):
    return [value[:, LANES * j : LANES * (j + 1)] for j in range(z.tiles)]


def put_tall(z, tall, value):
    rows = value.shape[0]
    value = jnp.concatenate([value, jnp.zeros((rows, z.wide - z.width), F32)], axis=1)
    for j, tile in enumerate(split_tiles(z, value)):
        tall[j, z.top : z.top + rows, :] = tile


def put_tall_wrapped(z, tall, value):
    rows = value.shape[0]
    gap = jnp.zeros((rows, z.wide - z.width - 2 * z.margin), F32)
    value = jnp.concatenate(
        [value, value[:, : z.margin], gap, value[:, z.width - z.margin :]], axis=1
    )
    for j, tile in enumerate(split_tiles(z, value)):
        tall[j, z.top : z.top + rows, :] = tile


def band_row(z, tall, offset):
    return jnp.concatenate(
        [tall[j, pl.ds(z.top + offset, z.bands, stride=z.rows), :] for j in range(z.tiles)], axis=1
    )


def put_band_row(z, tall, offset, value):
    for j, tile in enumerate(split_tiles(z, value)):
        tall[j, pl.ds(z.top + offset, z.bands, stride=z.rows), :] = tile


def put_packed(z, scratch, channel, row, value):
    for j, tile in enumerate(split_tiles(z, value)):
        scratch[row * z.tiles + j, pl.ds(channel, z.bands, stride=z.pad), :] = tile


def get_packed(z, scratch, channel, row):
    return jnp.concatenate(
        [
            scratch[row * z.tiles + j, pl.ds(channel, z.bands, stride=z.pad), :]
            for j in range(z.tiles)
        ],
        axis=1,
    )


def clear_packed_pad(z, scratch):
    zeros = jnp.zeros((z.bands, z.wide), F32)
    for channel in range(z.chan, z.pad):
        for row in range(z.rows):
            put_packed(z, scratch, channel, row, zeros)


def write_packed(z, scratch, refs):
    unit = 0
    for ref in refs:
        for k in range(ref.shape[1] // LANES):
            ref[:, LANES * k : LANES * (k + 1)] = scratch[unit].astype(BF16)
            unit += 1


def read_packed(z, refs, scratch):
    unit = 0
    for ref in refs:
        for k in range(ref.shape[1] // LANES):
            scratch[unit] = ref[:, LANES * k : LANES * (k + 1)].astype(F32)
            unit += 1


def whole(shape):
    return pl.BlockSpec(shape, lambda *_: (0,) * len(shape))


def smem():
    return pl.BlockSpec(memory_space=pltpu.SMEM)


def images(z, size):
    return pl.BlockSpec((size, z.height, z.width), lambda g: (g, 0, 0))


def banded(z, size):
    return pl.BlockSpec((size, z.rows, z.bands, z.wide), lambda g: (g, 0, 0, 0))


def lane_sum(z, value):
    total = jnp.sum(value, axis=0, keepdims=True)
    return sum(split_tiles(z, total))


def pack_out_grad(z, lengths, cot, land):
    size = block_of(z.chan, 10)

    def kernel(cot_ref, land_ref, *rest):
        outs, sums_ref, scratch, tall = rest[: len(lengths)], *rest[len(lengths) :]
        step = pl.program_id(0)

        @pl.when(step == 0)
        def _():
            clear_packed_pad(z, scratch)

        mask = land_ref[...].astype(F32)

        def body(c, carry):
            value = cot_ref[c].astype(F32) * mask
            put_tall(z, tall, value)
            sums_ref[c, :, :] = jnp.sum(value, axis=0, keepdims=True)
            for row in range(z.rows):
                put_packed(z, scratch, step * size + c, row, band_row(z, tall, row))
            return carry

        lax.fori_loop(0, size, body, 0)

        @pl.when(step == pl.num_programs(0) - 1)
        def _():
            write_packed(z, scratch, outs)

    packed = [jax.ShapeDtypeStruct((z.packed_rows, n), BF16) for n in lengths]
    out = pl.pallas_call(
        kernel,
        grid=(z.chan // size,),
        in_specs=[images(z, size), whole((z.height, z.width))],
        out_specs=[whole(p.shape) for p in packed]
        + [pl.BlockSpec((size, 1, z.width), lambda g: (g, 0, 0))],
        out_shape=packed + [jax.ShapeDtypeStruct((z.chan, 1, z.width), F32)],
        scratch_shapes=[z.pack_scratch(), z.tall_scratch()],
        compiler_params=params(),
        cost_estimate=pl.CostEstimate(flops=10**7, bytes_accessed=16 * 10**6, transcendentals=0),
    )(cot, land)
    return out[:-1], jnp.sum(out[-1], axis=(1, 2))


def conv_forward(z, taps, x):
    size = block_of(z.chan, 10)

    def kernel(taps_ref, x_ref, conv_ref, sum_ref, square_ref, tall):
        step = pl.program_id(0)

        @pl.when(step == 0)
        def _():
            tall[...] = jnp.zeros_like(tall)

        keep = lax.broadcasted_iota(jnp.int32, (z.bands, z.wide), 1) < z.width

        def body(c, carry):
            put_tall_wrapped(z, tall, x_ref[c].astype(F32))
            rows = [band_row(z, tall, m - z.margin) for m in range(z.rows + 2 * z.margin)]
            sums = [None] * z.rows
            for b in range(z.side):
                weights = [taps_ref[step * size + c, z.side * a + b] for a in range(z.side)]
                for row in range(z.rows):
                    part = weights[0] * rows[row]
                    for a in range(1, z.side):
                        part = part + weights[a] * rows[row + a]
                    if b != z.margin:
                        part = pltpu.roll(part, (z.margin - b) % z.wide, 1)
                    sums[row] = part if b == 0 else sums[row] + part
            total = jnp.zeros((z.bands, z.wide), F32)
            square = jnp.zeros((z.bands, z.wide), F32)
            for row in range(z.rows):
                value = jnp.where(keep, sums[row], 0.0)
                conv_ref[c, row] = value
                total = total + value
                square = square + value * value
            sum_ref[c] = lane_sum(z, total)
            square_ref[c] = lane_sum(z, square)
            return carry

        lax.fori_loop(0, size, body, 0)

    lane_spec = pl.BlockSpec((size, 1, LANES), lambda g: (g, 0, 0))
    lane_shape = jax.ShapeDtypeStruct((z.chan, 1, LANES), F32)
    conv, total, square = pl.pallas_call(
        kernel,
        grid=(z.chan // size,),
        in_specs=[smem(), images(z, size)],
        out_specs=[banded(z, size), lane_spec, lane_spec],
        out_shape=[
            jax.ShapeDtypeStruct((z.chan, z.rows, z.bands, z.wide), F32),
            lane_shape,
            lane_shape,
        ],
        scratch_shapes=[z.tall_scratch()],
        compiler_params=params(),
        cost_estimate=pl.CostEstimate(
            flops=10**10, bytes_accessed=16 * 10**6, transcendentals=0
        ),
    )(taps, x)
    return conv, jnp.sum(total, axis=(1, 2)), jnp.sum(square, axis=(1, 2))


def pack_normed(z, lengths, conv, affine):
    size = block_of(z.chan, 10)

    def kernel(affine_ref, conv_ref, *rest):
        outs, scratch = rest[:-1], rest[-1]
        step = pl.program_id(0)

        @pl.when(step == 0)
        def _():
            clear_packed_pad(z, scratch)

        def body(c, carry):
            channel = step * size + c
            mean, factor, offset = (affine_ref[channel, k] for k in range(3))
            for row in range(z.rows):
                put_packed(z, scratch, channel, row, (conv_ref[c, row] - mean) * factor + offset)
            return carry

        lax.fori_loop(0, size, body, 0)

        @pl.when(step == pl.num_programs(0) - 1)
        def _():
            write_packed(z, scratch, outs)

    packed = [jax.ShapeDtypeStruct((z.packed_rows, n), BF16) for n in lengths]
    return pl.pallas_call(
        kernel,
        grid=(z.chan // size,),
        in_specs=[smem(), banded(z, size)],
        out_specs=[whole(p.shape) for p in packed],
        out_shape=packed,
        scratch_shapes=[z.pack_scratch()],
        compiler_params=params(),
        cost_estimate=pl.CostEstimate(flops=10**7, bytes_accessed=16 * 10**6, transcendentals=0),
    )(affine, conv)


def gelu_parts(h):
    size = jnp.abs(h)
    t = 1.0 / (1.0 + (0.3275911 * math.sqrt(0.5)) * size)
    bell = jnp.exp(-0.5 * h * h)
    poly = t * (
        0.5 * 0.254829592
        + t
        * (
            0.5 * -0.284496736
            + t * (0.5 * 1.421413741 + t * (0.5 * -1.453152027 + t * (0.5 * 1.061405429)))
        )
    )
    tail = poly * bell
    phi = jnp.where(h >= 0, 1.0 - tail, tail)
    return h * phi, phi + h * bell * (1.0 / math.sqrt(2.0 * math.pi))


def mlp(normed, out_grad, w_in_t, w_in_p, w_out_p, w_out_t, b_in, b_out):
    wide, cells = normed.shape
    hidden = w_in_t.shape[0]
    block = block_of(hidden, 640)

    def kernel(
        n_ref, g_ref, w_in_t_ref, w_in_ref, w_out_ref, w_out_t_ref, b_in_ref, b_out_ref,
        branch_ref, norm_ref, active_ref, hidden_ref, bias_ref, branch_acc, norm_acc,
    ):
        step = pl.program_id(0)
        h = jnp.dot(w_in_t_ref[...], n_ref[...], preferred_element_type=F32) + b_in_ref[...]
        back = jnp.dot(w_out_ref[...], g_ref[...], preferred_element_type=F32)
        active, slope = gelu_parts(h)
        active = active.astype(BF16)
        grad = (back * slope).astype(BF16)
        active_ref[...] = active
        hidden_ref[...] = grad
        grad32 = grad.astype(F32)
        bias_ref[...] = sum(grad32[:, LANES * k : LANES * (k + 1)] for k in range(cells // LANES))
        branch = jnp.dot(w_out_t_ref[...], active, preferred_element_type=F32)
        norm = jnp.dot(w_in_ref[...], grad, preferred_element_type=F32)

        @pl.when(step == 0)
        def _():
            branch_acc[...] = branch + b_out_ref[...]
            norm_acc[...] = norm

        @pl.when(step > 0)
        def _():
            branch_acc[...] += branch
            norm_acc[...] += norm

        @pl.when(step == pl.num_programs(0) - 1)
        def _():
            branch_ref[...] = branch_acc[...].astype(BF16)
            norm_ref[...] = norm_acc[...].astype(BF16)

    tall_block = pl.BlockSpec((block, wide), lambda f: (f, 0))
    wide_block = pl.BlockSpec((wide, block), lambda f: (0, f))
    kept = pl.BlockSpec((block, cells), lambda f: (f, 0))
    return pl.pallas_call(
        kernel,
        grid=(hidden // block,),
        in_specs=[
            whole((wide, cells)), whole((wide, cells)),
            tall_block, wide_block, tall_block, wide_block,
            pl.BlockSpec((block, 1), lambda f: (f, 0)), whole((wide, 1)),
        ],
        out_specs=[
            whole((wide, cells)), whole((wide, cells)), kept, kept,
            pl.BlockSpec((block, LANES), lambda f: (f, 0)),
        ],
        out_shape=[
            jax.ShapeDtypeStruct((wide, cells), BF16),
            jax.ShapeDtypeStruct((wide, cells), BF16),
            jax.ShapeDtypeStruct((hidden, cells), BF16),
            jax.ShapeDtypeStruct((hidden, cells), BF16),
            jax.ShapeDtypeStruct((hidden, LANES), F32),
        ],
        scratch_shapes=[pltpu.VMEM((wide, cells), F32), pltpu.VMEM((wide, cells), F32)],
        compiler_params=params(),
        cost_estimate=pl.CostEstimate(
            flops=8 * wide * cells * hidden, bytes_accessed=4 * 10**7, transcendentals=cells * hidden
        ),
    )(normed, out_grad, w_in_t, w_in_p, w_out_p, w_out_t, b_in, b_out)


def weight_grad(lefts, rights):
    wide, hidden = lefts[0].shape[0], rights[0].shape[0]
    block = block_of(hidden, 640)
    count = len(lefts)

    def kernel(*refs):
        total = None
        for left, right in zip(refs[:count], refs[count : 2 * count]):
            part = lax.dot_general(
                left[...], right[...], (((1,), (1,)), ((), ())), preferred_element_type=F32
            )
            total = part if total is None else total + part
        refs[-1][...] = total.astype(BF16)

    cells = sum(left.shape[1] for left in lefts)
    return pl.pallas_call(
        kernel,
        grid=(hidden // block,),
        in_specs=[whole(left.shape) for left in lefts]
        + [pl.BlockSpec((block, right.shape[1]), lambda f: (f, 0)) for right in rights],
        out_specs=pl.BlockSpec((wide, block), lambda f: (0, f)),
        out_shape=jax.ShapeDtypeStruct((wide, hidden), BF16),
        compiler_params=params(),
        cost_estimate=pl.CostEstimate(
            flops=2 * wide * cells * hidden, bytes_accessed=24 * 10**6, transcendentals=0
        ),
    )(*lefts, *rights)


def norm_sums(z, parts, conv, affine):
    size = block_of(z.chan, 10)
    count = len(parts)

    def kernel(affine_ref, conv_ref, *rest):
        ins, (shift_ref, gain_ref, scratch) = rest[:count], rest[count:]
        step = pl.program_id(0)

        @pl.when(step == 0)
        def _():
            read_packed(z, ins, scratch)

        def body(c, carry):
            channel = step * size + c
            mean, scale = affine_ref[channel, 0], affine_ref[channel, 1]
            shift = jnp.zeros((z.bands, z.wide), F32)
            gain = jnp.zeros((z.bands, z.wide), F32)
            for row in range(z.rows):
                grad = get_packed(z, scratch, channel, row)
                shift = shift + grad
                gain = gain + grad * (conv_ref[c, row] - mean)
            shift_ref[c] = lane_sum(z, shift)
            gain_ref[c] = lane_sum(z, gain * scale)
            return carry

        lax.fori_loop(0, size, body, 0)

    lane_spec = pl.BlockSpec((size, 1, LANES), lambda g: (g, 0, 0))
    lane_shape = jax.ShapeDtypeStruct((z.chan, 1, LANES), F32)
    shift, gain = pl.pallas_call(
        kernel,
        grid=(z.chan // size,),
        in_specs=[smem(), banded(z, size)] + [whole(p.shape) for p in parts],
        out_specs=[lane_spec, lane_spec],
        out_shape=[lane_shape, lane_shape],
        scratch_shapes=[z.pack_scratch()],
        compiler_params=params(),
        cost_estimate=pl.CostEstimate(flops=10**7, bytes_accessed=16 * 10**6, transcendentals=0),
    )(affine, conv, *parts)
    return jnp.sum(shift, axis=(1, 2)), jnp.sum(gain, axis=(1, 2))


def conv_backward(z, taps, terms, parts, conv, x, cot, land):
    size = block_of(z.chan, 5)
    count = len(parts)
    reach = z.rows + 2 * z.margin
    ntaps = z.side * z.side

    def kernel(taps_ref, terms_ref, conv_ref, x_ref, cot_ref, land_ref, *rest):
        ins, (grad_ref, taps_out, scratch, tall, grads, tall_out) = rest[:count], rest[count:]
        step = pl.program_id(0)

        @pl.when(step == 0)
        def _():
            read_packed(z, ins, scratch)
            tall[...] = jnp.zeros_like(tall)
            grads[...] = jnp.zeros_like(grads)

        lane = lax.broadcasted_iota(jnp.int32, (z.bands, z.wide), 1)
        mask = land_ref[...].astype(F32)

        def body(c, carry):
            channel = step * size + c
            mean, scale, factor, shift, gain = (terms_ref[channel, k] for k in range(5))
            for row in range(z.rows):
                centred = (conv_ref[c, row] - mean) * scale
                value = factor * (get_packed(z, scratch, channel, row) - (shift + centred * gain))
                after = pltpu.roll(value, z.width, 1)
                before = pltpu.roll(value, z.wide - z.width, 1)
                value = jnp.where(
                    lane < z.width,
                    value,
                    jnp.where(lane < z.width + z.margin, after, before),
                )
                grads[row, SUBL : SUBL + z.bands, :] = value

            def grad_row(offset):
                band, row = divmod(offset, z.rows)
                return grads[row, SUBL + band : SUBL + band + z.bands, :]

            rows = [grad_row(m - z.margin) for m in range(reach)]
            sums = [None] * z.rows
            for b in range(z.side):
                weights = [taps_ref[channel, z.side * a + b] for a in range(z.side)]
                for row in range(z.rows):
                    part = weights[0] * rows[row + 2 * z.margin]
                    for a in range(1, z.side):
                        part = part + weights[a] * rows[row + 2 * z.margin - a]
                    if b != z.margin:
                        part = pltpu.roll(part, (b - z.margin) % z.wide, 1)
                    sums[row] = part if b == 0 else sums[row] + part
            for row in range(z.rows):
                put_band_row(z, tall_out, row, sums[row])
            transposed = jnp.concatenate(
                [tall_out[j, z.top : z.top + z.height, :] for j in range(z.tiles)], axis=1
            )[:, : z.width]
            grad_ref[c] = (mask * cot_ref[c].astype(F32) + transposed).astype(BF16)

            put_tall(z, tall, x_ref[c].astype(F32))
            rows = [band_row(z, tall, m - z.margin) for m in range(reach)]
            for b in range(z.side):
                moved = [grads[row, SUBL : SUBL + z.bands, :] for row in range(z.rows)]
                if b != z.margin:
                    moved = [pltpu.roll(m, (b - z.margin) % z.wide, 1) for m in moved]
                for a in range(z.side):
                    total = moved[0] * rows[a]
                    for row in range(1, z.rows):
                        total = total + moved[row] * rows[row + a]
                    tap = z.side * a + b
                    taps_out[c, tap : tap + 1, :] = lane_sum(z, total)
            return carry

        lax.fori_loop(0, size, body, 0)

    grad, products = pl.pallas_call(
        kernel,
        grid=(z.chan // size,),
        in_specs=[
            smem(), smem(), banded(z, size), images(z, size), images(z, size),
            whole((z.height, z.width)),
        ]
        + [whole(p.shape) for p in parts],
        out_specs=[
            images(z, size), pl.BlockSpec((size, ntaps, LANES), lambda g: (g, 0, 0)),
        ],
        out_shape=[
            jax.ShapeDtypeStruct((z.chan, z.height, z.width), BF16),
            jax.ShapeDtypeStruct((z.chan, ntaps, LANES), F32),
        ],
        scratch_shapes=[
            z.pack_scratch(),
            z.tall_scratch(),
            pltpu.VMEM((z.rows, z.bands + 2 * SUBL, z.wide), F32),
            z.tall_scratch(),
        ],
        compiler_params=params(),
        cost_estimate=pl.CostEstimate(
            flops=3 * 10**10, bytes_accessed=30 * 10**6, transcendentals=0
        ),
    )(taps, terms, conv, x, cot, land, *parts)
    return grad, jnp.sum(products, axis=2).T


def mix_branch(z, parts, x, land):
    size = block_of(z.chan, 10)
    count = len(parts)

    def kernel(x_ref, land_ref, *rest):
        ins, (out_ref, scratch, tall) = rest[:count], rest[count:]
        step = pl.program_id(0)

        @pl.when(step == 0)
        def _():
            read_packed(z, ins, scratch)

        mask = land_ref[...].astype(F32)

        def body(c, carry):
            for row in range(z.rows):
                put_band_row(z, tall, row, get_packed(z, scratch, step * size + c, row))
            branch = jnp.concatenate(
                [tall[j, z.top : z.top + z.height, :] for j in range(z.tiles)], axis=1
            )[:, : z.width]
            out_ref[c] = (mask * (x_ref[c].astype(F32) + branch)).astype(BF16)
            return carry

        lax.fori_loop(0, size, body, 0)

    return pl.pallas_call(
        kernel,
        grid=(z.chan // size,),
        in_specs=[images(z, size), whole((z.height, z.width))] + [whole(p.shape) for p in parts],
        out_specs=images(z, size),
        out_shape=jax.ShapeDtypeStruct((z.chan, z.height, z.width), BF16),
        scratch_shapes=[z.pack_scratch(), z.tall_scratch()],
        compiler_params=params(),
        cost_estimate=pl.CostEstimate(flops=10**7, bytes_accessed=16 * 10**6, transcendentals=0),
    )(x, land, *parts)


def exchange(value):
    return lax.all_to_all(value, "chan", split_axis=0, concat_axis=0, tiled=True)


def per_device(
    x_in, cotangent, land, grid_res, dw_kernel, gain, shift, res_bias, w_in, b_in, w_out, b_out
):
    samples, height, columns, chan = x_in.shape
    groups = lax.axis_size("chan")
    position = lax.axis_index("chan")
    first = position * chan
    width = chan * groups
    hidden = w_in.shape[1]
    z = Sizes(chan, height, columns, groups, dw_kernel.shape[0])
    pixels = float(samples * lax.axis_size("dp") * height * columns)
    third = z.units // 3 * LANES
    lengths = [third, third, z.units * LANES - 2 * third]

    def own(values, axis=0):
        return lax.dynamic_slice_in_dim(values, first, chan, axis)

    x = jnp.transpose(x_in[0], (2, 0, 1))
    cot = jnp.transpose(cotangent[0], (2, 0, 1))
    land2 = land[0]

    grad_parts, part_b_out = pack_out_grad(z, [sum(lengths)], cot, land2)
    grad_band = exchange(grad_parts[0])

    taps = own(dw_kernel, 1).astype(F32).T
    conv, total, square = conv_forward(z, taps, x)
    total, square = lax.psum((total, square), "dp")
    mean = total / pixels
    var = square / pixels - mean * mean
    scale = lax.rsqrt(var + 1e-05)
    own_gain = own(gain)
    chooser = (grid_res[:, None] == jnp.arange(2, dtype=jnp.int32)[None, :]).astype(F32)
    sample_bias = jnp.sum(chooser[0][:, None] * own(res_bias, 1), axis=0)
    affine = jnp.stack([mean, own_gain * scale, own(shift) + sample_bias], axis=1)
    normed_parts = [exchange(part) for part in pack_normed(z, lengths, conv, affine)]

    def pad_rows(matrix):
        blocks = matrix.reshape(groups, chan, matrix.shape[1])
        return jnp.pad(blocks, ((0, 0), (0, z.pad - chan), (0, 0))).reshape(
            z.packed_rows, matrix.shape[1]
        )

    w_in_p = pad_rows(w_in)
    w_out_t = pad_rows(w_out.T)
    w_in_t, w_out_p = w_in_p.T, w_out_t.T
    b_out_p = pad_rows(b_out[:, None])

    branch_parts, norm_parts, active, hidden_grad, bias = [], [], [], [], 0.0
    start = 0
    for normed in normed_parts:
        cells = normed.shape[1]
        grads = lax.slice_in_dim(grad_band, start, start + cells, axis=1)
        start += cells
        outs = mlp(
            normed, grads, w_in_t, w_in_p, w_out_p, w_out_t, b_in[:, None], b_out_p
        )
        branch_parts.append(outs[0])
        norm_parts.append(exchange(outs[1]))
        active.append(outs[2])
        hidden_grad.append(outs[3])
        bias = bias + jnp.sum(outs[4], axis=1)

    g_w_out_t = weight_grad([grad_band], [jnp.concatenate(active, axis=1)])
    g_w_in = weight_grad(
        [jnp.concatenate(normed_parts, axis=1)], [jnp.concatenate(hidden_grad, axis=1)]
    )
    g_w_in, g_w_out_t = lax.psum((g_w_in, g_w_out_t), ("dp", "chan"))
    branch = exchange(jnp.concatenate(branch_parts, axis=1))

    part_shift, part_gain = norm_sums(
        z, norm_parts, conv, jnp.stack([mean, scale], axis=1)
    )
    total_shift, total_gain = lax.psum((part_shift, part_gain), "dp")
    terms = jnp.stack(
        [mean, scale, own_gain * scale, total_shift / pixels, total_gain / pixels], axis=1
    )
    x_grad, g_kernel = conv_backward(z, taps, terms, norm_parts, conv, x, cot, land2)
    mixed = mix_branch(z, [branch], x, land2)

    rows = jnp.concatenate(
        [
            g_kernel,
            part_gain[None],
            part_shift[None],
            chooser[0][:, None] * part_shift[None],
            part_b_out[None],
        ],
        axis=0,
    )
    placed = lax.dynamic_update_slice_in_dim(
        jnp.zeros((rows.shape[0], width), F32), rows, first, axis=1
    )
    placed, g_b_in = lax.psum((placed, bias), ("dp", "chan"))
    count = dw_kernel.shape[0]

    def unpad_rows(matrix):
        return matrix.reshape(groups, z.pad, hidden)[:, :chan].reshape(width, hidden).astype(F32)

    return (
        jnp.transpose(mixed, (1, 2, 0))[None],
        jnp.transpose(x_grad, (1, 2, 0))[None],
        placed[:count],
        placed[count],
        placed[count + 1],
        placed[count + 2 : count + 4],
        unpad_rows(g_w_in),
        g_b_in,
        unpad_rows(g_w_out_t).T,
        placed[count + 4],
    )


def solution(mesh):
    cells = P("dp", None, None, "chan")
    return jax.shard_map(
        per_device,
        mesh=mesh,
        in_specs=(cells, cells, P("dp", None, None), P("dp")) + (P(),) * 8,
        out_specs=(cells, cells) + (P(),) * 8,
        check_vma=False,
    )
```

```python
from functools import partial
import math

import jax
import jax.numpy as jnp
from jax import lax
from jax.experimental import pallas as pl
from jax.experimental.pallas import tpu as pltpu
from jax.sharding import PartitionSpec as P

LANES = 128
SUBL = 8
VMEM_LIMIT = 56 * 1024 * 1024
F32 = jnp.float32
BF16 = jnp.bfloat16


def round_up(value, step):
    return (value + step - 1) // step * step


def block_of(total, most):
    return max(size for size in range(1, most + 1) if total % size == 0)


class Sizes:
    def __init__(self, chan, height, width, bands, taps):
        self.chan, self.height, self.width, self.bands = chan, height, width, bands
        self.side = math.isqrt(taps)
        self.margin = self.side // 2
        self.rows = height // bands
        self.wide = round_up(width + 2 * self.margin, LANES)
        self.tiles = self.wide // LANES
        self.pad = round_up(chan, SUBL)
        self.packed_rows = bands * self.pad
        self.units = self.rows * self.tiles
        self.top = SUBL
        self.tall = height + 2 * SUBL

    def tall_scratch(self):
        return pltpu.VMEM((self.tiles, self.tall, LANES), F32)

    def pack_scratch(self):
        return pltpu.VMEM((self.units, self.packed_rows, LANES), F32)


def params(semantics=("arbitrary",)):
    return pltpu.CompilerParams(dimension_semantics=semantics, vmem_limit_bytes=VMEM_LIMIT)


def split_tiles(z, value):
    return [value[:, LANES * j : LANES * (j + 1)] for j in range(z.tiles)]


def put_tall(z, tall, value):
    rows = value.shape[0]
    value = jnp.concatenate([value, jnp.zeros((rows, z.wide - z.width), F32)], axis=1)
    for j, tile in enumerate(split_tiles(z, value)):
        tall[j, z.top : z.top + rows, :] = tile


def put_tall_wrapped(z, tall, value):
    rows = value.shape[0]
    gap = jnp.zeros((rows, z.wide - z.width - 2 * z.margin), F32)
    value = jnp.concatenate(
        [value, value[:, : z.margin], gap, value[:, z.width - z.margin :]], axis=1
    )
    for j, tile in enumerate(split_tiles(z, value)):
        tall[j, z.top : z.top + rows, :] = tile


def band_row(z, tall, offset):
    return jnp.concatenate(
        [tall[j, pl.ds(z.top + offset, z.bands, stride=z.rows), :] for j in range(z.tiles)], axis=1
    )


def put_band_row(z, tall, offset, value):
    for j, tile in enumerate(split_tiles(z, value)):
        tall[j, pl.ds(z.top + offset, z.bands, stride=z.rows), :] = tile


def put_packed(z, scratch, channel, row, value):
    for j, tile in enumerate(split_tiles(z, value)):
        scratch[row * z.tiles + j, pl.ds(channel, z.bands, stride=z.pad), :] = tile


def get_packed(z, scratch, channel, row):
    return jnp.concatenate(
        [
            scratch[row * z.tiles + j, pl.ds(channel, z.bands, stride=z.pad), :]
            for j in range(z.tiles)
        ],
        axis=1,
    )


def clear_packed_pad(z, scratch):
    zeros = jnp.zeros((z.bands, z.wide), F32)
    for channel in range(z.chan, z.pad):
        for row in range(z.rows):
            put_packed(z, scratch, channel, row, zeros)


def write_packed(z, scratch, refs):
    unit = 0
    for ref in refs:
        for k in range(ref.shape[1] // LANES):
            ref[:, LANES * k : LANES * (k + 1)] = scratch[unit].astype(BF16)
            unit += 1


def read_packed(z, refs, scratch):
    unit = 0
    for ref in refs:
        for k in range(ref.shape[1] // LANES):
            scratch[unit] = ref[:, LANES * k : LANES * (k + 1)].astype(F32)
            unit += 1


def whole(shape):
    return pl.BlockSpec(shape, lambda *_: (0,) * len(shape))


def smem():
    return pl.BlockSpec(memory_space=pltpu.SMEM)


def images(z, size):
    return pl.BlockSpec((size, z.height, z.width), lambda g: (g, 0, 0))


def banded(z, size):
    return pl.BlockSpec((size, z.rows, z.bands, z.wide), lambda g: (g, 0, 0, 0))


def lane_sum(z, value):
    return jnp.sum(sum(split_tiles(z, value)), axis=0, keepdims=True)


def pack_out_grad(z, lengths, cot, land):
    size = block_of(z.chan, 10)

    def kernel(cot_ref, land_ref, *rest):
        outs, sums_ref, scratch, tall = rest[: len(lengths)], *rest[len(lengths) :]
        step = pl.program_id(0)

        @pl.when(step == 0)
        def _():
            clear_packed_pad(z, scratch)

        mask = land_ref[...].astype(F32)

        def body(c, carry):
            value = cot_ref[c].astype(F32) * mask
            put_tall(z, tall, value)
            sums_ref[c, :, :] = jnp.sum(value, axis=0, keepdims=True)
            for row in range(z.rows):
                put_packed(z, scratch, step * size + c, row, band_row(z, tall, row))
            return carry

        lax.fori_loop(0, size, body, 0)

        @pl.when(step == pl.num_programs(0) - 1)
        def _():
            write_packed(z, scratch, outs)

    packed = [jax.ShapeDtypeStruct((z.packed_rows, n), BF16) for n in lengths]
    out = pl.pallas_call(
        kernel,
        grid=(z.chan // size,),
        in_specs=[images(z, size), whole((z.height, z.width))],
        out_specs=[whole(p.shape) for p in packed]
        + [pl.BlockSpec((size, 1, z.width), lambda g: (g, 0, 0))],
        out_shape=packed + [jax.ShapeDtypeStruct((z.chan, 1, z.width), F32)],
        scratch_shapes=[z.pack_scratch(), z.tall_scratch()],
        compiler_params=params(),
        cost_estimate=pl.CostEstimate(flops=10**7, bytes_accessed=16 * 10**6, transcendentals=0),
    )(cot, land)
    return out[:-1], jnp.sum(out[-1], axis=(1, 2))


def conv_forward(z, taps, x):
    size = block_of(z.chan, 10)

    def kernel(taps_ref, x_ref, conv_ref, sum_ref, square_ref, tall):
        step = pl.program_id(0)

        @pl.when(step == 0)
        def _():
            tall[...] = jnp.zeros_like(tall)

        keep = lax.broadcasted_iota(jnp.int32, (z.bands, z.wide), 1) < z.width

        def body(c, carry):
            put_tall_wrapped(z, tall, x_ref[c].astype(F32))
            rows = [band_row(z, tall, m - z.margin) for m in range(z.rows + 2 * z.margin)]
            sums = [None] * z.rows
            for b in range(z.side):
                weights = [taps_ref[step * size + c, z.side * a + b] for a in range(z.side)]
                for row in range(z.rows):
                    part = weights[0] * rows[row]
                    for a in range(1, z.side):
                        part = part + weights[a] * rows[row + a]
                    if b != z.margin:
                        part = pltpu.roll(part, (z.margin - b) % z.wide, 1)
                    sums[row] = part if b == 0 else sums[row] + part
            total = jnp.zeros((z.bands, z.wide), F32)
            square = jnp.zeros((z.bands, z.wide), F32)
            for row in range(z.rows):
                value = jnp.where(keep, sums[row], 0.0)
                conv_ref[c, row] = value
                total = total + value
                square = square + value * value
            sum_ref[c] = lane_sum(z, total)
            square_ref[c] = lane_sum(z, square)
            return carry

        lax.fori_loop(0, size, body, 0)

    lane_spec = pl.BlockSpec((size, 1, LANES), lambda g: (g, 0, 0))
    lane_shape = jax.ShapeDtypeStruct((z.chan, 1, LANES), F32)
    conv, total, square = pl.pallas_call(
        kernel,
        grid=(z.chan // size,),
        in_specs=[smem(), images(z, size)],
        out_specs=[banded(z, size), lane_spec, lane_spec],
        out_shape=[
            jax.ShapeDtypeStruct((z.chan, z.rows, z.bands, z.wide), F32),
            lane_shape,
            lane_shape,
        ],
        scratch_shapes=[z.tall_scratch()],
        compiler_params=params(),
        cost_estimate=pl.CostEstimate(
            flops=10**10, bytes_accessed=16 * 10**6, transcendentals=0
        ),
    )(taps, x)
    return conv, jnp.sum(total, axis=(1, 2)), jnp.sum(square, axis=(1, 2))


def pack_normed(z, lengths, conv, affine):
    size = block_of(z.chan, 10)

    def kernel(affine_ref, conv_ref, *rest):
        outs, scratch = rest[:-1], rest[-1]
        step = pl.program_id(0)

        @pl.when(step == 0)
        def _():
            clear_packed_pad(z, scratch)

        def body(c, carry):
            channel = step * size + c
            mean, factor, offset = (affine_ref[channel, k] for k in range(3))
            for row in range(z.rows):
                put_packed(z, scratch, channel, row, (conv_ref[c, row] - mean) * factor + offset)
            return carry

        lax.fori_loop(0, size, body, 0)

        @pl.when(step == pl.num_programs(0) - 1)
        def _():
            write_packed(z, scratch, outs)

    packed = [jax.ShapeDtypeStruct((z.packed_rows, n), BF16) for n in lengths]
    return pl.pallas_call(
        kernel,
        grid=(z.chan // size,),
        in_specs=[smem(), banded(z, size)],
        out_specs=[whole(p.shape) for p in packed],
        out_shape=packed,
        scratch_shapes=[z.pack_scratch()],
        compiler_params=params(),
        cost_estimate=pl.CostEstimate(flops=10**7, bytes_accessed=16 * 10**6, transcendentals=0),
    )(affine, conv)


def gelu_parts(h):
    span = 1.0 + (0.3275911 * math.sqrt(0.5)) * jnp.abs(h)
    t = pl.reciprocal(span, approx=True)
    t = t * (2.0 - span * t)
    bell = jnp.exp2((-0.5 / math.log(2.0)) * (h * h))
    poly = t * (
        0.5 * 0.254829592
        + t
        * (
            0.5 * -0.284496736
            + t * (0.5 * 1.421413741 + t * (0.5 * -1.453152027 + t * (0.5 * 1.061405429)))
        )
    )
    tail = poly * bell
    phi = jnp.where(h >= 0, 1.0 - tail, tail)
    return h * phi, phi + h * ((1.0 / math.sqrt(2.0 * math.pi)) * bell)


def lane_block(rows, cells, part):
    return pl.BlockSpec((rows, cells), lambda *_: (0, part))


def mlp(z, part, normed, out_grad, w_in_t, w_in, w_out, w_out_t, b_in, b_out, branch_all):
    packed, cells = normed.shape
    hidden, width = w_in_t.shape
    block = block_of(hidden, 640)
    blocks = hidden // block
    pieces = 5 if block % (5 * 16) == 0 and width % (5 * 16) == 0 else 1
    rows_in, rows_out = block // pieces, width // pieces
    groups = packed // z.pad

    def kernel(
        n_ref, g_ref, w_in_t_ref, w_in_ref, w_out_ref, w_out_t_ref, b_in_ref, b_out_ref, *rest
    ):
        (
            branch_ref, norm_ref, active_ref, hidden_ref, bias_ref,
            n, g, branch_acc, norm_acc, h_buf, back_buf, active_buf, hidden_buf, wide_buf,
        ) = rest[-14:]
        step = pl.program_id(0)

        def unpad(source, target):
            wide_buf[...] = source[...].astype(F32)
            target[...] = jnp.concatenate(
                [wide_buf[z.pad * k : z.pad * k + z.chan, :] for k in range(groups)], axis=0
            ).astype(BF16)

        def pad(source, target):
            if z.pad != z.chan:
                for k in range(groups):
                    wide_buf[z.pad * k : z.pad * (k + 1), :] = jnp.concatenate(
                        [
                            source[z.chan * k : z.chan * (k + 1), :],
                            jnp.zeros((z.pad - z.chan, cells), F32),
                        ],
                        axis=0,
                    )
                target[...] = wide_buf[...].astype(BF16)
            else:
                target[...] = source[...].astype(BF16)

        def products_in(piece):
            at = slice(rows_in * piece, rows_in * (piece + 1))
            slot = lax.rem(step, 2)
            h_buf[slot, at, :] = (
                jnp.dot(w_in_t_ref[at, :], n[...], preferred_element_type=F32) + b_in_ref[at, :]
            )
            back_buf[slot, at, :] = jnp.dot(w_out_ref[at, :], g[...], preferred_element_type=F32)

        def gelu(piece):
            at = slice(rows_in * piece, rows_in * (piece + 1))
            slot = lax.rem(step + 1, 2)
            active, slope = gelu_parts(h_buf[slot, at, :])
            grad = back_buf[slot, at, :] * slope
            bias_ref[at, :] = sum(
                grad[:, LANES * k : LANES * (k + 1)] for k in range(cells // LANES)
            )
            active, grad = active.astype(BF16), grad.astype(BF16)
            active_buf[slot, at, :] = active
            hidden_buf[slot, at, :] = grad
            active_ref[at, :] = active
            hidden_ref[at, :] = grad

        def products_out(piece):
            at = slice(rows_out * piece, rows_out * (piece + 1))
            slot = lax.rem(step, 2)
            branch_acc[at, :] += jnp.dot(
                w_out_t_ref[at, :], active_buf[slot], preferred_element_type=F32
            )
            norm_acc[at, :] += jnp.dot(
                w_in_ref[at, :], hidden_buf[slot], preferred_element_type=F32
            )

        def run(*stages):
            for piece in range(pieces):
                for stage in stages:
                    stage(piece)

        @pl.when(step == 0)
        def _():
            unpad(n_ref, n)
            unpad(g_ref, g)
            branch_acc[...] = jnp.broadcast_to(b_out_ref[...], branch_acc.shape)
            norm_acc[...] = jnp.zeros_like(norm_acc)
            run(products_in)

        @pl.when(step == 1)
        def _():
            run(products_in, gelu)

        @pl.when((step >= 2) & (step < blocks))
        def _():
            run(products_in, gelu, products_out)

        @pl.when(step == blocks)
        def _():
            run(gelu, products_out)

        @pl.when(step == blocks + 1)
        def _():
            run(products_out)
            pad(branch_acc, branch_ref)
            pad(norm_acc, norm_ref)

    def at_in(f):
        return jnp.minimum(f, blocks - 1)

    def at_gelu(f):
        return jnp.clip(f - 1, 0, blocks - 1)

    def at_out(f):
        return jnp.clip(f - 2, 0, blocks - 1)

    tall_block = pl.BlockSpec((block, width), lambda f: (at_in(f), 0))
    wide_block = pl.BlockSpec((width, block), lambda f: (0, at_out(f)))
    kept = pl.BlockSpec((block, cells), lambda f: (at_gelu(f), 0))
    operands = [normed, out_grad, w_in_t, w_in, w_out, w_out_t, b_in, b_out]
    in_specs = [
        whole((packed, cells)), lane_block(packed, cells, part),
        tall_block, wide_block, tall_block, wide_block,
        pl.BlockSpec((block, 1), lambda f: (at_in(f), 0)), whole((width, 1)),
    ]
    aliases = {}
    if branch_all is not None:
        aliases = {len(operands): 0}
        operands.append(branch_all)
        in_specs.append(pl.BlockSpec(memory_space=pl.ANY))
    return pl.pallas_call(
        kernel,
        grid=(blocks + 2,),
        in_specs=in_specs,
        out_specs=[
            lane_block(packed, cells, part), whole((packed, cells)), kept, kept,
            pl.BlockSpec((block, LANES), lambda f: (at_gelu(f), 0)),
        ],
        out_shape=[
            jax.ShapeDtypeStruct(out_grad.shape, BF16),
            jax.ShapeDtypeStruct((packed, cells), BF16),
            jax.ShapeDtypeStruct((hidden, cells), BF16),
            jax.ShapeDtypeStruct((hidden, cells), BF16),
            jax.ShapeDtypeStruct((hidden, LANES), F32),
        ],
        scratch_shapes=[
            pltpu.VMEM((width, cells), BF16), pltpu.VMEM((width, cells), BF16),
            pltpu.VMEM((width, cells), F32), pltpu.VMEM((width, cells), F32),
            pltpu.VMEM((2, block, cells), F32), pltpu.VMEM((2, block, cells), F32),
            pltpu.VMEM((2, block, cells), BF16), pltpu.VMEM((2, block, cells), BF16),
            pltpu.VMEM((packed, cells), F32),
        ],
        input_output_aliases=aliases,
        compiler_params=params(),
        cost_estimate=pl.CostEstimate(
            flops=8 * width * cells * hidden, bytes_accessed=4 * 10**7, transcendentals=cells * hidden
        ),
    )(*operands)


def weight_grad(lefts, rights):
    rows, hidden = lefts[0][0].shape[0], rights[0].shape[0]
    block = block_of(hidden, 640)
    count = len(lefts)

    def kernel(*refs):
        total = None
        for left, right in zip(refs[:count], refs[count : 2 * count]):
            part = lax.dot_general(
                left[...], right[...], (((1,), (1,)), ((), ())), preferred_element_type=F32
            )
            total = part if total is None else total + part
        refs[-1][...] = total.astype(BF16)

    cells = sum(right.shape[1] for right in rights)
    return pl.pallas_call(
        kernel,
        grid=(hidden // block,),
        in_specs=[
            lane_block(rows, right.shape[1], 0 if part is None else part)
            for (_, part), right in zip(lefts, rights)
        ]
        + [pl.BlockSpec((block, right.shape[1]), lambda f: (f, 0)) for right in rights],
        out_specs=pl.BlockSpec((rows, block), lambda f: (0, f)),
        out_shape=jax.ShapeDtypeStruct((rows, hidden), BF16),
        compiler_params=params(),
        cost_estimate=pl.CostEstimate(
            flops=2 * rows * cells * hidden, bytes_accessed=24 * 10**6, transcendentals=0
        ),
    )(*(left for left, _ in lefts), *rights)


def unpad_rows(z, matrix):
    groups, hidden = matrix.shape[0] // z.pad, matrix.shape[1]
    several = next(k for k in range(1, groups + 1) if groups % k == 0 and k * z.chan % SUBL == 0)
    block = block_of(hidden // LANES, 13) * LANES

    def kernel(in_ref, out_ref):
        value = in_ref[...].astype(F32)
        for k in range(several):
            out_ref[z.chan * k : z.chan * (k + 1), :] = value[z.pad * k : z.pad * k + z.chan, :]

    return pl.pallas_call(
        kernel,
        grid=(groups // several, hidden // block),
        in_specs=[pl.BlockSpec((several * z.pad, block), lambda g, h: (g, h))],
        out_specs=pl.BlockSpec((several * z.chan, block), lambda g, h: (g, h)),
        out_shape=jax.ShapeDtypeStruct((groups * z.chan, hidden), F32),
        compiler_params=params(("arbitrary", "arbitrary")),
        cost_estimate=pl.CostEstimate(flops=10**6, bytes_accessed=16 * 10**6, transcendentals=0),
    )(matrix)


def norm_sums(z, parts, conv, affine):
    size = block_of(z.chan, 10)
    count = len(parts)

    def kernel(affine_ref, conv_ref, *rest):
        ins, (shift_ref, gain_ref, scratch) = rest[:count], rest[count:]
        step = pl.program_id(0)

        @pl.when(step == 0)
        def _():
            read_packed(z, ins, scratch)

        def body(c, carry):
            channel = step * size + c
            mean, scale = affine_ref[channel, 0], affine_ref[channel, 1]
            shift = jnp.zeros((z.bands, z.wide), F32)
            gain = jnp.zeros((z.bands, z.wide), F32)
            for row in range(z.rows):
                grad = get_packed(z, scratch, channel, row)
                shift = shift + grad
                gain = gain + grad * (conv_ref[c, row] - mean)
            shift_ref[c] = lane_sum(z, shift)
            gain_ref[c] = lane_sum(z, gain * scale)
            return carry

        lax.fori_loop(0, size, body, 0)

    lane_spec = pl.BlockSpec((size, 1, LANES), lambda g: (g, 0, 0))
    lane_shape = jax.ShapeDtypeStruct((z.chan, 1, LANES), F32)
    shift, gain = pl.pallas_call(
        kernel,
        grid=(z.chan // size,),
        in_specs=[smem(), banded(z, size)] + [whole(p.shape) for p in parts],
        out_specs=[lane_spec, lane_spec],
        out_shape=[lane_shape, lane_shape],
        scratch_shapes=[z.pack_scratch()],
        compiler_params=params(),
        cost_estimate=pl.CostEstimate(flops=10**7, bytes_accessed=16 * 10**6, transcendentals=0),
    )(affine, conv, *parts)
    return jnp.sum(shift, axis=(1, 2)), jnp.sum(gain, axis=(1, 2))


def conv_backward(z, taps, terms, parts, conv, x, cot, land):
    size = block_of(z.chan, 5)
    count = len(parts)
    reach = z.rows + 2 * z.margin
    ntaps = z.side * z.side

    def kernel(taps_ref, terms_ref, conv_ref, x_ref, cot_ref, land_ref, *rest):
        ins, (grad_ref, taps_out, scratch, tall, grads, tall_out) = rest[:count], rest[count:]
        step = pl.program_id(0)

        @pl.when(step == 0)
        def _():
            read_packed(z, ins, scratch)
            tall[...] = jnp.zeros_like(tall)
            grads[...] = jnp.zeros_like(grads)

        lane = lax.broadcasted_iota(jnp.int32, (z.bands, z.wide), 1)
        mask = land_ref[...].astype(F32)

        def body(c, carry):
            channel = step * size + c
            mean, scale, factor, shift, gain = (terms_ref[channel, k] for k in range(5))
            for row in range(z.rows):
                centred = (conv_ref[c, row] - mean) * scale
                value = factor * (get_packed(z, scratch, channel, row) - (shift + centred * gain))
                after = pltpu.roll(value, z.width, 1)
                before = pltpu.roll(value, z.wide - z.width, 1)
                value = jnp.where(
                    lane < z.width,
                    value,
                    jnp.where(lane < z.width + z.margin, after, before),
                )
                grads[row, SUBL : SUBL + z.bands, :] = value

            def grad_row(offset):
                band, row = divmod(offset, z.rows)
                return grads[row, SUBL + band : SUBL + band + z.bands, :]

            rows = [grad_row(m - z.margin) for m in range(reach)]
            sums = [None] * z.rows
            for b in range(z.side):
                weights = [taps_ref[channel, z.side * a + b] for a in range(z.side)]
                for row in range(z.rows):
                    part = weights[0] * rows[row + 2 * z.margin]
                    for a in range(1, z.side):
                        part = part + weights[a] * rows[row + 2 * z.margin - a]
                    if b != z.margin:
                        part = pltpu.roll(part, (b - z.margin) % z.wide, 1)
                    sums[row] = part if b == 0 else sums[row] + part
            for row in range(z.rows):
                put_band_row(z, tall_out, row, sums[row])
            transposed = jnp.concatenate(
                [tall_out[j, z.top : z.top + z.height, :] for j in range(z.tiles)], axis=1
            )[:, : z.width]
            grad_ref[c] = (mask * cot_ref[c].astype(F32) + transposed).astype(BF16)

            put_tall(z, tall, x_ref[c].astype(F32))
            rows = [band_row(z, tall, m - z.margin) for m in range(reach)]
            for b in range(z.side):
                moved = [grads[row, SUBL : SUBL + z.bands, :] for row in range(z.rows)]
                if b != z.margin:
                    moved = [pltpu.roll(m, (b - z.margin) % z.wide, 1) for m in moved]
                for a in range(z.side):
                    total = moved[0] * rows[a]
                    for row in range(1, z.rows):
                        total = total + moved[row] * rows[row + a]
                    tap = z.side * a + b
                    taps_out[c, tap : tap + 1, :] = lane_sum(z, total)
            return carry

        lax.fori_loop(0, size, body, 0)

    grad, products = pl.pallas_call(
        kernel,
        grid=(z.chan // size,),
        in_specs=[
            smem(), smem(), banded(z, size), images(z, size), images(z, size),
            whole((z.height, z.width)),
        ]
        + [whole(p.shape) for p in parts],
        out_specs=[
            images(z, size), pl.BlockSpec((size, ntaps, LANES), lambda g: (g, 0, 0)),
        ],
        out_shape=[
            jax.ShapeDtypeStruct((z.chan, z.height, z.width), BF16),
            jax.ShapeDtypeStruct((z.chan, ntaps, LANES), F32),
        ],
        scratch_shapes=[
            z.pack_scratch(),
            z.tall_scratch(),
            pltpu.VMEM((z.rows, z.bands + 2 * SUBL, z.wide), F32),
            z.tall_scratch(),
        ],
        compiler_params=params(),
        cost_estimate=pl.CostEstimate(
            flops=3 * 10**10, bytes_accessed=30 * 10**6, transcendentals=0
        ),
    )(taps, terms, conv, x, cot, land, *parts)
    return grad, jnp.sum(products, axis=2).T


def mix_branch(z, parts, x, land):
    size = block_of(z.chan, 10)
    count = len(parts)

    def kernel(x_ref, land_ref, *rest):
        ins, (out_ref, scratch, tall) = rest[:count], rest[count:]
        step = pl.program_id(0)

        @pl.when(step == 0)
        def _():
            read_packed(z, ins, scratch)

        mask = land_ref[...].astype(F32)

        def body(c, carry):
            for row in range(z.rows):
                put_band_row(z, tall, row, get_packed(z, scratch, step * size + c, row))
            branch = jnp.concatenate(
                [tall[j, z.top : z.top + z.height, :] for j in range(z.tiles)], axis=1
            )[:, : z.width]
            out_ref[c] = (mask * (x_ref[c].astype(F32) + branch)).astype(BF16)
            return carry

        lax.fori_loop(0, size, body, 0)

    return pl.pallas_call(
        kernel,
        grid=(z.chan // size,),
        in_specs=[images(z, size), whole((z.height, z.width))] + [whole(p.shape) for p in parts],
        out_specs=images(z, size),
        out_shape=jax.ShapeDtypeStruct((z.chan, z.height, z.width), BF16),
        scratch_shapes=[z.pack_scratch(), z.tall_scratch()],
        compiler_params=params(),
        cost_estimate=pl.CostEstimate(flops=10**7, bytes_accessed=16 * 10**6, transcendentals=0),
    )(x, land, *parts)


def exchange(value):
    return lax.all_to_all(value, "chan", split_axis=0, concat_axis=0, tiled=True)


def after(value, *others):
    return lax.optimization_barrier((value, *others))[0]


def sum_over_devices(partial):
    rows, hidden = partial.shape
    count = lax.axis_size("chan")
    ways = lax.axis_size("dp")
    odd = lax.rem(lax.axis_index("chan"), 2)
    half = rows // 2
    pairs = [(i, i ^ 1) for i in range(count)]
    mine = lax.dynamic_slice_in_dim(partial, odd * half, half, 0)
    other = lax.ppermute(lax.dynamic_slice_in_dim(partial, (1 - odd) * half, half, 0), "chan", pairs)
    both = (mine.astype(F32) + other.astype(F32)).astype(BF16)
    quarters = lax.all_to_all(both, "dp", split_axis=0, concat_axis=0, tiled=True)
    summed = jnp.sum(quarters.reshape(ways, half // ways, hidden).astype(F32), axis=0).astype(BF16)
    same_core = [list(range(core, count, 2)) for core in range(2)]
    shares = lax.all_gather(summed, "chan", axis_index_groups=same_core)
    summed = jnp.sum(shares.astype(F32), axis=0).astype(BF16)
    ours = lax.all_gather(summed, "dp", tiled=True)
    theirs = lax.ppermute(ours, "chan", pairs)
    low = jnp.where(odd == 0, ours, theirs)
    high = jnp.where(odd == 0, theirs, ours)
    return jnp.concatenate([low, high], axis=0)


def per_device(
    x_in, cotangent, land, grid_res, dw_kernel, gain, shift, res_bias, w_in, b_in, w_out, b_out
):
    samples, height, columns, chan = x_in.shape
    groups = lax.axis_size("chan")
    first = lax.axis_index("chan") * chan
    width = chan * groups
    z = Sizes(chan, height, columns, groups, dw_kernel.shape[0])
    pixels = float(samples * lax.axis_size("dp") * height * columns)
    parts = 3
    lengths = [z.units // parts * LANES] * parts

    def own(values, axis=0):
        return lax.dynamic_slice_in_dim(values, first, chan, axis)

    x = jnp.transpose(x_in[0], (2, 0, 1))
    cot = jnp.transpose(cotangent[0], (2, 0, 1))
    land2 = land[0]

    (grad_packed,), part_b_out = pack_out_grad(z, [sum(lengths)], cot, land2)
    grad_band = exchange(grad_packed)

    taps = own(dw_kernel, 1).astype(F32).T
    conv, total, square = conv_forward(z, taps, after(x, grad_packed))
    total, square = lax.psum((total, square), "dp")
    mean = total / pixels
    var = square / pixels - mean * mean
    scale = lax.rsqrt(var + 1e-05)
    own_gain = own(gain)
    chooser = (grid_res[:, None] == jnp.arange(2, dtype=jnp.int32)[None, :]).astype(F32)
    sample_bias = jnp.sum(chooser[0][:, None] * own(res_bias, 1), axis=0)
    affine = jnp.stack([mean, own_gain * scale, own(shift) + sample_bias], axis=1)
    packed = pack_normed(z, lengths, conv, affine)
    w_in_late, w_out_late = after(w_in, packed[0]), after(w_out, packed[0])
    w_in_t, w_out_t = w_in_late.T, w_out_late.T

    normed, before = [], grad_band
    for part in packed:
        before = exchange(after(part, before))
        normed.append(before)

    norm_parts, active, hidden_grad, bias, branch = [], [], [], 0.0, None
    for k, part in enumerate(normed):
        branch, norm, active_k, hidden_k, bias_k = mlp(
            z, k, part, grad_band, w_in_t, w_in_late, w_out_late, w_out_t,
            b_in[:, None], b_out[:, None], branch,
        )
        before = exchange(after(norm, before))
        norm_parts.append(before)
        active.append(active_k)
        hidden_grad.append(hidden_k)
        bias = bias + jnp.sum(bias_k, axis=1)

    g_w_out_t = weight_grad([(grad_band, k) for k in range(parts)], active)
    g_w_in = weight_grad([(part, None) for part in normed], hidden_grad)
    g_w_out_t = sum_over_devices(g_w_out_t)
    g_w_in = sum_over_devices(g_w_in)
    branch = exchange(after(branch, before))

    part_shift, part_gain = norm_sums(
        z, norm_parts, conv, jnp.stack([mean, scale], axis=1)
    )
    total_shift, total_gain = lax.psum((part_shift, part_gain), "dp")
    terms = jnp.stack(
        [mean, scale, own_gain * scale, total_shift / pixels, total_gain / pixels], axis=1
    )
    x_grad, g_kernel = conv_backward(z, taps, terms, norm_parts, conv, x, cot, land2)
    mixed = mix_branch(z, [branch], x, land2)

    rows = jnp.concatenate(
        [
            g_kernel,
            part_gain[None],
            part_shift[None],
            chooser[0][:, None] * part_shift[None],
            part_b_out[None],
        ],
        axis=0,
    )
    gathered = lax.all_gather(rows, ("dp", "chan"))
    gathered = gathered.reshape(lax.axis_size("dp"), groups, rows.shape[0], chan)
    placed = jnp.transpose(jnp.sum(gathered, axis=0), (1, 0, 2)).reshape(rows.shape[0], width)
    g_b_in = jnp.sum(lax.all_gather(bias, ("dp", "chan")), axis=0)
    count = dw_kernel.shape[0]

    return (
        jnp.transpose(mixed, (1, 2, 0))[None],
        jnp.transpose(x_grad, (1, 2, 0))[None],
        placed[:count],
        placed[count],
        placed[count + 1],
        placed[count + 2 : count + 4],
        unpad_rows(z, g_w_in),
        g_b_in,
        unpad_rows(z, g_w_out_t).T,
        placed[count + 4],
    )


def solution(mesh):
    cells = P("dp", None, None, "chan")
    return jax.shard_map(
        per_device,
        mesh=mesh,
        in_specs=(cells, cells, P("dp", None, None), P("dp")) + (P(),) * 8,
        out_specs=(cells, cells) + (P(),) * 8,
        check_vma=False,
    )
```

```python
from functools import partial
import math

import jax
import jax.numpy as jnp
from jax import lax
from jax.experimental import pallas as pl
from jax.experimental.pallas import tpu as pltpu
from jax.sharding import PartitionSpec as P

LANES = 128
SUBL = 8
VMEM_LIMIT = 56 * 1024 * 1024
F32 = jnp.float32
BF16 = jnp.bfloat16


def round_up(value, step):
    return (value + step - 1) // step * step


def block_of(total, most):
    return max(size for size in range(1, most + 1) if total % size == 0)


class Sizes:
    def __init__(self, chan, height, width, bands, taps):
        self.chan, self.height, self.width, self.bands = chan, height, width, bands
        self.side = math.isqrt(taps)
        self.margin = self.side // 2
        self.rows = height // bands
        self.wide = round_up(width + 2 * self.margin, LANES)
        self.tiles = self.wide // LANES
        self.tail = width - (self.tiles - 1) * LANES
        self.pad = round_up(chan + 1, SUBL)
        self.stride = self.pad + 1
        self.packed_rows = bands * self.pad
        self.tail_units = round_up(self.rows * self.tail, LANES) // LANES
        self.units = self.rows * (self.tiles - 1) + self.tail_units
        self.top = SUBL
        self.tall = height + 2 * SUBL

    def tall_scratch(self):
        return pltpu.VMEM((self.tiles, self.tall, LANES), F32)

    def pack_scratch(self):
        return pltpu.VMEM((self.units, round_up(self.bands * self.stride, SUBL), LANES), F32)


def params(semantics=("arbitrary",)):
    return pltpu.CompilerParams(dimension_semantics=semantics, vmem_limit_bytes=VMEM_LIMIT)


def split_tiles(z, value):
    return [value[:, LANES * j : LANES * (j + 1)] for j in range(z.tiles)]


def put_tall(z, tall, value):
    rows = value.shape[0]
    value = jnp.concatenate([value, jnp.zeros((rows, z.wide - z.width), F32)], axis=1)
    for j, tile in enumerate(split_tiles(z, value)):
        tall[j, z.top : z.top + rows, :] = tile


def put_tall_wrapped(z, tall, value):
    rows = value.shape[0]
    gap = jnp.zeros((rows, z.wide - z.width - 2 * z.margin), F32)
    value = jnp.concatenate(
        [value, value[:, : z.margin], gap, value[:, z.width - z.margin :]], axis=1
    )
    for j, tile in enumerate(split_tiles(z, value)):
        tall[j, z.top : z.top + rows, :] = tile


def band_row(z, tall, offset):
    return jnp.concatenate(
        [tall[j, pl.ds(z.top + offset, z.bands, stride=z.rows), :] for j in range(z.tiles)], axis=1
    )


def put_band_row(z, tall, offset, value):
    for j, tile in enumerate(split_tiles(z, value)):
        tall[j, pl.ds(z.top + offset, z.bands, stride=z.rows), :] = tile


def put_packed(z, scratch, channel, values):
    at = pl.ds(channel, z.bands, stride=z.stride)
    lane = lax.broadcasted_iota(jnp.int32, (z.bands, LANES), 1)
    full = z.tiles - 1
    for row, value in enumerate(values):
        for j in range(full):
            scratch[row * full + j, at, :] = value[:, LANES * j : LANES * (j + 1)]
    tails = [value[:, LANES * full :] for value in values]
    for t in range(z.tail_units):
        begin, tile = LANES * t, None
        for row, tail in enumerate(tails):
            low = z.tail * row - begin
            if low >= LANES or low + z.tail <= 0:
                continue
            moved = pltpu.roll(tail, low % LANES, 1) if low % LANES else tail
            tile = moved if tile is None else jnp.where(lane >= low, moved, tile)
        end = z.tail * z.rows - begin
        if end < LANES:
            tile = jnp.where(lane < end, tile, 0.0)
        scratch[z.rows * full + t, at, :] = tile


def get_packed(z, scratch, channel):
    at = pl.ds(channel, z.bands, stride=z.stride)
    lane = lax.broadcasted_iota(jnp.int32, (z.bands, LANES), 1)
    full = z.tiles - 1
    tiles = [scratch[z.rows * full + t, at, :] for t in range(z.tail_units)]
    values = []
    for row in range(z.rows):
        t, low = divmod(z.tail * row, LANES)
        tail = pltpu.roll(tiles[t], LANES - low, 1) if low else tiles[t]
        if LANES - low < z.tail:
            tail = jnp.where(lane < LANES - low, tail, pltpu.roll(tiles[t + 1], LANES - low, 1))
        tail = jnp.where(lane < z.tail, tail, 0.0)
        values.append(
            jnp.concatenate([scratch[row * full + j, at, :] for j in range(full)] + [tail], axis=1)
        )
    return values


def fill_packed_pad(z, scratch, first):
    at_rows = z.units
    for channel in range(z.chan, z.pad):
        value = jnp.full((z.bands, LANES), first if channel == z.chan else 0.0, F32)
        for unit in range(at_rows):
            scratch[unit, pl.ds(channel, z.bands, stride=z.stride), :] = value


def write_packed(z, scratch, refs):
    unit = 0
    for ref in refs:
        for k in range(ref.shape[1] // LANES):
            value = jnp.concatenate(
                [scratch[unit, z.stride * g : z.stride * g + z.pad, :] for g in range(z.bands)],
                axis=0,
            )
            ref[:, LANES * k : LANES * (k + 1)] = value.astype(BF16)
            unit += 1


def read_packed(z, refs, scratch):
    unit = 0
    for ref in refs:
        for k in range(ref.shape[1] // LANES):
            value = ref[:, LANES * k : LANES * (k + 1)].astype(F32)
            for g in range(z.bands):
                scratch[unit, z.stride * g : z.stride * g + z.pad, :] = value[
                    z.pad * g : z.pad * (g + 1), :
                ]
            unit += 1


def band_rows_of(z, tall):
    return [band_row(z, tall, row) for row in range(z.rows)]


def whole(shape):
    return pl.BlockSpec(shape, lambda *_: (0,) * len(shape))


def smem():
    return pl.BlockSpec(memory_space=pltpu.SMEM)


def images(z, size):
    return pl.BlockSpec((size, z.height, z.width), lambda g: (g, 0, 0))


def banded(z, size):
    return pl.BlockSpec((size, z.rows, z.bands, z.wide), lambda g: (g, 0, 0, 0))


def lane_sum(z, value):
    return jnp.sum(sum(split_tiles(z, value)), axis=0, keepdims=True)


def pack_out_grad(z, lengths, cot, land):
    size = block_of(z.chan, 10)

    def kernel(cot_ref, land_ref, *rest):
        outs, sums_ref, scratch, tall = rest[: len(lengths)], *rest[len(lengths) :]
        step = pl.program_id(0)

        @pl.when(step == 0)
        def _():
            fill_packed_pad(z, scratch, 0.0)

        mask = land_ref[...].astype(F32)

        def body(c, carry):
            value = cot_ref[c].astype(F32) * mask
            put_tall(z, tall, value)
            sums_ref[c, :, :] = jnp.sum(value, axis=0, keepdims=True)
            put_packed(z, scratch, step * size + c, band_rows_of(z, tall))
            return carry

        lax.fori_loop(0, size, body, 0)

        @pl.when(step == pl.num_programs(0) - 1)
        def _():
            write_packed(z, scratch, outs)

    packed = [jax.ShapeDtypeStruct((z.packed_rows, n), BF16) for n in lengths]
    out = pl.pallas_call(
        kernel,
        grid=(z.chan // size,),
        in_specs=[images(z, size), whole((z.height, z.width))],
        out_specs=[whole(p.shape) for p in packed]
        + [pl.BlockSpec((size, 1, z.width), lambda g: (g, 0, 0))],
        out_shape=packed + [jax.ShapeDtypeStruct((z.chan, 1, z.width), F32)],
        scratch_shapes=[z.pack_scratch(), z.tall_scratch()],
        compiler_params=params(),
        cost_estimate=pl.CostEstimate(flops=10**7, bytes_accessed=16 * 10**6, transcendentals=0),
    )(cot, land)
    return out[:-1], jnp.sum(out[-1], axis=(1, 2))


def conv_forward(z, taps, x):
    size = block_of(z.chan, 10)

    def kernel(taps_ref, x_ref, conv_ref, sum_ref, square_ref, tall):
        step = pl.program_id(0)

        @pl.when(step == 0)
        def _():
            tall[...] = jnp.zeros_like(tall)

        keep = lax.broadcasted_iota(jnp.int32, (z.bands, z.wide), 1) < z.width

        def body(c, carry):
            put_tall_wrapped(z, tall, x_ref[c].astype(F32))
            rows = [band_row(z, tall, m - z.margin) for m in range(z.rows + 2 * z.margin)]
            sums = [None] * z.rows
            for b in range(z.side):
                weights = [taps_ref[step * size + c, z.side * a + b] for a in range(z.side)]
                for row in range(z.rows):
                    part = weights[0] * rows[row]
                    for a in range(1, z.side):
                        part = part + weights[a] * rows[row + a]
                    if b != z.margin:
                        part = pltpu.roll(part, (z.margin - b) % z.wide, 1)
                    sums[row] = part if b == 0 else sums[row] + part
            total = jnp.zeros((z.bands, z.wide), F32)
            square = jnp.zeros((z.bands, z.wide), F32)
            for row in range(z.rows):
                value = jnp.where(keep, sums[row], 0.0)
                conv_ref[c, row] = value
                total = total + value
                square = square + value * value
            sum_ref[c] = lane_sum(z, total)
            square_ref[c] = lane_sum(z, square)
            return carry

        lax.fori_loop(0, size, body, 0)

    lane_spec = pl.BlockSpec((size, 1, LANES), lambda g: (g, 0, 0))
    lane_shape = jax.ShapeDtypeStruct((z.chan, 1, LANES), F32)
    conv, total, square = pl.pallas_call(
        kernel,
        grid=(z.chan // size,),
        in_specs=[smem(), images(z, size)],
        out_specs=[banded(z, size), lane_spec, lane_spec],
        out_shape=[
            jax.ShapeDtypeStruct((z.chan, z.rows, z.bands, z.wide), F32),
            lane_shape,
            lane_shape,
        ],
        scratch_shapes=[z.tall_scratch()],
        compiler_params=params(),
        cost_estimate=pl.CostEstimate(
            flops=10**10, bytes_accessed=16 * 10**6, transcendentals=0
        ),
    )(taps, x)
    return conv, jnp.sum(total, axis=(1, 2)), jnp.sum(square, axis=(1, 2))


def pack_normed(z, lengths, conv, affine):
    size = block_of(z.chan, 10)

    def kernel(affine_ref, conv_ref, *rest):
        outs, scratch = rest[:-1], rest[-1]
        step = pl.program_id(0)

        @pl.when(step == 0)
        def _():
            fill_packed_pad(z, scratch, 1.0)

        def body(c, carry):
            channel = step * size + c
            mean, factor, offset = (affine_ref[channel, k] for k in range(3))
            put_packed(
                z, scratch, channel,
                [(conv_ref[c, row] - mean) * factor + offset for row in range(z.rows)],
            )
            return carry

        lax.fori_loop(0, size, body, 0)

        @pl.when(step == pl.num_programs(0) - 1)
        def _():
            write_packed(z, scratch, outs)

    packed = [jax.ShapeDtypeStruct((z.packed_rows, n), BF16) for n in lengths]
    return pl.pallas_call(
        kernel,
        grid=(z.chan // size,),
        in_specs=[smem(), banded(z, size)],
        out_specs=[whole(p.shape) for p in packed],
        out_shape=packed,
        scratch_shapes=[z.pack_scratch()],
        compiler_params=params(),
        cost_estimate=pl.CostEstimate(flops=10**7, bytes_accessed=16 * 10**6, transcendentals=0),
    )(affine, conv)


def gelu_parts(h):
    span = 1.0 + (0.3275911 * math.sqrt(0.5)) * jnp.abs(h)
    t = pl.reciprocal(span, approx=True)
    t = t * (2.0 - span * t)
    bell = jnp.exp2((-0.5 / math.log(2.0)) * (h * h))
    poly = t * (
        0.5 * 0.254829592
        + t
        * (
            0.5 * -0.284496736
            + t * (0.5 * 1.421413741 + t * (0.5 * -1.453152027 + t * (0.5 * 1.061405429)))
        )
    )
    tail = poly * bell
    phi = jnp.where(h >= 0, 1.0 - tail, tail)
    return h * phi, phi + h * ((1.0 / math.sqrt(2.0 * math.pi)) * bell)


def mlp(z, start, normed, out_grad, w_in_t, w_in, w_out, w_out_t, b_in, b_out, branch_all):
    packed, cells = normed.shape
    hidden, width = w_in_t.shape
    block = block_of(hidden, 640)
    blocks = hidden // block
    groups = packed // z.pad
    pieces = [slice(k, min(k + 2 * LANES, cells)) for k in range(0, cells, 2 * LANES)]

    def kernel(
        n_ref, g_ref, w_in_t_ref, w_in_ref, w_out_ref, w_out_t_ref, b_in_ref, b_out_ref, *rest
    ):
        (
            branch_ref, norm_ref, active_ref, hidden_ref,
            n, g, branch_acc, norm_acc, h_buf, back_buf, active_buf, hidden_buf, wide_buf, out_buf,
        ) = rest[-14:]
        step = pl.program_id(0)

        def unpad(value, target):
            wide_buf[...] = value.astype(F32)
            target[...] = jnp.concatenate(
                [wide_buf[z.pad * k : z.pad * k + z.chan, :] for k in range(groups)], axis=0
            ).astype(BF16)

        def pad(source, target):
            for k in range(groups):
                wide_buf[z.pad * k : z.pad * (k + 1), :] = jnp.concatenate(
                    [
                        source[z.chan * k : z.chan * (k + 1), :],
                        jnp.zeros((z.pad - z.chan, cells), F32),
                    ],
                    axis=0,
                )
            target[...] = wide_buf[...].astype(BF16)

        def products_in(at):
            slot = lax.rem(step, 2)
            h_buf[slot, :, at] = (
                jnp.dot(w_in_t_ref[...], n[:, at], preferred_element_type=F32) + b_in_ref[...]
            )
            back_buf[slot, :, at] = jnp.dot(w_out_ref[...], g[:, at], preferred_element_type=F32)

        def gelu(at):
            slot = lax.rem(step + 1, 2)
            active, slope = gelu_parts(h_buf[slot, :, at])
            grad = (back_buf[slot, :, at] * slope).astype(BF16)
            active = active.astype(BF16)
            active_buf[slot, :, at] = active
            hidden_buf[slot, :, at] = grad
            active_ref[:, at] = active
            hidden_ref[:, at] = grad

        def products_out(at):
            slot = lax.rem(step, 2)
            branch_acc[:, at] += jnp.dot(
                w_out_t_ref[...], active_buf[slot, :, at], preferred_element_type=F32
            )
            norm_acc[:, at] += jnp.dot(
                w_in_ref[...], hidden_buf[slot, :, at], preferred_element_type=F32
            )

        def run(*stages):
            for at in pieces:
                for stage in stages:
                    stage(at)

        @pl.when(step == 0)
        def _():
            unpad(n_ref[...], n)
            unpad(g_ref[:, start : start + cells], g)
            branch_acc[...] = jnp.broadcast_to(b_out_ref[...], branch_acc.shape)
            norm_acc[...] = jnp.zeros_like(norm_acc)
            run(products_in)

        @pl.when(step == 1)
        def _():
            run(products_in, gelu)

        @pl.when((step >= 2) & (step < blocks))
        def _():
            run(products_in, gelu, products_out)

        @pl.when(step == blocks)
        def _():
            run(gelu, products_out)

        @pl.when(step == blocks + 1)
        def _():
            run(products_out)
            pad(branch_acc, out_buf)
            pltpu.sync_copy(out_buf, branch_ref.at[:, pl.ds(start, cells)])
            pad(norm_acc, norm_ref)

    def at_in(f):
        return jnp.minimum(f, blocks - 1)

    def at_gelu(f):
        return jnp.clip(f - 1, 0, blocks - 1)

    def at_out(f):
        return jnp.clip(f - 2, 0, blocks - 1)

    tall_block = pl.BlockSpec((block, width), lambda f: (at_in(f), 0))
    wide_block = pl.BlockSpec((width, block), lambda f: (0, at_out(f)))
    kept = pl.BlockSpec((block, cells), lambda f: (at_gelu(f), 0))
    anywhere = pl.BlockSpec(memory_space=pl.ANY)
    operands = [normed, out_grad, w_in_t, w_in, w_out, w_out_t, b_in, b_out]
    in_specs = [
        whole((packed, cells)), whole(out_grad.shape),
        tall_block, wide_block, tall_block, wide_block,
        pl.BlockSpec((block, 1), lambda f: (at_in(f), 0)), whole((width, 1)),
    ]
    aliases = {}
    if branch_all is not None:
        aliases = {len(operands): 0}
        operands.append(branch_all)
        in_specs.append(anywhere)
    return pl.pallas_call(
        kernel,
        grid=(blocks + 2,),
        in_specs=in_specs,
        out_specs=[anywhere, whole((packed, cells)), kept, kept],
        out_shape=[
            jax.ShapeDtypeStruct(out_grad.shape, BF16),
            jax.ShapeDtypeStruct((packed, cells), BF16),
            jax.ShapeDtypeStruct((hidden, cells), BF16),
            jax.ShapeDtypeStruct((hidden, cells), BF16),
        ],
        scratch_shapes=[
            pltpu.VMEM((width, cells), BF16), pltpu.VMEM((width, cells), BF16),
            pltpu.VMEM((width, cells), F32), pltpu.VMEM((width, cells), F32),
            pltpu.VMEM((2, block, cells), F32), pltpu.VMEM((2, block, cells), F32),
            pltpu.VMEM((2, block, cells), BF16), pltpu.VMEM((2, block, cells), BF16),
            pltpu.VMEM((packed, cells), F32), pltpu.VMEM((packed, cells), BF16),
        ],
        input_output_aliases=aliases,
        compiler_params=params(),
        cost_estimate=pl.CostEstimate(
            flops=8 * width * cells * hidden, bytes_accessed=4 * 10**7, transcendentals=cells * hidden
        ),
    )(*operands)


def weight_grad(lefts, rights):
    rows, hidden = lefts[0][0].shape[0], rights[0].shape[0]
    block = block_of(hidden, 640)
    arrays = []
    for array, _ in lefts:
        if not any(array is known for known in arrays):
            arrays.append(array)
    which = [next(k for k, known in enumerate(arrays) if known is array) for array, _ in lefts]

    def kernel(*refs):
        total = None
        for k, (_, start), right in zip(which, lefts, refs[len(arrays) : -1]):
            part = lax.dot_general(
                refs[k][:, start : start + right.shape[1]], right[...],
                (((1,), (1,)), ((), ())), preferred_element_type=F32,
            )
            total = part if total is None else total + part
        refs[-1][...] = total.astype(BF16)

    cells = sum(right.shape[1] for right in rights)
    return pl.pallas_call(
        kernel,
        grid=(hidden // block,),
        in_specs=[whole(array.shape) for array in arrays]
        + [pl.BlockSpec((block, right.shape[1]), lambda f: (f, 0)) for right in rights],
        out_specs=pl.BlockSpec((rows, block), lambda f: (0, f)),
        out_shape=jax.ShapeDtypeStruct((rows, hidden), BF16),
        compiler_params=params(),
        cost_estimate=pl.CostEstimate(
            flops=2 * rows * cells * hidden, bytes_accessed=24 * 10**6, transcendentals=0
        ),
    )(*arrays, *rights)


def unpad_rows(z, odd, ours, theirs):
    half, hidden = ours.shape[0] // z.pad, ours.shape[1]
    several = next(k for k in range(1, half + 1) if half % k == 0 and k * z.chan % SUBL == 0)
    steps = half // several

    def kernel(odd_ref, ours_ref, theirs_ref, out_ref):
        def put(ref):
            value = ref[...].astype(F32)
            for k in range(several):
                out_ref[z.chan * k : z.chan * (k + 1), :] = value[z.pad * k : z.pad * k + z.chan, :]

        mine = pl.program_id(0) == odd_ref[0]
        pl.when(mine)(lambda: put(ours_ref))
        pl.when(jnp.logical_not(mine))(lambda: put(theirs_ref))

    block = (several * z.pad, hidden)
    return pl.pallas_call(
        kernel,
        grid_spec=pltpu.PrefetchScalarGridSpec(
            num_scalar_prefetch=1,
            grid=(2, steps),
            in_specs=[
                pl.BlockSpec(block, lambda h, g, odd_ref: (jnp.where(h == odd_ref[0], g, 0), 0)),
                pl.BlockSpec(block, lambda h, g, odd_ref: (jnp.where(h == odd_ref[0], 0, g), 0)),
            ],
            out_specs=pl.BlockSpec(
                (several * z.chan, hidden), lambda h, g, odd_ref: (h * steps + g, 0)
            ),
        ),
        out_shape=jax.ShapeDtypeStruct((2 * half * z.chan, hidden), F32),
        compiler_params=params(("arbitrary", "arbitrary")),
        cost_estimate=pl.CostEstimate(flops=10**6, bytes_accessed=16 * 10**6, transcendentals=0),
    )(odd[None], ours, theirs)


def norm_sums(z, parts, conv, affine):
    size = block_of(z.chan, 10)
    count = len(parts)

    def kernel(affine_ref, conv_ref, *rest):
        ins, (shift_ref, gain_ref, scratch) = rest[:count], rest[count:]
        step = pl.program_id(0)

        @pl.when(step == 0)
        def _():
            read_packed(z, ins, scratch)

        def body(c, carry):
            channel = step * size + c
            mean, scale = affine_ref[channel, 0], affine_ref[channel, 1]
            shift = jnp.zeros((z.bands, z.wide), F32)
            gain = jnp.zeros((z.bands, z.wide), F32)
            for row, grad in enumerate(get_packed(z, scratch, channel)):
                shift = shift + grad
                gain = gain + grad * (conv_ref[c, row] - mean)
            shift_ref[c] = lane_sum(z, shift)
            gain_ref[c] = lane_sum(z, gain * scale)
            return carry

        lax.fori_loop(0, size, body, 0)

    lane_spec = pl.BlockSpec((size, 1, LANES), lambda g: (g, 0, 0))
    lane_shape = jax.ShapeDtypeStruct((z.chan, 1, LANES), F32)
    shift, gain = pl.pallas_call(
        kernel,
        grid=(z.chan // size,),
        in_specs=[smem(), banded(z, size)] + [whole(p.shape) for p in parts],
        out_specs=[lane_spec, lane_spec],
        out_shape=[lane_shape, lane_shape],
        scratch_shapes=[z.pack_scratch()],
        compiler_params=params(),
        cost_estimate=pl.CostEstimate(flops=10**7, bytes_accessed=16 * 10**6, transcendentals=0),
    )(affine, conv, *parts)
    return jnp.sum(shift, axis=(1, 2)), jnp.sum(gain, axis=(1, 2))


def conv_backward(z, taps, terms, parts, conv, x, cot, land):
    size = block_of(z.chan, 5)
    count = len(parts)
    reach = z.rows + 2 * z.margin
    ntaps = z.side * z.side

    def kernel(taps_ref, terms_ref, conv_ref, x_ref, cot_ref, land_ref, *rest):
        ins, (grad_ref, taps_out, scratch, tall, grads, tall_out) = rest[:count], rest[count:]
        step = pl.program_id(0)

        @pl.when(step == 0)
        def _():
            read_packed(z, ins, scratch)
            tall[...] = jnp.zeros_like(tall)
            grads[...] = jnp.zeros_like(grads)

        lane = lax.broadcasted_iota(jnp.int32, (z.bands, z.wide), 1)
        mask = land_ref[...].astype(F32)

        def body(c, carry):
            channel = step * size + c
            mean, scale, factor, shift, gain = (terms_ref[channel, k] for k in range(5))
            for row, grad in enumerate(get_packed(z, scratch, channel)):
                centred = (conv_ref[c, row] - mean) * scale
                value = factor * (grad - (shift + centred * gain))
                after = pltpu.roll(value, z.width, 1)
                before = pltpu.roll(value, z.wide - z.width, 1)
                value = jnp.where(
                    lane < z.width,
                    value,
                    jnp.where(lane < z.width + z.margin, after, before),
                )
                grads[row, SUBL : SUBL + z.bands, :] = value

            def grad_row(offset):
                band, row = divmod(offset, z.rows)
                return grads[row, SUBL + band : SUBL + band + z.bands, :]

            rows = [grad_row(m - z.margin) for m in range(reach)]
            sums = [None] * z.rows
            for b in range(z.side):
                weights = [taps_ref[channel, z.side * a + b] for a in range(z.side)]
                for row in range(z.rows):
                    part = weights[0] * rows[row + 2 * z.margin]
                    for a in range(1, z.side):
                        part = part + weights[a] * rows[row + 2 * z.margin - a]
                    if b != z.margin:
                        part = pltpu.roll(part, (b - z.margin) % z.wide, 1)
                    sums[row] = part if b == 0 else sums[row] + part
            for row in range(z.rows):
                put_band_row(z, tall_out, row, sums[row])
            transposed = jnp.concatenate(
                [tall_out[j, z.top : z.top + z.height, :] for j in range(z.tiles)], axis=1
            )[:, : z.width]
            grad_ref[c] = (mask * cot_ref[c].astype(F32) + transposed).astype(BF16)

            put_tall(z, tall, x_ref[c].astype(F32))
            rows = [band_row(z, tall, m - z.margin) for m in range(reach)]
            for b in range(z.side):
                moved = [grads[row, SUBL : SUBL + z.bands, :] for row in range(z.rows)]
                if b != z.margin:
                    moved = [pltpu.roll(m, (b - z.margin) % z.wide, 1) for m in moved]
                for a in range(z.side):
                    total = moved[0] * rows[a]
                    for row in range(1, z.rows):
                        total = total + moved[row] * rows[row + a]
                    tap = z.side * a + b
                    taps_out[c, tap : tap + 1, :] = lane_sum(z, total)
            return carry

        lax.fori_loop(0, size, body, 0)

    grad, products = pl.pallas_call(
        kernel,
        grid=(z.chan // size,),
        in_specs=[
            smem(), smem(), banded(z, size), images(z, size), images(z, size),
            whole((z.height, z.width)),
        ]
        + [whole(p.shape) for p in parts],
        out_specs=[
            images(z, size), pl.BlockSpec((size, ntaps, LANES), lambda g: (g, 0, 0)),
        ],
        out_shape=[
            jax.ShapeDtypeStruct((z.chan, z.height, z.width), BF16),
            jax.ShapeDtypeStruct((z.chan, ntaps, LANES), F32),
        ],
        scratch_shapes=[
            z.pack_scratch(),
            z.tall_scratch(),
            pltpu.VMEM((z.rows, z.bands + 2 * SUBL, z.wide), F32),
            z.tall_scratch(),
        ],
        compiler_params=params(),
        cost_estimate=pl.CostEstimate(
            flops=3 * 10**10, bytes_accessed=30 * 10**6, transcendentals=0
        ),
    )(taps, terms, conv, x, cot, land, *parts)
    return grad, jnp.sum(products, axis=2).T


def mix_branch(z, parts, x, land):
    size = block_of(z.chan, 10)
    count = len(parts)

    def kernel(x_ref, land_ref, *rest):
        ins, (out_ref, scratch, tall) = rest[:count], rest[count:]
        step = pl.program_id(0)

        @pl.when(step == 0)
        def _():
            read_packed(z, ins, scratch)

        mask = land_ref[...].astype(F32)

        def body(c, carry):
            for row, value in enumerate(get_packed(z, scratch, step * size + c)):
                put_band_row(z, tall, row, value)
            branch = jnp.concatenate(
                [tall[j, z.top : z.top + z.height, :] for j in range(z.tiles)], axis=1
            )[:, : z.width]
            out_ref[c] = (mask * (x_ref[c].astype(F32) + branch)).astype(BF16)
            return carry

        lax.fori_loop(0, size, body, 0)

    return pl.pallas_call(
        kernel,
        grid=(z.chan // size,),
        in_specs=[images(z, size), whole((z.height, z.width))] + [whole(p.shape) for p in parts],
        out_specs=images(z, size),
        out_shape=jax.ShapeDtypeStruct((z.chan, z.height, z.width), BF16),
        scratch_shapes=[z.pack_scratch(), z.tall_scratch()],
        compiler_params=params(),
        cost_estimate=pl.CostEstimate(flops=10**7, bytes_accessed=16 * 10**6, transcendentals=0),
    )(x, land, *parts)


CHAN = ("pair", "core")
CORES = 2


def exchange(value):
    return lax.all_to_all(value, CHAN, split_axis=0, concat_axis=0, tiled=True)


def after(value, *others):
    return lax.optimization_barrier((value, *others))[0]


def swap_cores(value):
    return lax.ppermute(value, "core", [(0, 1), (1, 0)])


def half_sum(partial, odd):
    half = partial.shape[0] // CORES
    mine = lax.dynamic_slice_in_dim(partial, odd * half, half, 0)
    other = swap_cores(lax.dynamic_slice_in_dim(partial, (1 - odd) * half, half, 0))
    return (mine.astype(F32) + other.astype(F32)).astype(BF16)


def per_device(
    x_in, cotangent, land, grid_res, dw_kernel, gain, shift, res_bias, w_in, b_in, w_out, b_out
):
    samples, height, columns, chan = x_in.shape
    groups = lax.axis_size("pair") * CORES
    odd = lax.axis_index("core")
    first = (lax.axis_index("pair") * CORES + odd) * chan
    width = chan * groups
    z = Sizes(chan, height, columns, groups, dw_kernel.shape[0])
    pixels = float(samples * lax.axis_size("dp") * height * columns)
    part = (z.units + 2) // 3 * LANES
    lengths = [part, part, z.units * LANES - 2 * part]
    starts = [0, part, 2 * part]

    def own(values, axis=0):
        return lax.dynamic_slice_in_dim(values, first, chan, axis)

    x = jnp.transpose(x_in[0], (2, 0, 1))
    cot = jnp.transpose(cotangent[0], (2, 0, 1))
    land2 = land[0]

    (grad_packed,), part_b_out = pack_out_grad(z, [sum(lengths)], cot, land2)
    grad_band = exchange(grad_packed)

    taps = own(dw_kernel, 1).astype(F32).T
    conv, total, square = conv_forward(z, taps, after(x, grad_packed))
    total, square = lax.psum((total, square), "dp")
    mean = total / pixels
    var = square / pixels - mean * mean
    scale = lax.rsqrt(var + 1e-05)
    own_gain = own(gain)
    chooser = (grid_res[:, None] == jnp.arange(2, dtype=jnp.int32)[None, :]).astype(F32)
    sample_bias = jnp.sum(chooser[0][:, None] * own(res_bias, 1), axis=0)
    affine = jnp.stack([mean, own_gain * scale, own(shift) + sample_bias], axis=1)
    packed = pack_normed(z, lengths, conv, affine)

    w_in_late, w_out_late = after(w_in, packed[0]), after(w_out, packed[0])
    w_in_t, w_out_t = w_in_late.T, w_out_late.T
    w_out_p = after(w_out_late, w_out_t)
    weights = (w_in_t, w_in_late, w_out_p, w_out_t, b_in[:, None], b_out[:, None])
    normed = [exchange(after(packed[0], grad_band))]
    normed.append(exchange(after(packed[1], normed[0], w_in_t, w_out_p)))
    branch, norm1, active1, hidden1 = mlp(z, starts[0], normed[0], grad_band, *weights, None)
    normed.append(exchange(after(packed[2], normed[1], norm1)))
    branch, norm2, active2, hidden2 = mlp(z, starts[1], normed[1], grad_band, *weights, branch)
    norm_parts = [exchange(after(norm1, normed[2], norm2))]
    branch, norm3, active3, hidden3 = mlp(z, starts[2], normed[2], grad_band, *weights, branch)
    norm_parts.append(exchange(after(norm2, norm_parts[0], norm3)))
    g_w_out_t = weight_grad(
        [(grad_band, start) for start in starts], [active1, active2, after(active3, norm_parts[0])]
    )
    norm_parts.append(exchange(after(norm3, norm_parts[1], g_w_out_t)))
    g_w_in = weight_grad(
        [(value, 0) for value in normed], [hidden1, hidden2, after(hidden3, norm_parts[1])]
    )
    others = ("dp", "pair")
    g_w_out_t = lax.psum(half_sum(g_w_out_t, odd), others)
    branch = exchange(after(branch, norm_parts[2], g_w_in))

    part_shift, part_gain = norm_sums(
        z, norm_parts, conv, jnp.stack([mean, scale], axis=1)
    )
    small = jnp.concatenate(
        [part_shift[None], part_gain[None], chooser[0][:, None] * part_shift[None], part_b_out[None]],
        axis=0,
    )
    small = lax.psum(small, "dp")
    g_w_in = lax.psum(after(half_sum(g_w_in, odd), small, g_w_out_t), others)
    terms = jnp.stack(
        [mean, scale, own_gain * scale, small[0] / pixels, small[1] / pixels], axis=1
    )
    x_grad, g_kernel = conv_backward(z, taps, terms, norm_parts, conv, x, cot, land2)
    mixed = mix_branch(z, [branch], x, land2)
    g_w_out_2, g_w_in_2 = swap_cores(g_w_out_t), swap_cores(g_w_in)
    g_b_in = jnp.where(odd == 0, g_w_in[chan], g_w_in_2[chan]).astype(F32)

    rows = jnp.concatenate([lax.psum(g_kernel, "dp"), small], axis=0)
    gathered = lax.all_gather(rows, CHAN)
    placed = jnp.transpose(gathered, (1, 0, 2)).reshape(rows.shape[0], width)
    count = dw_kernel.shape[0]

    return (
        jnp.transpose(mixed, (1, 2, 0))[None],
        jnp.transpose(x_grad, (1, 2, 0))[None],
        placed[:count],
        placed[count + 1],
        placed[count],
        placed[count + 2 : count + 4],
        unpad_rows(z, odd, g_w_in, g_w_in_2),
        g_b_in,
        unpad_rows(z, odd, g_w_out_t, g_w_out_2).T,
        placed[count + 4],
    )


def solution(mesh):
    shape = mesh.shape
    mesh = jax.sharding.Mesh(
        mesh.devices.reshape(shape["dp"], shape["chan"] // CORES, CORES), ("dp",) + CHAN
    )
    cells = P("dp", None, None, CHAN)
    return jax.shard_map(
        per_device,
        mesh=mesh,
        in_specs=(cells, cells, P("dp", None, None), P("dp")) + (P(),) * 8,
        out_specs=(cells, cells) + (P(),) * 8,
        check_vma=False,
    )
```

```python
from functools import partial
import math

import jax
import jax.numpy as jnp
from jax import lax
from jax.experimental import pallas as pl
from jax.experimental.pallas import tpu as pltpu
from jax.sharding import PartitionSpec as P

LANES = 128
SUBL = 8
VMEM_LIMIT = 56 * 1024 * 1024
CHAN = ("pair", "core")
CORES = 2
F32 = jnp.float32
BF16 = jnp.bfloat16


def round_up(value, step):
    return (value + step - 1) // step * step


def block_of(total, most):
    return max(size for size in range(1, most + 1) if total % size == 0)


class Sizes:
    def __init__(self, chan, height, width, bands, taps):
        self.chan, self.height, self.width, self.bands = chan, height, width, bands
        self.side = math.isqrt(taps)
        self.margin = self.side // 2
        self.rows = height // bands
        self.wide = round_up(width + 2 * self.margin, LANES)
        self.tiles = self.wide // LANES
        self.tail = width - (self.tiles - 1) * LANES
        self.pad = round_up(chan + 1, SUBL)
        self.stride = self.pad + 1
        self.packed_rows = bands * self.pad
        self.tail_units = round_up(self.rows * self.tail, LANES) // LANES
        self.units = self.rows * (self.tiles - 1) + self.tail_units
        self.top = SUBL
        self.tall = height + 2 * SUBL

    def tall_scratch(self):
        return pltpu.VMEM((self.tiles, self.tall, LANES), F32)

    def pack_scratch(self):
        return pltpu.VMEM((self.units, round_up(self.bands * self.stride, SUBL), LANES), F32)


def params(semantics=("arbitrary",)):
    return pltpu.CompilerParams(dimension_semantics=semantics, vmem_limit_bytes=VMEM_LIMIT)


def split_tiles(z, value):
    return [value[:, LANES * j : LANES * (j + 1)] for j in range(z.tiles)]


def put_tall(z, tall, value):
    rows = value.shape[0]
    value = jnp.concatenate([value, jnp.zeros((rows, z.wide - z.width), F32)], axis=1)
    for j, tile in enumerate(split_tiles(z, value)):
        tall[j, z.top : z.top + rows, :] = tile


def put_tall_wrapped(z, tall, value):
    rows = value.shape[0]
    gap = jnp.zeros((rows, z.wide - z.width - 2 * z.margin), F32)
    value = jnp.concatenate(
        [value, value[:, : z.margin], gap, value[:, z.width - z.margin :]], axis=1
    )
    for j, tile in enumerate(split_tiles(z, value)):
        tall[j, z.top : z.top + rows, :] = tile


def band_row(z, tall, offset):
    return jnp.concatenate(
        [tall[j, pl.ds(z.top + offset, z.bands, stride=z.rows), :] for j in range(z.tiles)], axis=1
    )


def put_band_row(z, tall, offset, value):
    for j, tile in enumerate(split_tiles(z, value)):
        tall[j, pl.ds(z.top + offset, z.bands, stride=z.rows), :] = tile


def put_packed(z, scratch, channel, values):
    at = pl.ds(channel, z.bands, stride=z.stride)
    lane = lax.broadcasted_iota(jnp.int32, (z.bands, LANES), 1)
    full = z.tiles - 1
    for row, value in enumerate(values):
        for j in range(full):
            scratch[row * full + j, at, :] = value[:, LANES * j : LANES * (j + 1)]
    tails = [value[:, LANES * full :] for value in values]
    for t in range(z.tail_units):
        begin, tile = LANES * t, None
        for row, tail in enumerate(tails):
            low = z.tail * row - begin
            if low >= LANES or low + z.tail <= 0:
                continue
            moved = pltpu.roll(tail, low % LANES, 1) if low % LANES else tail
            tile = moved if tile is None else jnp.where(lane >= low, moved, tile)
        end = z.tail * z.rows - begin
        if end < LANES:
            tile = jnp.where(lane < end, tile, 0.0)
        scratch[z.rows * full + t, at, :] = tile


def get_packed(z, scratch, channel):
    at = pl.ds(channel, z.bands, stride=z.stride)
    lane = lax.broadcasted_iota(jnp.int32, (z.bands, LANES), 1)
    full = z.tiles - 1
    tiles = [scratch[z.rows * full + t, at, :] for t in range(z.tail_units)]
    values = []
    for row in range(z.rows):
        t, low = divmod(z.tail * row, LANES)
        tail = pltpu.roll(tiles[t], LANES - low, 1) if low else tiles[t]
        if LANES - low < z.tail:
            tail = jnp.where(lane < LANES - low, tail, pltpu.roll(tiles[t + 1], LANES - low, 1))
        tail = jnp.where(lane < z.tail, tail, 0.0)
        values.append(
            jnp.concatenate([scratch[row * full + j, at, :] for j in range(full)] + [tail], axis=1)
        )
    return values


def fill_packed_pad(z, scratch, first):
    at_rows = z.units
    for channel in range(z.chan, z.pad):
        value = jnp.full((z.bands, LANES), first if channel == z.chan else 0.0, F32)
        for unit in range(at_rows):
            scratch[unit, pl.ds(channel, z.bands, stride=z.stride), :] = value


def write_packed(z, scratch, refs):
    unit = 0
    for ref in refs:
        for k in range(ref.shape[1] // LANES):
            value = jnp.concatenate(
                [scratch[unit, z.stride * g : z.stride * g + z.pad, :] for g in range(z.bands)],
                axis=0,
            )
            ref[:, LANES * k : LANES * (k + 1)] = value.astype(BF16)
            unit += 1


def read_packed(z, refs, scratch):
    unit = 0
    for ref in refs:
        for k in range(ref.shape[1] // LANES):
            value = ref[:, LANES * k : LANES * (k + 1)].astype(F32)
            for g in range(z.bands):
                scratch[unit, z.stride * g : z.stride * g + z.pad, :] = value[
                    z.pad * g : z.pad * (g + 1), :
                ]
            unit += 1


def band_rows_of(z, tall):
    return [band_row(z, tall, row) for row in range(z.rows)]


def whole(shape):
    return pl.BlockSpec(shape, lambda *_: (0,) * len(shape))


def smem():
    return pl.BlockSpec(memory_space=pltpu.SMEM)


def images(z, size):
    return pl.BlockSpec((size, z.height, z.width), lambda g: (g, 0, 0))


def banded(z, size):
    return pl.BlockSpec((size, z.rows, z.bands, z.wide), lambda g: (g, 0, 0, 0))


def lane_sum(z, value):
    return jnp.sum(sum(split_tiles(z, value)), axis=0, keepdims=True)


def pack_out_grad(z, lengths, cot, land):
    size = block_of(z.chan, 10)

    def kernel(cot_ref, land_ref, *rest):
        outs, sums_ref, scratch, tall = rest[: len(lengths)], *rest[len(lengths) :]
        step = pl.program_id(0)

        @pl.when(step == 0)
        def _():
            fill_packed_pad(z, scratch, 0.0)

        mask = land_ref[...].astype(F32)

        def body(c, carry):
            value = cot_ref[c].astype(F32) * mask
            put_tall(z, tall, value)
            sums_ref[c, :, :] = jnp.sum(value, axis=0, keepdims=True)
            put_packed(z, scratch, step * size + c, band_rows_of(z, tall))
            return carry

        lax.fori_loop(0, size, body, 0)

        @pl.when(step == pl.num_programs(0) - 1)
        def _():
            write_packed(z, scratch, outs)

    packed = [jax.ShapeDtypeStruct((z.packed_rows, n), BF16) for n in lengths]
    out = pl.pallas_call(
        kernel,
        grid=(z.chan // size,),
        in_specs=[images(z, size), whole((z.height, z.width))],
        out_specs=[whole(p.shape) for p in packed]
        + [pl.BlockSpec((size, 1, z.width), lambda g: (g, 0, 0))],
        out_shape=packed + [jax.ShapeDtypeStruct((z.chan, 1, z.width), F32)],
        scratch_shapes=[z.pack_scratch(), z.tall_scratch()],
        compiler_params=params(),
        cost_estimate=pl.CostEstimate(flops=10**7, bytes_accessed=16 * 10**6, transcendentals=0),
    )(cot, land)
    return out[:-1], jnp.sum(out[-1], axis=(1, 2))


def conv_forward(z, taps, x):
    size = block_of(z.chan, 10)

    def kernel(taps_ref, x_ref, conv_ref, sum_ref, square_ref, tall):
        step = pl.program_id(0)

        @pl.when(step == 0)
        def _():
            tall[...] = jnp.zeros_like(tall)

        keep = lax.broadcasted_iota(jnp.int32, (z.bands, z.wide), 1) < z.width

        def body(c, carry):
            put_tall_wrapped(z, tall, x_ref[c].astype(F32))
            rows = [band_row(z, tall, m - z.margin) for m in range(z.rows + 2 * z.margin)]
            sums = [None] * z.rows
            for b in range(z.side):
                weights = [taps_ref[step * size + c, z.side * a + b] for a in range(z.side)]
                for row in range(z.rows):
                    part = weights[0] * rows[row]
                    for a in range(1, z.side):
                        part = part + weights[a] * rows[row + a]
                    if b != z.margin:
                        part = pltpu.roll(part, (z.margin - b) % z.wide, 1)
                    sums[row] = part if b == 0 else sums[row] + part
            total = jnp.zeros((z.bands, z.wide), F32)
            square = jnp.zeros((z.bands, z.wide), F32)
            for row in range(z.rows):
                value = jnp.where(keep, sums[row], 0.0)
                conv_ref[c, row] = value
                total = total + value
                square = square + value * value
            sum_ref[c] = lane_sum(z, total)
            square_ref[c] = lane_sum(z, square)
            return carry

        lax.fori_loop(0, size, body, 0)

    lane_spec = pl.BlockSpec((size, 1, LANES), lambda g: (g, 0, 0))
    lane_shape = jax.ShapeDtypeStruct((z.chan, 1, LANES), F32)
    conv, total, square = pl.pallas_call(
        kernel,
        grid=(z.chan // size,),
        in_specs=[smem(), images(z, size)],
        out_specs=[banded(z, size), lane_spec, lane_spec],
        out_shape=[
            jax.ShapeDtypeStruct((z.chan, z.rows, z.bands, z.wide), F32),
            lane_shape,
            lane_shape,
        ],
        scratch_shapes=[z.tall_scratch()],
        compiler_params=params(),
        cost_estimate=pl.CostEstimate(
            flops=10**10, bytes_accessed=16 * 10**6, transcendentals=0
        ),
    )(taps, x)
    return conv, jnp.sum(total, axis=(1, 2)), jnp.sum(square, axis=(1, 2))


def pack_normed(z, lengths, conv, affine):
    size = block_of(z.chan, 10)

    def kernel(affine_ref, conv_ref, *rest):
        outs, scratch = rest[:-1], rest[-1]
        step = pl.program_id(0)

        @pl.when(step == 0)
        def _():
            fill_packed_pad(z, scratch, 1.0)

        def body(c, carry):
            channel = step * size + c
            mean, factor, offset = (affine_ref[channel, k] for k in range(3))
            put_packed(
                z, scratch, channel,
                [(conv_ref[c, row] - mean) * factor + offset for row in range(z.rows)],
            )
            return carry

        lax.fori_loop(0, size, body, 0)

        @pl.when(step == pl.num_programs(0) - 1)
        def _():
            write_packed(z, scratch, outs)

    packed = [jax.ShapeDtypeStruct((z.packed_rows, n), BF16) for n in lengths]
    return pl.pallas_call(
        kernel,
        grid=(z.chan // size,),
        in_specs=[smem(), banded(z, size)],
        out_specs=[whole(p.shape) for p in packed],
        out_shape=packed,
        scratch_shapes=[z.pack_scratch()],
        compiler_params=params(),
        cost_estimate=pl.CostEstimate(flops=10**7, bytes_accessed=16 * 10**6, transcendentals=0),
    )(affine, conv)


def gelu_parts(h):
    span = 1.0 + (0.3275911 * math.sqrt(0.5)) * jnp.abs(h)
    t = pl.reciprocal(span, approx=True)
    t = t * (2.0 - span * t)
    bell = jnp.exp2((-0.5 / math.log(2.0)) * (h * h))
    poly = t * (
        0.5 * 0.254829592
        + t
        * (
            0.5 * -0.284496736
            + t * (0.5 * 1.421413741 + t * (0.5 * -1.453152027 + t * (0.5 * 1.061405429)))
        )
    )
    tail = poly * bell
    phi = jnp.where(h >= 0, 1.0 - tail, tail)
    return h * phi, phi + h * ((1.0 / math.sqrt(2.0 * math.pi)) * bell)


def lane_block(rows, cells, part):
    return pl.BlockSpec((rows, cells), lambda *_: (0, part))


def mlp(part, length, normed, out_grad, w_in_t, w_in, w_out, w_out_t, b_in, b_out, branch_all):
    packed, cells = normed.shape
    hidden = w_in_t.shape[0]
    block = block_of(hidden, 640)
    blocks = hidden // block
    pieces = [slice(k, min(k + 2 * LANES, cells)) for k in range(0, cells, 2 * LANES)]

    def kernel(
        n_ref, g_ref, w_in_t_ref, w_in_ref, w_out_ref, w_out_t_ref, b_in_ref, b_out_ref, *rest
    ):
        (
            branch_ref, norm_ref, active_ref, hidden_ref, branch_acc, norm_acc,
            h_even, h_odd, back_even, back_odd, active_even, active_odd, hidden_even, hidden_odd,
        ) = rest[-14:]
        step = pl.program_id(0)

        def run(parity, *stages):
            h_bufs, back_bufs = (h_even, h_odd), (back_even, back_odd)
            active_bufs, hidden_bufs = (active_even, active_odd), (hidden_even, hidden_odd)
            now, other = parity, 1 - parity
            for at in pieces:
                if "in" in stages:
                    h_bufs[now][:, at] = (
                        jnp.dot(w_in_t_ref[...], n_ref[:, at], preferred_element_type=F32)
                        + b_in_ref[...]
                    )
                    back_bufs[now][:, at] = jnp.dot(
                        w_out_ref[...], g_ref[:, at], preferred_element_type=F32
                    )
                if "gelu" in stages:
                    active, slope = gelu_parts(h_bufs[other][:, at])
                    grad = (back_bufs[other][:, at] * slope).astype(BF16)
                    active = active.astype(BF16)
                    active_bufs[other][:, at] = active
                    hidden_bufs[other][:, at] = grad
                    active_ref[:, at] = active
                    hidden_ref[:, at] = grad
                if "out" in stages:
                    branch_acc[:, at] += jnp.dot(
                        w_out_t_ref[...], active_bufs[now][:, at], preferred_element_type=F32
                    )
                    norm_acc[:, at] += jnp.dot(
                        w_in_ref[...], hidden_bufs[now][:, at], preferred_element_type=F32
                    )

        @pl.when(step == 0)
        def _():
            branch_acc[...] = jnp.broadcast_to(b_out_ref[...], branch_acc.shape)
            norm_acc[...] = jnp.zeros_like(norm_acc)
            run(0, "in")

        @pl.when(step == 1)
        def _():
            run(1, "in", "gelu")

        for parity in range(2):

            @pl.when((step >= 2) & (step < blocks) & (lax.rem(step, 2) == parity))
            def _():
                run(parity, "in", "gelu", "out")

        @pl.when(step == blocks)
        def _():
            run(blocks % 2, "gelu", "out")

        @pl.when(step == blocks + 1)
        def _():
            run((blocks + 1) % 2, "out")
            branch_ref[:, :cells] = branch_acc[...].astype(BF16)
            norm_ref[...] = norm_acc[...].astype(BF16)

    def at_in(f):
        return jnp.minimum(f, blocks - 1)

    def at_gelu(f):
        return jnp.clip(f - 1, 0, blocks - 1)

    def at_out(f):
        return jnp.clip(f - 2, 0, blocks - 1)

    tall_block = pl.BlockSpec((block, packed), lambda f: (at_in(f), 0))
    wide_block = pl.BlockSpec((packed, block), lambda f: (0, at_out(f)))
    kept = pl.BlockSpec((block, cells), lambda f: (at_gelu(f), 0))
    operands = [normed, out_grad, w_in_t, w_in, w_out, w_out_t, b_in, b_out]
    in_specs = [
        whole((packed, cells)), lane_block(packed, length, part),
        tall_block, wide_block, tall_block, wide_block,
        pl.BlockSpec((block, 1), lambda f: (at_in(f), 0)), whole((packed, 1)),
    ]
    aliases = {}
    if branch_all is not None:
        aliases = {len(operands): 0}
        operands.append(branch_all)
        in_specs.append(pl.BlockSpec(memory_space=pl.ANY))
    wide, narrow = pltpu.VMEM((block, cells), F32), pltpu.VMEM((block, cells), BF16)
    return pl.pallas_call(
        kernel,
        grid=(blocks + 2,),
        in_specs=in_specs,
        out_specs=[lane_block(packed, length, part), whole((packed, cells)), kept, kept],
        out_shape=[
            jax.ShapeDtypeStruct(out_grad.shape, BF16),
            jax.ShapeDtypeStruct((packed, cells), BF16),
            jax.ShapeDtypeStruct((hidden, cells), BF16),
            jax.ShapeDtypeStruct((hidden, cells), BF16),
        ],
        scratch_shapes=[pltpu.VMEM((packed, cells), F32)] * 2 + [wide] * 4 + [narrow] * 4,
        input_output_aliases=aliases,
        compiler_params=params(),
        cost_estimate=pl.CostEstimate(
            flops=8 * packed * cells * hidden, bytes_accessed=4 * 10**7, transcendentals=cells * hidden
        ),
    )(*operands)


def weight_grad(odd, lefts, rights):
    rows, hidden = lefts[0][0].shape[0], rights[0].shape[0]
    half = rows // CORES
    block = block_of(hidden, 640)
    arrays = []
    for array, _ in lefts:
        if not any(array is known for known in arrays):
            arrays.append(array)
    which = [next(k for k, known in enumerate(arrays) if known is array) for array, _ in lefts]

    def kernel(odd_ref, *refs):
        total = None
        for k, (_, start), right in zip(which, lefts, refs[len(arrays) : -3]):
            part = lax.dot_general(
                refs[k][:, start : start + right.shape[1]], right[...],
                (((1,), (1,)), ((), ())), preferred_element_type=F32,
            )
            total = part if total is None else total + part
        mine_ref, sent_ref, both = refs[-3:]
        both[0] = total[:half].astype(BF16)
        both[1] = total[half:].astype(BF16)
        mine_ref[...] = both[odd_ref[0]]
        sent_ref[...] = both[1 - odd_ref[0]]

    cells = sum(right.shape[1] for right in rights)
    out = jax.ShapeDtypeStruct((half, hidden), BF16)
    return pl.pallas_call(
        kernel,
        grid=(hidden // block,),
        in_specs=[smem()] + [whole(array.shape) for array in arrays]
        + [pl.BlockSpec((block, right.shape[1]), lambda f: (f, 0)) for right in rights],
        out_specs=[pl.BlockSpec((half, block), lambda f: (0, f))] * 2,
        out_shape=[out, out],
        scratch_shapes=[pltpu.VMEM((CORES, half, block), BF16)],
        compiler_params=params(),
        cost_estimate=pl.CostEstimate(
            flops=2 * rows * cells * hidden, bytes_accessed=24 * 10**6, transcendentals=0
        ),
    )(odd[None], *arrays, *rights)


def unpad_rows(z, odd, ours, theirs):
    half, hidden = ours.shape[0] // z.pad, ours.shape[1]
    several = next(k for k in range(1, half + 1) if half % k == 0 and k * z.chan % SUBL == 0)
    steps = half // several

    def kernel(odd_ref, ours_ref, theirs_ref, out_ref):
        def put(ref):
            value = ref[...].astype(F32)
            for k in range(several):
                out_ref[z.chan * k : z.chan * (k + 1), :] = value[z.pad * k : z.pad * k + z.chan, :]

        mine = pl.program_id(0) == odd_ref[0]
        pl.when(mine)(lambda: put(ours_ref))
        pl.when(jnp.logical_not(mine))(lambda: put(theirs_ref))

    block = (several * z.pad, hidden)
    return pl.pallas_call(
        kernel,
        grid_spec=pltpu.PrefetchScalarGridSpec(
            num_scalar_prefetch=1,
            grid=(2, steps),
            in_specs=[
                pl.BlockSpec(block, lambda h, g, odd_ref: (jnp.where(h == odd_ref[0], g, 0), 0)),
                pl.BlockSpec(block, lambda h, g, odd_ref: (jnp.where(h == odd_ref[0], 0, g), 0)),
            ],
            out_specs=pl.BlockSpec(
                (several * z.chan, hidden), lambda h, g, odd_ref: (h * steps + g, 0)
            ),
        ),
        out_shape=jax.ShapeDtypeStruct((2 * half * z.chan, hidden), F32),
        compiler_params=params(("arbitrary", "arbitrary")),
        cost_estimate=pl.CostEstimate(flops=10**6, bytes_accessed=16 * 10**6, transcendentals=0),
    )(odd[None], ours, theirs)


def norm_sums(z, parts, conv, affine):
    size = block_of(z.chan, 10)
    count = len(parts)

    def kernel(affine_ref, conv_ref, *rest):
        ins, (shift_ref, gain_ref, scratch) = rest[:count], rest[count:]
        step = pl.program_id(0)

        @pl.when(step == 0)
        def _():
            read_packed(z, ins, scratch)

        def body(c, carry):
            channel = step * size + c
            mean, scale = affine_ref[channel, 0], affine_ref[channel, 1]
            shift = jnp.zeros((z.bands, z.wide), F32)
            gain = jnp.zeros((z.bands, z.wide), F32)
            for row, grad in enumerate(get_packed(z, scratch, channel)):
                shift = shift + grad
                gain = gain + grad * (conv_ref[c, row] - mean)
            shift_ref[c] = lane_sum(z, shift)
            gain_ref[c] = lane_sum(z, gain * scale)
            return carry

        lax.fori_loop(0, size, body, 0)

    lane_spec = pl.BlockSpec((size, 1, LANES), lambda g: (g, 0, 0))
    lane_shape = jax.ShapeDtypeStruct((z.chan, 1, LANES), F32)
    shift, gain = pl.pallas_call(
        kernel,
        grid=(z.chan // size,),
        in_specs=[smem(), banded(z, size)] + [whole(p.shape) for p in parts],
        out_specs=[lane_spec, lane_spec],
        out_shape=[lane_shape, lane_shape],
        scratch_shapes=[z.pack_scratch()],
        compiler_params=params(),
        cost_estimate=pl.CostEstimate(flops=10**7, bytes_accessed=16 * 10**6, transcendentals=0),
    )(affine, conv, *parts)
    return jnp.sum(shift, axis=(1, 2)), jnp.sum(gain, axis=(1, 2))


def conv_backward(z, taps, terms, parts, conv, x, cot, land):
    size = block_of(z.chan, 5)
    count = len(parts)
    reach = z.rows + 2 * z.margin
    ntaps = z.side * z.side

    def kernel(taps_ref, terms_ref, conv_ref, x_ref, cot_ref, land_ref, *rest):
        ins, (grad_ref, taps_out, scratch, tall, grads, tall_out) = rest[:count], rest[count:]
        step = pl.program_id(0)

        @pl.when(step == 0)
        def _():
            read_packed(z, ins, scratch)
            tall[...] = jnp.zeros_like(tall)
            grads[...] = jnp.zeros_like(grads)

        lane = lax.broadcasted_iota(jnp.int32, (z.bands, z.wide), 1)
        mask = land_ref[...].astype(F32)

        def body(c, carry):
            channel = step * size + c
            mean, scale, factor, shift, gain = (terms_ref[channel, k] for k in range(5))
            for row, grad in enumerate(get_packed(z, scratch, channel)):
                centred = (conv_ref[c, row] - mean) * scale
                value = factor * (grad - (shift + centred * gain))
                after = pltpu.roll(value, z.width, 1)
                before = pltpu.roll(value, z.wide - z.width, 1)
                value = jnp.where(
                    lane < z.width,
                    value,
                    jnp.where(lane < z.width + z.margin, after, before),
                )
                grads[row, SUBL : SUBL + z.bands, :] = value

            def grad_row(offset):
                band, row = divmod(offset, z.rows)
                return grads[row, SUBL + band : SUBL + band + z.bands, :]

            rows = [grad_row(m - z.margin) for m in range(reach)]
            sums = [None] * z.rows
            for b in range(z.side):
                weights = [taps_ref[channel, z.side * a + b] for a in range(z.side)]
                for row in range(z.rows):
                    part = weights[0] * rows[row + 2 * z.margin]
                    for a in range(1, z.side):
                        part = part + weights[a] * rows[row + 2 * z.margin - a]
                    if b != z.margin:
                        part = pltpu.roll(part, (b - z.margin) % z.wide, 1)
                    sums[row] = part if b == 0 else sums[row] + part
            for row in range(z.rows):
                put_band_row(z, tall_out, row, sums[row])
            transposed = jnp.concatenate(
                [tall_out[j, z.top : z.top + z.height, :] for j in range(z.tiles)], axis=1
            )[:, : z.width]
            grad_ref[c] = (mask * cot_ref[c].astype(F32) + transposed).astype(BF16)

            put_tall(z, tall, x_ref[c].astype(F32))
            rows = [band_row(z, tall, m - z.margin) for m in range(reach)]
            for b in range(z.side):
                moved = [grads[row, SUBL : SUBL + z.bands, :] for row in range(z.rows)]
                if b != z.margin:
                    moved = [pltpu.roll(m, (b - z.margin) % z.wide, 1) for m in moved]
                for a in range(z.side):
                    total = moved[0] * rows[a]
                    for row in range(1, z.rows):
                        total = total + moved[row] * rows[row + a]
                    tap = z.side * a + b
                    taps_out[c, tap : tap + 1, :] = lane_sum(z, total)
            return carry

        lax.fori_loop(0, size, body, 0)

    grad, products = pl.pallas_call(
        kernel,
        grid=(z.chan // size,),
        in_specs=[
            smem(), smem(), banded(z, size), images(z, size), images(z, size),
            whole((z.height, z.width)),
        ]
        + [whole(p.shape) for p in parts],
        out_specs=[
            images(z, size), pl.BlockSpec((size, ntaps, LANES), lambda g: (g, 0, 0)),
        ],
        out_shape=[
            jax.ShapeDtypeStruct((z.chan, z.height, z.width), BF16),
            jax.ShapeDtypeStruct((z.chan, ntaps, LANES), F32),
        ],
        scratch_shapes=[
            z.pack_scratch(),
            z.tall_scratch(),
            pltpu.VMEM((z.rows, z.bands + 2 * SUBL, z.wide), F32),
            z.tall_scratch(),
        ],
        compiler_params=params(),
        cost_estimate=pl.CostEstimate(
            flops=3 * 10**10, bytes_accessed=30 * 10**6, transcendentals=0
        ),
    )(taps, terms, conv, x, cot, land, *parts)
    return grad, jnp.sum(products, axis=2).T


def mix_branch(z, parts, x, land):
    size = block_of(z.chan, 10)
    count = len(parts)

    def kernel(x_ref, land_ref, *rest):
        ins, (out_ref, scratch, tall) = rest[:count], rest[count:]
        step = pl.program_id(0)

        @pl.when(step == 0)
        def _():
            read_packed(z, ins, scratch)

        mask = land_ref[...].astype(F32)

        def body(c, carry):
            for row, value in enumerate(get_packed(z, scratch, step * size + c)):
                put_band_row(z, tall, row, value)
            branch = jnp.concatenate(
                [tall[j, z.top : z.top + z.height, :] for j in range(z.tiles)], axis=1
            )[:, : z.width]
            out_ref[c] = (mask * (x_ref[c].astype(F32) + branch)).astype(BF16)
            return carry

        lax.fori_loop(0, size, body, 0)

    return pl.pallas_call(
        kernel,
        grid=(z.chan // size,),
        in_specs=[images(z, size), whole((z.height, z.width))] + [whole(p.shape) for p in parts],
        out_specs=images(z, size),
        out_shape=jax.ShapeDtypeStruct((z.chan, z.height, z.width), BF16),
        scratch_shapes=[z.pack_scratch(), z.tall_scratch()],
        compiler_params=params(),
        cost_estimate=pl.CostEstimate(flops=10**7, bytes_accessed=16 * 10**6, transcendentals=0),
    )(x, land, *parts)


def exchange(value):
    return lax.all_to_all(value, CHAN, split_axis=0, concat_axis=0, tiled=True)


def after(value, *others):
    return lax.optimization_barrier((value, *others))[0]


def swap_cores(value):
    return lax.ppermute(value, "core", [(0, 1), (1, 0)])


def quarter_sum(mine, other):
    ways = lax.axis_size("dp")
    place = lax.axis_index("dp")
    rows = mine.shape[0] // ways

    def share(index):
        at = index * rows
        return lax.dynamic_slice_in_dim(mine, at, rows, 0).astype(F32) + lax.dynamic_slice_in_dim(
            other, at, rows, 0
        ).astype(F32)

    total = share(place)
    for turn in range(1, ways):
        sent = share(jnp.bitwise_xor(place, turn)).astype(BF16)
        pairs = [(i, i ^ turn) for i in range(ways)]
        total = total + lax.ppermute(sent, "dp", pairs).astype(F32)
    return total.astype(BF16)


def per_device(
    x_in, cotangent, land, grid_res, dw_kernel, gain, shift, res_bias, w_in, b_in, w_out, b_out
):
    samples, height, columns, chan = x_in.shape
    groups = lax.axis_size("pair") * CORES
    odd = lax.axis_index("core")
    first = (lax.axis_index("pair") * CORES + odd) * chan
    width = chan * groups
    z = Sizes(chan, height, columns, groups, dw_kernel.shape[0])
    pixels = float(samples * lax.axis_size("dp") * height * columns)
    part = (z.units + 2) // 3 * LANES
    lengths = [part, part, z.units * LANES - 2 * part]
    starts = [0, part, 2 * part]

    def own(values, axis=0):
        return lax.dynamic_slice_in_dim(values, first, chan, axis)

    x = jnp.transpose(x_in[0], (2, 0, 1))
    cot = jnp.transpose(cotangent[0], (2, 0, 1))
    land2 = land[0]

    (grad_packed,), part_b_out = pack_out_grad(z, [sum(lengths)], cot, land2)
    grad_band = exchange(grad_packed)

    taps = own(dw_kernel, 1).astype(F32).T
    conv, total, square = conv_forward(z, taps, after(x, grad_packed))
    total, square = lax.psum((total, square), "dp")
    mean = total / pixels
    var = square / pixels - mean * mean
    scale = lax.rsqrt(var + 1e-05)
    own_gain = own(gain)
    chooser = (grid_res[:, None] == jnp.arange(2, dtype=jnp.int32)[None, :]).astype(F32)
    sample_bias = jnp.sum(chooser[0][:, None] * own(res_bias, 1), axis=0)
    affine = jnp.stack([mean, own_gain * scale, own(shift) + sample_bias], axis=1)
    packed = pack_normed(z, lengths, conv, affine)

    def pad_rows(matrix):
        blocks = matrix.reshape(groups, chan, matrix.shape[1])
        return jnp.pad(blocks, ((0, 0), (0, z.pad - chan), (0, 0))).reshape(
            z.packed_rows, matrix.shape[1]
        )

    w_in_p = pad_rows(after(w_in, packed[0]))
    w_in_t = w_in_p.T
    w_out_t = pad_rows(after(w_out, packed[0]).T)
    w_out_p = w_out_t.T
    weights = (w_in_t, w_in_p, w_out_p, w_out_t, b_in[:, None], pad_rows(b_out[:, None]))

    normed = [exchange(after(packed[0], grad_band))]
    normed.append(exchange(after(packed[1], normed[0], w_in_t, w_out_p)))
    branch, norm1, active1, hidden1 = mlp(0, part, normed[0], grad_band, *weights, None)
    normed.append(exchange(after(packed[2], normed[1], norm1)))
    branch, norm2, active2, hidden2 = mlp(1, part, normed[1], grad_band, *weights, branch)
    norm_parts = [exchange(after(norm1, normed[2], norm2))]
    branch, norm3, active3, hidden3 = mlp(2, part, normed[2], grad_band, *weights, branch)
    norm_parts.append(exchange(after(norm2, norm_parts[0], norm3)))
    out_mine, out_sent = weight_grad(
        odd,
        [(grad_band, start) for start in starts],
        [active1, active2, after(active3, norm_parts[0])],
    )
    out_other = swap_cores(out_sent)
    norm_parts.append(exchange(after(norm3, norm_parts[1], out_sent)))
    in_mine, in_sent = weight_grad(
        odd,
        [(value, 0) for value in normed],
        [hidden1, hidden2, after(hidden3, norm_parts[1])],
    )
    in_other = swap_cores(in_sent)
    branch = exchange(after(branch, norm_parts[2], in_sent))
    out_share = quarter_sum(out_mine, out_other)
    in_share = quarter_sum(in_mine, in_other)

    part_shift, part_gain = norm_sums(
        z, norm_parts, conv, jnp.stack([mean, scale], axis=1)
    )
    small = jnp.concatenate(
        [part_shift[None], part_gain[None], chooser[0][:, None] * part_shift[None], part_b_out[None]],
        axis=0,
    )
    small = lax.psum(small, "dp")
    out_share, in_share = lax.psum((out_share, in_share), "pair")
    terms = jnp.stack(
        [mean, scale, own_gain * scale, small[0] / pixels, small[1] / pixels], axis=1
    )
    x_grad, g_kernel = conv_backward(
        z, taps, terms, norm_parts, conv, after(x, out_share, in_share), cot, land2
    )
    g_w_out_t = after(lax.all_gather(out_share, "dp", tiled=True), x_grad)
    g_w_in = after(lax.all_gather(in_share, "dp", tiled=True), x_grad)
    g_w_out_2, g_w_in_2 = swap_cores(g_w_out_t), swap_cores(g_w_in)
    mixed = mix_branch(z, [branch], x, land2)
    g_b_in = jnp.where(odd == 0, g_w_in[chan], g_w_in_2[chan]).astype(F32)

    rows = jnp.concatenate([lax.psum(g_kernel, "dp"), small], axis=0)
    gathered = lax.all_gather(rows, CHAN)
    placed = jnp.transpose(gathered, (1, 0, 2)).reshape(rows.shape[0], width)
    count = dw_kernel.shape[0]

    return (
        jnp.transpose(mixed, (1, 2, 0))[None],
        jnp.transpose(x_grad, (1, 2, 0))[None],
        placed[:count],
        placed[count + 1],
        placed[count],
        placed[count + 2 : count + 4],
        unpad_rows(z, odd, g_w_in, g_w_in_2),
        g_b_in,
        unpad_rows(z, odd, g_w_out_t, g_w_out_2).T,
        placed[count + 4],
    )


def solution(mesh):
    shape = mesh.shape
    mesh = jax.sharding.Mesh(
        mesh.devices.reshape(shape["dp"], shape["chan"] // CORES, CORES), ("dp",) + CHAN
    )
    cells = P("dp", None, None, CHAN)
    return jax.shard_map(
        per_device,
        mesh=mesh,
        in_specs=(cells, cells, P("dp", None, None), P("dp")) + (P(),) * 8,
        out_specs=(cells, cells) + (P(),) * 8,
        check_vma=False,
    )
```

```python
from functools import partial
import math

import jax
import jax.numpy as jnp
from jax import lax
from jax.experimental import pallas as pl
from jax.experimental.pallas import tpu as pltpu
from jax.sharding import PartitionSpec as P

LANES = 128
SUBL = 8
VMEM_LIMIT = 56 * 1024 * 1024
CHAN = ("pair", "core")
CORES = 2
F32 = jnp.float32
BF16 = jnp.bfloat16


def round_up(value, step):
    return (value + step - 1) // step * step


def block_of(total, most):
    return max(size for size in range(1, most + 1) if total % size == 0)


class Sizes:
    def __init__(self, chan, height, width, bands, taps):
        self.chan, self.height, self.width, self.bands = chan, height, width, bands
        self.side = math.isqrt(taps)
        self.margin = self.side // 2
        self.rows = height // bands
        self.wide = round_up(width + 2 * self.margin, LANES)
        self.tiles = self.wide // LANES
        self.tail = width - (self.tiles - 1) * LANES
        self.pad = round_up(chan + 1, SUBL)
        self.packed_rows = bands * self.pad
        self.tail_units = round_up(self.rows * self.tail, LANES) // LANES
        self.units = self.rows * (self.tiles - 1) + self.tail_units


def params(semantics=("arbitrary",)):
    return pltpu.CompilerParams(dimension_semantics=semantics, vmem_limit_bytes=VMEM_LIMIT)


def roll_tiles(z, tiles, shift):
    jump, low = divmod(shift % z.wide, LANES)
    count = z.tiles
    if low == 0:
        return [tiles[(j - jump) % count] for j in range(count)]
    lane = lax.broadcasted_iota(jnp.int32, tiles[0].shape, 1)
    moved = [pltpu.roll(tile, low, 1) for tile in tiles]
    return [
        jnp.where(lane < low, moved[(j - jump - 1) % count], moved[(j - jump) % count])
        for j in range(count)
    ]


def wrap_tiles(z, tiles):
    last = tiles[-1]
    lane = lax.broadcasted_iota(jnp.int32, last.shape, 1)
    ahead = pltpu.roll(tiles[0], z.tail, 1)
    behind = pltpu.roll(last, LANES - z.tail, 1)
    last = jnp.where(lane < z.tail, last, jnp.where(lane < z.tail + z.margin, ahead, behind))
    return tiles[:-1] + [last]


def row_tiles(z, value):
    tiles = [value[:, LANES * j : LANES * (j + 1)] for j in range(z.tiles - 1)]
    tail = value[:, LANES * (z.tiles - 1) :]
    zeros = jnp.zeros((value.shape[0], LANES - z.tail), F32)
    return tiles + [jnp.concatenate([tail, zeros], axis=1)]


def pack_tails(z, tails):
    lane = lax.broadcasted_iota(jnp.int32, tails[0].shape, 1)
    tiles = []
    for t in range(z.tail_units):
        begin, tile = LANES * t, None
        for row, tail in enumerate(tails):
            low = z.tail * row - begin
            if low >= LANES or low + z.tail <= 0:
                continue
            moved = pltpu.roll(tail, low % LANES, 1) if low % LANES else tail
            tile = moved if tile is None else jnp.where(lane >= low, moved, tile)
        end = z.tail * z.rows - begin
        tiles.append(jnp.where(lane < end, tile, 0.0) if end < LANES else tile)
    return tiles


def unpack_tails(z, tiles):
    lane = lax.broadcasted_iota(jnp.int32, tiles[0].shape, 1)
    tails = []
    for row in range(z.rows):
        t, low = divmod(z.tail * row, LANES)
        tail = pltpu.roll(tiles[t], LANES - low, 1) if low else tiles[t]
        if LANES - low < z.tail:
            tail = jnp.where(lane < LANES - low, tail, pltpu.roll(tiles[t + 1], LANES - low, 1))
        tails.append(jnp.where(lane < z.tail, tail, 0.0))
    return tails


def pack_rows(z, rows):
    full = z.tiles - 1
    return [row[j] for row in rows for j in range(full)] + pack_tails(z, [row[full] for row in rows])


def unpack_rows(z, tiles):
    full = z.tiles - 1
    tails = unpack_tails(z, tiles[z.rows * full :])
    return [tiles[row * full : (row + 1) * full] + [tails[row]] for row in range(z.rows)]


def packed_tiles(refs, read):
    return [
        read(ref, slice(LANES * k, LANES * (k + 1)))
        for ref in refs
        for k in range(ref.shape[-1] // LANES)
    ]


def whole(shape):
    return pl.BlockSpec(shape, lambda *_: (0,) * len(shape))


def smem():
    return pl.BlockSpec(memory_space=pltpu.SMEM)


def cost(bytes_accessed, flops=10**7):
    return pl.CostEstimate(flops=flops, bytes_accessed=bytes_accessed, transcendentals=0)


PAIR = 2
GROUP = 16


def pair_rows(z):
    return pl.BlockSpec((PAIR * z.rows, z.pad, z.width), lambda g: (g, 0, 0))


def pair_wide(z):
    return pl.BlockSpec((PAIR * z.rows, z.pad, z.wide), lambda g: (g, 0, 0))


def pair_land(z):
    return pl.BlockSpec((PAIR * z.rows, 1, z.width), lambda g: (g, 0, 0))


def pair_packed(z, cells):
    return pl.BlockSpec((PAIR * z.pad, cells), lambda g: (g, 0))


def group_rows(z):
    return pl.BlockSpec((z.height, GROUP, z.width), lambda c: (0, c, 0))


def group_wide(z):
    return pl.BlockSpec((z.height, GROUP, z.wide), lambda c: (0, c, 0))


def group_lanes(count):
    return pl.BlockSpec((count, GROUP, LANES), lambda c: (0, c, 0))


def write_pair(z, refs, bands):
    tiles = [jnp.concatenate(both, axis=0).astype(BF16) for both in zip(*bands)]
    unit = 0
    for ref in refs:
        for k in range(ref.shape[1] // LANES):
            ref[:, LANES * k : LANES * (k + 1)] = tiles[unit]
            unit += 1


def pack_out_grad(z, cells, cot, land):
    def kernel(cot_ref, land_ref, out_ref, sum_ref):
        @pl.when(pl.program_id(0) == 0)
        def _():
            sum_ref[...] = jnp.zeros_like(sum_ref)

        channel = lax.broadcasted_iota(jnp.int32, (z.pad, z.width), 0)
        total = jnp.zeros((z.pad, LANES), F32)
        bands = []
        for band in range(PAIR):
            rows = []
            for row in range(z.rows * band, z.rows * (band + 1)):
                value = cot_ref[row].astype(F32) * land_ref[row].astype(F32)
                rows.append(row_tiles(z, jnp.where(channel < z.chan, value, 0.0)))
                total = total + sum(rows[-1])
            bands.append(pack_rows(z, rows))
        sum_ref[...] += total
        write_pair(z, [out_ref], bands)

    out, sums = pl.pallas_call(
        kernel,
        grid=(z.bands // PAIR,),
        in_specs=[pair_rows(z), pair_land(z)],
        out_specs=[pair_packed(z, cells), whole((z.pad, LANES))],
        out_shape=[
            jax.ShapeDtypeStruct((z.packed_rows, cells), BF16),
            jax.ShapeDtypeStruct((z.pad, LANES), F32),
        ],
        compiler_params=params(),
        cost_estimate=cost(8 * 10**6),
    )(cot, land)
    return out, jnp.sum(sums, axis=1)[: z.chan]


def fill_rows(z, target, read, wrap):
    zeros = jnp.zeros(target.shape[1:], F32)
    for k in range(z.margin):
        target[k] = zeros
        target[z.margin + z.height + k] = zeros

    def body(h, carry):
        tiles = row_tiles(z, read(h))
        if wrap:
            tiles = wrap_tiles(z, tiles)
        for j, tile in enumerate(tiles):
            target[z.margin + h, :, LANES * j : LANES * (j + 1)] = tile
        return carry

    lax.fori_loop(0, z.height, body, 0, unroll=4)


def convolve(z, steps, at, taps_ref, source, flip, put, carry):
    span = steps + 2 * z.margin

    def body(block, carry):
        h0 = block * steps
        rows = [
            [source[h0 + m, at, LANES * j : LANES * (j + 1)] for j in range(z.tiles)]
            for m in range(span)
        ]
        sums = [None] * steps
        for b in range(z.side):
            weights = [taps_ref[z.side * a + b, at, :] for a in range(z.side)]
            for r in range(steps):
                part = None
                for a in range(z.side):
                    row = rows[r + 2 * z.margin - a] if flip else rows[r + a]
                    terms = [weights[a] * tile for tile in row]
                    part = terms if part is None else [p + t for p, t in zip(part, terms)]
                part = roll_tiles(z, part, b - z.margin if flip else z.margin - b)
                sums[r] = part if b == 0 else [s + p for s, p in zip(sums[r], part)]
        for r in range(steps):
            carry = put(h0 + r, sums[r], carry)
        return carry

    return lax.fori_loop(0, z.height // steps, body, carry)


def conv_forward(z, taps, x):
    def kernel(taps_ref, x_ref, conv_ref, sum_ref, square_ref, source):
        fill_rows(z, source, lambda h: x_ref[h].astype(F32), True)
        lane = lax.broadcasted_iota(jnp.int32, (SUBL, LANES), 1)
        for part in range(GROUP // SUBL):
            at = slice(SUBL * part, SUBL * (part + 1))

            def put(h, tiles, carry):
                for j, tile in enumerate(tiles):
                    conv_ref[h, at, LANES * j : LANES * (j + 1)] = tile
                tiles = tiles[:-1] + [jnp.where(lane < z.tail, tiles[-1], 0.0)]
                return carry[0] + sum(tiles), carry[1] + sum(t * t for t in tiles)

            @pl.when(pl.program_id(0) * GROUP + SUBL * part < z.chan)
            def _():
                zero = jnp.zeros((SUBL, LANES), F32)
                total, square = convolve(z, 4, at, taps_ref, source, False, put, (zero, zero))
                sum_ref[at, :] = total
                square_ref[at, :] = square

    lane_spec = pl.BlockSpec((GROUP, LANES), lambda c: (c, 0))
    lane_shape = jax.ShapeDtypeStruct((z.pad, LANES), F32)
    conv, total, square = pl.pallas_call(
        kernel,
        grid=(pl.cdiv(z.chan, GROUP),),
        in_specs=[group_lanes(taps.shape[0]), group_rows(z)],
        out_specs=[group_wide(z), lane_spec, lane_spec],
        out_shape=[
            jax.ShapeDtypeStruct((z.height, z.pad, z.wide), F32), lane_shape, lane_shape,
        ],
        scratch_shapes=[pltpu.VMEM((z.height + 2 * z.margin, GROUP, z.wide), F32)],
        compiler_params=params(),
        cost_estimate=cost(16 * 10**6, 10**10),
    )(taps, x)
    return conv, jnp.sum(total, axis=1)[: z.chan], jnp.sum(square, axis=1)[: z.chan]


def pack_normed(z, lengths, conv, columns):
    def kernel(columns_ref, conv_ref, *outs):
        channel = lax.broadcasted_iota(jnp.int32, (z.pad, LANES), 0)
        filler = jnp.where(channel == z.chan, 1.0, 0.0)
        mean, factor, offset = columns_ref[0], columns_ref[1], columns_ref[2]
        bands = []
        for band in range(PAIR):
            rows = []
            for row in range(z.rows * band, z.rows * (band + 1)):
                tiles = [conv_ref[row, :, LANES * j : LANES * (j + 1)] for j in range(z.tiles)]
                rows.append(
                    [
                        jnp.where(channel < z.chan, (tile - mean) * factor + offset, filler)
                        for tile in tiles
                    ]
                )
            bands.append(pack_rows(z, rows))
        write_pair(z, outs, bands)

    return pl.pallas_call(
        kernel,
        grid=(z.bands // PAIR,),
        in_specs=[whole(columns.shape), pair_wide(z)],
        out_specs=[pair_packed(z, n) for n in lengths],
        out_shape=[jax.ShapeDtypeStruct((z.packed_rows, n), BF16) for n in lengths],
        compiler_params=params(),
        cost_estimate=cost(12 * 10**6),
    )(columns, conv)


def norm_sums(z, parts, conv, columns):
    count = len(parts)

    def kernel(columns_ref, conv_ref, *rest):
        ins, (shift_ref, gain_ref) = rest[:count], rest[count:]

        @pl.when(pl.program_id(0) == 0)
        def _():
            shift_ref[...] = jnp.zeros_like(shift_ref)
            gain_ref[...] = jnp.zeros_like(gain_ref)

        mean = columns_ref[0]
        tiles = packed_tiles(ins, lambda ref, lanes: ref[:, lanes].astype(F32))
        shift = jnp.zeros((z.pad, LANES), F32)
        gain = jnp.zeros((z.pad, LANES), F32)
        for band in range(PAIR):
            rows = unpack_rows(z, [tile[z.pad * band : z.pad * (band + 1)] for tile in tiles])
            for row, grads in enumerate(rows):
                for j, grad in enumerate(grads):
                    value = conv_ref[z.rows * band + row, :, LANES * j : LANES * (j + 1)]
                    shift = shift + grad
                    gain = gain + grad * (value - mean)
        shift_ref[...] += shift
        gain_ref[...] += gain * columns_ref[1]

    lane_shape = jax.ShapeDtypeStruct((z.pad, LANES), F32)
    shift, gain = pl.pallas_call(
        kernel,
        grid=(z.bands // PAIR,),
        in_specs=[whole(columns.shape), pair_wide(z)] + [pair_packed(z, p.shape[1]) for p in parts],
        out_specs=[whole((z.pad, LANES))] * 2,
        out_shape=[lane_shape, lane_shape],
        compiler_params=params(),
        cost_estimate=cost(12 * 10**6),
    )(columns, conv, *parts)
    return jnp.sum(shift, axis=1)[: z.chan], jnp.sum(gain, axis=1)[: z.chan]


def conv_gradient(z, columns, parts, conv, x, ntaps):
    count = len(parts)
    parts = [part.reshape(z.bands, z.pad, part.shape[1]) for part in parts]
    steps = 4

    def kernel(columns_ref, conv_ref, x_ref, *rest):
        ins, (grad_ref, product_ref, grads, source) = rest[:count], rest[count:]
        mean, scale, factor, shift, gain = (columns_ref[k] for k in range(5))

        def band_body(band, carry):
            tiles = packed_tiles(ins, lambda ref, lanes: ref[band, :, lanes].astype(F32))
            for row, values in enumerate(unpack_rows(z, tiles)):
                h = band * z.rows + row
                made = []
                for j, value in enumerate(values):
                    centred = (conv_ref[h, :, LANES * j : LANES * (j + 1)] - mean) * scale
                    made.append(factor * (value - (shift + centred * gain)))
                for j, tile in enumerate(wrap_tiles(z, made)):
                    at = slice(LANES * j, LANES * (j + 1))
                    grads[h, :, at] = tile
                    grad_ref[h, :, at] = tile.astype(BF16)
            return carry

        lax.fori_loop(0, z.bands, band_body, 0)
        fill_rows(z, source, lambda h: x_ref[h].astype(F32), False)
        for part in range(GROUP // SUBL):
            at = slice(SUBL * part, SUBL * (part + 1))

            @pl.when(pl.program_id(0) * GROUP + SUBL * part < z.chan)
            def _():
                for b in range(z.side):

                    def body(block, totals):
                        h0 = block * steps
                        rows = [
                            [source[h0 + m, at, LANES * j : LANES * (j + 1)] for j in range(z.tiles)]
                            for m in range(steps + 2 * z.margin)
                        ]
                        totals = list(totals)
                        for r in range(steps):
                            moved = roll_tiles(
                                z,
                                [grads[h0 + r, at, LANES * j : LANES * (j + 1)] for j in range(z.tiles)],
                                b - z.margin,
                            )
                            for a in range(z.side):
                                for m, tile in zip(moved, rows[r + a]):
                                    totals[a] = totals[a] + m * tile
                        return tuple(totals)

                    zero = jnp.zeros((SUBL, LANES), F32)
                    totals = lax.fori_loop(0, z.height // steps, body, (zero,) * z.side)
                    for a in range(z.side):
                        product_ref[z.side * a + b, at, :] = totals[a]

    grad, products = pl.pallas_call(
        kernel,
        grid=(pl.cdiv(z.chan, GROUP),),
        in_specs=[group_lanes(5), group_wide(z), group_rows(z)]
        + [pl.BlockSpec((z.bands, GROUP, p.shape[2]), lambda c: (0, c, 0)) for p in parts],
        out_specs=[group_wide(z), group_lanes(ntaps)],
        out_shape=[
            jax.ShapeDtypeStruct((z.height, z.pad, z.wide), BF16),
            jax.ShapeDtypeStruct((ntaps, z.pad, LANES), F32),
        ],
        scratch_shapes=[
            pltpu.VMEM((z.height, GROUP, z.wide), F32),
            pltpu.VMEM((z.height + 2 * z.margin, GROUP, z.wide), F32),
        ],
        compiler_params=params(),
        cost_estimate=cost(20 * 10**6, 10**10),
    )(columns, conv, x, *parts)
    return grad, jnp.sum(products, axis=2)[:, : z.chan]


def conv_backward(z, taps, grad, cot, land):
    def kernel(taps_ref, grad_ref, cot_ref, land_ref, out_ref, source, result):
        zeros = jnp.zeros(source.shape[1:], F32)
        for k in range(z.margin):
            source[k] = zeros
            source[z.margin + z.height + k] = zeros

        def fill(h, carry):
            source[z.margin + h] = grad_ref[h].astype(F32)
            return carry

        lax.fori_loop(0, z.height, fill, 0, unroll=4)
        for part in range(GROUP // SUBL):
            at = slice(SUBL * part, SUBL * (part + 1))

            def put(h, tiles, carry):
                for j, tile in enumerate(tiles):
                    result[h, at, LANES * j : LANES * (j + 1)] = tile
                return carry

            @pl.when(pl.program_id(0) * GROUP + SUBL * part < z.chan)
            def _():
                convolve(z, 4, at, taps_ref, source, True, put, 0)

        def finish(h, carry):
            direct = cot_ref[h].astype(F32) * land_ref[h].astype(F32)
            out_ref[h] = (direct + result[h][:, : z.width]).astype(BF16)
            return carry

        lax.fori_loop(0, z.height, finish, 0, unroll=4)

    return pl.pallas_call(
        kernel,
        grid=(pl.cdiv(z.chan, GROUP),),
        in_specs=[
            group_lanes(taps.shape[0]), group_wide(z), group_rows(z),
            whole((z.height, 1, z.width)),
        ],
        out_specs=group_rows(z),
        out_shape=jax.ShapeDtypeStruct((z.height, z.chan, z.width), BF16),
        scratch_shapes=[
            pltpu.VMEM((z.height + 2 * z.margin, GROUP, z.wide), F32),
            pltpu.VMEM((z.height, GROUP, z.wide), F32),
        ],
        compiler_params=params(),
        cost_estimate=cost(16 * 10**6, 10**10),
    )(taps, grad, cot, land)


def mix_branch(z, branch, x, land):
    def kernel(x_ref, land_ref, branch_ref, out_ref):
        tiles = packed_tiles([branch_ref], lambda ref, lanes: ref[:, lanes].astype(F32))
        for band in range(PAIR):
            rows = unpack_rows(z, [tile[z.pad * band : z.pad * (band + 1)] for tile in tiles])
            for k, row in enumerate(rows):
                h = z.rows * band + k
                value = jnp.concatenate(row, axis=1)[:, : z.width]
                value = land_ref[h].astype(F32) * (x_ref[h].astype(F32) + value)
                out_ref[h] = value.astype(BF16)

    return pl.pallas_call(
        kernel,
        grid=(z.bands // PAIR,),
        in_specs=[pair_rows(z), pair_land(z), pair_packed(z, branch.shape[1])],
        out_specs=pair_rows(z),
        out_shape=jax.ShapeDtypeStruct((z.height, z.chan, z.width), BF16),
        compiler_params=params(),
        cost_estimate=cost(12 * 10**6),
    )(x, land, branch)


def gelu_parts(h):
    span = 1.0 + (0.3275911 * math.sqrt(0.5)) * jnp.abs(h)
    t = pl.reciprocal(span, approx=True)
    t = t * (2.0 - span * t)
    bell = jnp.exp2((-0.5 / math.log(2.0)) * (h * h))
    poly = t * (
        0.5 * 0.254829592
        + t
        * (
            0.5 * -0.284496736
            + t * (0.5 * 1.421413741 + t * (0.5 * -1.453152027 + t * (0.5 * 1.061405429)))
        )
    )
    tail = poly * bell
    phi = jnp.where(h >= 0, 1.0 - tail, tail)
    return h * phi, phi + h * ((1.0 / math.sqrt(2.0 * math.pi)) * bell)


def lane_block(rows, cells, part):
    return pl.BlockSpec((rows, cells), lambda *_: (0, part))


def row_step(rows, most):
    return max(n for n in range(16, most + 1, 16) if rows % n == 0)


def mlp(part, length, normed, out_grad, w_in_t, w_in, w_out, w_out_t, b_in, b_out, branch_all):
    packed, cells = normed.shape
    hidden = w_in_t.shape[0]
    block = block_of(hidden, 640)
    inner = row_step(block, 160)
    blocks = hidden // block
    pairs = block // inner // 2
    rows = row_step(packed, 208)
    outs = packed // rows

    def kernel(
        n_ref, g_ref, w_in_t_ref, w_in_ref, w_out_ref, w_out_t_ref, b_in_ref, b_out_ref, *rest
    ):
        (
            branch_ref, norm_ref, active_out, hidden_out,
            h_0, h_1, back_0, back_1, active, grads, sems,
        ) = rest[-11:]
        step = pl.program_id(0)

        def products(k, h, back):
            at = pl.ds(k * inner, inner)
            h[...] = (
                jnp.dot(w_in_t_ref[at, :], n_ref[...], preferred_element_type=F32) + b_in_ref[at, :]
            )
            back[...] = jnp.dot(w_out_ref[at, :], g_ref[:, :cells], preferred_element_type=F32)

        def gelu(k, h, back):
            at = pl.ds(pl.multiple_of(jnp.maximum(k, 0) * inner, inner), inner)
            value, slope = gelu_parts(h[...])
            active[at, :] = value.astype(BF16)
            grads[at, :] = (back[...] * slope).astype(BF16)

        @pl.when(step < blocks)
        def _():
            first = step * (2 * pairs)

            def body(i, carry):
                products(2 * i, h_0, back_0)
                gelu(first + 2 * i - 1, h_1, back_1)
                products(2 * i + 1, h_1, back_1)
                gelu(first + 2 * i, h_0, back_0)
                return carry

            lax.fori_loop(0, pairs, body, 0)

        copies = [
            pltpu.make_async_copy(active, active_out, sems.at[0]),
            pltpu.make_async_copy(grads, hidden_out, sems.at[1]),
        ]

        @pl.when(step == blocks)
        def _():
            gelu(2 * pairs * blocks - 1, h_1, back_1)
            for copy in copies:
                copy.start()

        @pl.when(step >= blocks)
        def _():
            branch = jnp.dot(w_out_t_ref[...], active[...], preferred_element_type=F32)
            branch_ref[:, :cells] = (branch + b_out_ref[...]).astype(BF16)
            norm = jnp.dot(w_in_ref[...], grads[...], preferred_element_type=F32)
            norm_ref[...] = norm.astype(BF16)

        @pl.when(step == blocks + outs - 1)
        def _():
            for copy in copies:
                copy.wait()

    def at_in(f):
        return jnp.minimum(f, blocks - 1)

    def at_out(f):
        return jnp.maximum(f - blocks, 0)

    tall_block = pl.BlockSpec((block, packed), lambda f: (at_in(f), 0))
    wide_block = pl.BlockSpec((rows, hidden), lambda f: (at_out(f), 0))
    anywhere = pl.BlockSpec(memory_space=pl.ANY)
    operands = [normed, out_grad, w_in_t, w_in, w_out, w_out_t, b_in, b_out]
    in_specs = [
        whole((packed, cells)), lane_block(packed, length, part),
        tall_block, wide_block, tall_block, wide_block,
        pl.BlockSpec((block, 1), lambda f: (at_in(f), 0)),
        pl.BlockSpec((rows, 1), lambda f: (at_out(f), 0)),
    ]
    aliases = {}
    if branch_all is not None:
        aliases = {len(operands): 0}
        operands.append(branch_all)
        in_specs.append(anywhere)
    buffer = pltpu.VMEM((inner, cells), F32)
    return pl.pallas_call(
        kernel,
        grid=(blocks + outs,),
        in_specs=in_specs,
        out_specs=[
            pl.BlockSpec((rows, length), lambda f: (at_out(f), part)),
            pl.BlockSpec((rows, cells), lambda f: (at_out(f), 0)),
            anywhere, anywhere,
        ],
        out_shape=[
            jax.ShapeDtypeStruct(out_grad.shape, BF16),
            jax.ShapeDtypeStruct((packed, cells), BF16),
            jax.ShapeDtypeStruct((hidden, cells), BF16),
            jax.ShapeDtypeStruct((hidden, cells), BF16),
        ],
        scratch_shapes=[buffer] * 4
        + [pltpu.VMEM((hidden, cells), BF16)] * 2
        + [pltpu.SemaphoreType.DMA((2,))],
        input_output_aliases=aliases,
        compiler_params=params(),
        cost_estimate=pl.CostEstimate(
            flops=8 * packed * cells * hidden, bytes_accessed=4 * 10**7, transcendentals=cells * hidden
        ),
    )(*operands)


def weight_grad(lefts, rights):
    rows, hidden = lefts[0][0].shape[0], rights[0].shape[0]
    block = block_of(hidden, 640)
    inner = row_step(rows, 208)
    arrays = []
    for array, _ in lefts:
        if not any(array is known for known in arrays):
            arrays.append(array)
    which = [next(k for k, known in enumerate(arrays) if known is array) for array, _ in lefts]

    def kernel(*refs):
        def body(m, carry):
            at = pl.ds(pl.multiple_of(m * inner, inner), inner)
            total = None
            for k, (_, start), right in zip(which, lefts, refs[len(arrays) : -1]):
                part = lax.dot_general(
                    refs[k][at, start : start + right.shape[1]], right[...],
                    (((1,), (1,)), ((), ())), preferred_element_type=F32,
                )
                total = part if total is None else total + part
            refs[-1][at, :] = total.astype(BF16)
            return carry

        lax.fori_loop(0, rows // inner, body, 0)

    cells = sum(right.shape[1] for right in rights)
    return pl.pallas_call(
        kernel,
        grid=(hidden // block,),
        in_specs=[whole(array.shape) for array in arrays]
        + [pl.BlockSpec((block, right.shape[1]), lambda f: (f, 0)) for right in rights],
        out_specs=pl.BlockSpec((rows, block), lambda f: (0, f)),
        out_shape=jax.ShapeDtypeStruct((rows, hidden), BF16),
        compiler_params=params(),
        cost_estimate=cost(24 * 10**6, 2 * rows * cells * hidden),
    )(*arrays, *rights)


def unpad_rows(z, matrix):
    groups, hidden = matrix.shape[0] // z.pad, matrix.shape[1]
    several = next(k for k in range(2, groups + 1, 2) if groups % k == 0 and k * z.chan % SUBL == 0)

    def kernel(in_ref, out_ref):
        value = in_ref[...].astype(F32)
        for k in range(several):
            out_ref[z.chan * k : z.chan * (k + 1), :] = value[z.pad * k : z.pad * k + z.chan, :]

    return pl.pallas_call(
        kernel,
        grid=(groups // several,),
        in_specs=[pl.BlockSpec((several * z.pad, hidden), lambda g: (g, 0))],
        out_specs=pl.BlockSpec((several * z.chan, hidden), lambda g: (g, 0)),
        out_shape=jax.ShapeDtypeStruct((groups * z.chan, hidden), F32),
        compiler_params=params(),
        cost_estimate=cost(16 * 10**6),
    )(matrix)


def exchange(value):
    return lax.all_to_all(value, CHAN, split_axis=0, concat_axis=0, tiled=True)


def after(value, *others):
    return lax.optimization_barrier((value, *others))[0]


def dp_sum(value):
    ways = lax.axis_size("dp")
    total = value
    for turn in range(1, ways):
        total = total + lax.ppermute(value, "dp", [(i, i ^ turn) for i in range(ways)])
    return total


def per_device(
    x_in, cotangent, land, grid_res, dw_kernel, gain, shift, res_bias, w_in, b_in, w_out, b_out
):
    samples, height, columns, chan = x_in.shape
    groups = lax.axis_size("pair") * CORES
    first = (lax.axis_index("pair") * CORES + lax.axis_index("core")) * chan
    width = chan * groups
    ntaps = dw_kernel.shape[0]
    z = Sizes(chan, height, columns, groups, ntaps)
    pixels = float(samples * lax.axis_size("dp") * height * columns)
    part = (z.units + 1) // 2 * LANES
    lengths = [part, z.units * LANES - part]
    starts = [0, part]

    def own(values, axis=0):
        return lax.dynamic_slice_in_dim(values, first, chan, axis)

    def over_lanes(rows):
        rows = jnp.pad(rows, ((0, 0), (0, z.pad - chan)))
        return jnp.broadcast_to(rows[:, :, None], rows.shape + (LANES,))

    x = jnp.transpose(x_in[0], (0, 2, 1))
    cot = jnp.transpose(cotangent[0], (0, 2, 1))
    land3 = land[0][:, None, :]

    grad_packed, part_b_out = pack_out_grad(z, sum(lengths), cot, land3)
    grad_band = exchange(grad_packed)

    taps = over_lanes(own(dw_kernel, 1).astype(F32))
    conv, total, square = conv_forward(z, taps, after(x, grad_packed))
    total, square = lax.psum((total, square), "dp")
    mean = total / pixels
    var = square / pixels - mean * mean
    scale = lax.rsqrt(var + 1e-05)
    own_gain = own(gain)
    chooser = (grid_res[:, None] == jnp.arange(2, dtype=jnp.int32)[None, :]).astype(F32)
    sample_bias = jnp.sum(chooser[0][:, None] * own(res_bias, 1), axis=0)
    affine = over_lanes(jnp.stack([mean, own_gain * scale, own(shift) + sample_bias]))
    packed = pack_normed(z, lengths, conv, affine)

    def pad_rows(matrix):
        blocks = matrix.reshape(groups, chan, matrix.shape[1])
        return jnp.pad(blocks, ((0, 0), (0, z.pad - chan), (0, 0))).reshape(
            z.packed_rows, matrix.shape[1]
        )

    w_in_p = pad_rows(after(w_in, packed[0]))
    w_in_t = w_in_p.T
    w_out_t = pad_rows(after(w_out, packed[0]).T)
    w_out_p = w_out_t.T
    weights = (w_in_t, w_in_p, w_out_p, w_out_t, b_in[:, None], pad_rows(b_out[:, None]))

    normed = [exchange(after(packed[0], grad_band))]
    normed.append(exchange(after(packed[1], normed[0], w_in_t, w_out_p)))
    branch, norm1, active1, hidden1 = mlp(0, part, normed[0], grad_band, *weights, None)
    norm_parts = [exchange(after(norm1, normed[1]))]
    branch, norm2, active2, hidden2 = mlp(1, part, normed[1], grad_band, *weights, branch)
    norm_parts.append(exchange(after(norm2, norm_parts[0])))
    g_w_out_t = weight_grad(
        [(grad_band, start) for start in starts], [active1, after(active2, norm_parts[0])]
    )
    g_w_in = weight_grad(
        [(value, 0) for value in normed], [hidden1, after(hidden2, g_w_out_t)]
    )
    branch = exchange(after(branch, norm_parts[1], g_w_in))
    everywhere = ("dp",) + CHAN
    g_w_out_t = lax.psum(g_w_out_t, everywhere)
    g_w_in = lax.psum(after(g_w_in, norm_parts[1]), everywhere)

    part_shift, part_gain = norm_sums(z, norm_parts, conv, over_lanes(jnp.stack([mean, scale])))
    small = jnp.concatenate(
        [part_shift[None], part_gain[None], chooser[0][:, None] * part_shift[None], part_b_out[None]],
        axis=0,
    )
    small = lax.psum(small, "dp")
    terms = over_lanes(
        jnp.stack([mean, scale, own_gain * scale, small[0] / pixels, small[1] / pixels])
    )
    conv_grad, g_kernel = conv_gradient(z, terms, norm_parts, conv, x, ntaps)
    g_kernel = dp_sum(g_kernel)
    x_grad = conv_backward(z, taps, conv_grad, cot, land3)
    rows = jnp.concatenate([after(g_kernel, x_grad), small], axis=0)
    gathered = lax.all_gather(rows, CHAN)
    placed = jnp.transpose(gathered, (1, 0, 2)).reshape(rows.shape[0], width)
    mixed = mix_branch(z, branch, after(x, x_grad), land3)
    g_w_out_t, g_w_in = after(g_w_out_t, mixed), after(g_w_in, mixed)

    return (
        jnp.transpose(mixed, (0, 2, 1))[None],
        jnp.transpose(x_grad, (0, 2, 1))[None],
        placed[:ntaps],
        placed[ntaps + 1],
        placed[ntaps],
        placed[ntaps + 2 : ntaps + 4],
        unpad_rows(z, g_w_in),
        g_w_in[chan].astype(F32),
        unpad_rows(z, g_w_out_t).T,
        placed[ntaps + 4],
    )


def solution(mesh):
    shape = mesh.shape
    mesh = jax.sharding.Mesh(
        mesh.devices.reshape(shape["dp"], shape["chan"] // CORES, CORES), ("dp",) + CHAN
    )
    cells = P("dp", None, None, CHAN)
    return jax.shard_map(
        per_device,
        mesh=mesh,
        in_specs=(cells, cells, P("dp", None, None), P("dp")) + (P(),) * 8,
        out_specs=(cells, cells) + (P(),) * 8,
        check_vma=False,
    )
```

```python
from functools import partial
import math

import jax
import jax.numpy as jnp
from jax import lax
from jax.experimental import pallas as pl
from jax.experimental.pallas import tpu as pltpu
from jax.sharding import PartitionSpec as P

LANES = 128
SUBL = 8
VMEM_LIMIT = 56 * 1024 * 1024
CHAN = ("pair", "core")
CORES = 2
F32 = jnp.float32
BF16 = jnp.bfloat16


def round_up(value, step):
    return (value + step - 1) // step * step


def block_of(total, most):
    return max(size for size in range(1, most + 1) if total % size == 0)


class Sizes:
    def __init__(self, chan, height, width, bands, taps):
        self.chan, self.height, self.width, self.bands = chan, height, width, bands
        self.side = math.isqrt(taps)
        self.margin = self.side // 2
        self.rows = height // bands
        self.wide = round_up(width + 2 * self.margin, LANES)
        self.tiles = self.wide // LANES
        self.tail = width - (self.tiles - 1) * LANES
        self.pad = round_up(chan + 1, SUBL)
        self.packed_rows = bands * self.pad
        self.tail_units = round_up(self.rows * self.tail, LANES) // LANES
        self.units = self.rows * (self.tiles - 1) + self.tail_units


def params(semantics=("arbitrary",)):
    return pltpu.CompilerParams(dimension_semantics=semantics, vmem_limit_bytes=VMEM_LIMIT)


def roll_tiles(z, tiles, shift):
    jump, low = divmod(shift % z.wide, LANES)
    count = z.tiles
    if low == 0:
        return [tiles[(j - jump) % count] for j in range(count)]
    lane = lax.broadcasted_iota(jnp.int32, tiles[0].shape, 1)
    moved = [pltpu.roll(tile, low, 1) for tile in tiles]
    return [
        jnp.where(lane < low, moved[(j - jump - 1) % count], moved[(j - jump) % count])
        for j in range(count)
    ]


def wrap_tiles(z, tiles):
    last = tiles[-1]
    lane = lax.broadcasted_iota(jnp.int32, last.shape, 1)
    ahead = pltpu.roll(tiles[0], z.tail, 1)
    behind = pltpu.roll(last, LANES - z.tail, 1)
    last = jnp.where(lane < z.tail, last, jnp.where(lane < z.tail + z.margin, ahead, behind))
    return tiles[:-1] + [last]


def row_tiles(z, value):
    tiles = [value[:, LANES * j : LANES * (j + 1)] for j in range(z.tiles - 1)]
    tail = value[:, LANES * (z.tiles - 1) :]
    zeros = jnp.zeros((value.shape[0], LANES - z.tail), F32)
    return tiles + [jnp.concatenate([tail, zeros], axis=1)]


def pack_tails(z, tails):
    lane = lax.broadcasted_iota(jnp.int32, tails[0].shape, 1)
    tiles = []
    for t in range(z.tail_units):
        begin, tile = LANES * t, None
        for row, tail in enumerate(tails):
            low = z.tail * row - begin
            if low >= LANES or low + z.tail <= 0:
                continue
            moved = pltpu.roll(tail, low % LANES, 1) if low % LANES else tail
            tile = moved if tile is None else jnp.where(lane >= low, moved, tile)
        end = z.tail * z.rows - begin
        tiles.append(jnp.where(lane < end, tile, 0.0) if end < LANES else tile)
    return tiles


def unpack_tails(z, tiles):
    lane = lax.broadcasted_iota(jnp.int32, tiles[0].shape, 1)
    tails = []
    for row in range(z.rows):
        t, low = divmod(z.tail * row, LANES)
        tail = pltpu.roll(tiles[t], LANES - low, 1) if low else tiles[t]
        if LANES - low < z.tail:
            tail = jnp.where(lane < LANES - low, tail, pltpu.roll(tiles[t + 1], LANES - low, 1))
        tails.append(jnp.where(lane < z.tail, tail, 0.0))
    return tails


def pack_rows(z, rows):
    full = z.tiles - 1
    return [row[j] for row in rows for j in range(full)] + pack_tails(z, [row[full] for row in rows])


def unpack_rows(z, tiles):
    full = z.tiles - 1
    tails = unpack_tails(z, tiles[z.rows * full :])
    return [tiles[row * full : (row + 1) * full] + [tails[row]] for row in range(z.rows)]


def packed_tiles(refs, read):
    return [
        read(ref, slice(LANES * k, LANES * (k + 1)))
        for ref in refs
        for k in range(ref.shape[-1] // LANES)
    ]


def whole(shape):
    return pl.BlockSpec(shape, lambda *_: (0,) * len(shape))


def smem():
    return pl.BlockSpec(memory_space=pltpu.SMEM)


def cost(bytes_accessed, flops=10**7):
    return pl.CostEstimate(flops=flops, bytes_accessed=bytes_accessed, transcendentals=0)


PAIR = 2
GROUP = 16


def pair_rows(z):
    return pl.BlockSpec((PAIR * z.rows, z.pad, z.width), lambda g: (g, 0, 0))


def pair_wide(z):
    return pl.BlockSpec((PAIR * z.rows, z.pad, z.wide), lambda g: (g, 0, 0))


def pair_land(z):
    return pl.BlockSpec((PAIR * z.rows, 1, z.width), lambda g: (g, 0, 0))


def pair_packed(z, cells):
    return pl.BlockSpec((PAIR * z.pad, cells), lambda g: (g, 0))


def group_rows(z):
    return pl.BlockSpec((z.height, GROUP, z.width), lambda c: (0, c, 0))


def group_wide(z):
    return pl.BlockSpec((z.height, GROUP, z.wide), lambda c: (0, c, 0))


def group_lanes(count):
    return pl.BlockSpec((count, GROUP, LANES), lambda c: (0, c, 0))


def write_pair(z, refs, bands):
    tiles = [jnp.concatenate(both, axis=0).astype(BF16) for both in zip(*bands)]
    unit = 0
    for ref in refs:
        for k in range(ref.shape[1] // LANES):
            ref[:, LANES * k : LANES * (k + 1)] = tiles[unit]
            unit += 1


def pack_out_grad(z, cells, cot, land):
    def kernel(cot_ref, land_ref, out_ref, sum_ref):
        @pl.when(pl.program_id(0) == 0)
        def _():
            sum_ref[...] = jnp.zeros_like(sum_ref)

        channel = lax.broadcasted_iota(jnp.int32, (z.pad, z.width), 0)
        total = jnp.zeros((z.pad, LANES), F32)
        bands = []
        for band in range(PAIR):
            rows = []
            for row in range(z.rows * band, z.rows * (band + 1)):
                value = cot_ref[row].astype(F32) * land_ref[row].astype(F32)
                rows.append(row_tiles(z, jnp.where(channel < z.chan, value, 0.0)))
                total = total + sum(rows[-1])
            bands.append(pack_rows(z, rows))
        sum_ref[...] += total
        write_pair(z, [out_ref], bands)

    out, sums = pl.pallas_call(
        kernel,
        grid=(z.bands // PAIR,),
        in_specs=[pair_rows(z), pair_land(z)],
        out_specs=[pair_packed(z, cells), whole((z.pad, LANES))],
        out_shape=[
            jax.ShapeDtypeStruct((z.packed_rows, cells), BF16),
            jax.ShapeDtypeStruct((z.pad, LANES), F32),
        ],
        compiler_params=params(),
        cost_estimate=cost(8 * 10**6),
    )(cot, land)
    return out, jnp.sum(sums, axis=1)[: z.chan]


def fill_rows(z, target, read, wrap):
    zeros = jnp.zeros(target.shape[1:], F32)
    for k in range(z.margin):
        target[k] = zeros
        target[z.margin + z.height + k] = zeros

    def body(h, carry):
        tiles = row_tiles(z, read(h))
        if wrap:
            tiles = wrap_tiles(z, tiles)
        for j, tile in enumerate(tiles):
            target[z.margin + h, :, LANES * j : LANES * (j + 1)] = tile
        return carry

    lax.fori_loop(0, z.height, body, 0, unroll=8)


def convolve(z, steps, at, taps_ref, source, flip, put, carry):
    span = steps + 2 * z.margin

    def body(block, carry):
        h0 = block * steps
        rows = [
            [source[h0 + m, at, LANES * j : LANES * (j + 1)] for j in range(z.tiles)]
            for m in range(span)
        ]
        sums = [None] * steps
        for b in range(z.side):
            weights = [taps_ref[z.side * a + b, at, :] for a in range(z.side)]
            for r in range(steps):
                part = None
                for a in range(z.side):
                    row = rows[r + 2 * z.margin - a] if flip else rows[r + a]
                    terms = [weights[a] * tile for tile in row]
                    part = terms if part is None else [p + t for p, t in zip(part, terms)]
                part = roll_tiles(z, part, b - z.margin if flip else z.margin - b)
                sums[r] = part if b == 0 else [s + p for s, p in zip(sums[r], part)]
        for r in range(steps):
            carry = put(h0 + r, sums[r], carry)
        return carry

    return lax.fori_loop(0, z.height // steps, body, carry, unroll=2)


def conv_forward(z, taps, x):
    def kernel(taps_ref, x_ref, conv_ref, sum_ref, square_ref, source):
        fill_rows(z, source, lambda h: x_ref[h].astype(F32), True)
        lane = lax.broadcasted_iota(jnp.int32, (SUBL, LANES), 1)
        for part in range(GROUP // SUBL):
            at = slice(SUBL * part, SUBL * (part + 1))

            def put(h, tiles, carry):
                for j, tile in enumerate(tiles):
                    conv_ref[h, at, LANES * j : LANES * (j + 1)] = tile
                tiles = tiles[:-1] + [jnp.where(lane < z.tail, tiles[-1], 0.0)]
                return carry[0] + sum(tiles), carry[1] + sum(t * t for t in tiles)

            @pl.when(pl.program_id(0) * GROUP + SUBL * part < z.chan)
            def _():
                zero = jnp.zeros((SUBL, LANES), F32)
                total, square = convolve(z, 4, at, taps_ref, source, False, put, (zero, zero))
                sum_ref[at, :] = total
                square_ref[at, :] = square

    lane_spec = pl.BlockSpec((GROUP, LANES), lambda c: (c, 0))
    lane_shape = jax.ShapeDtypeStruct((z.pad, LANES), F32)
    conv, total, square = pl.pallas_call(
        kernel,
        grid=(pl.cdiv(z.chan, GROUP),),
        in_specs=[group_lanes(taps.shape[0]), group_rows(z)],
        out_specs=[group_wide(z), lane_spec, lane_spec],
        out_shape=[
            jax.ShapeDtypeStruct((z.height, z.pad, z.wide), F32), lane_shape, lane_shape,
        ],
        scratch_shapes=[pltpu.VMEM((z.height + 2 * z.margin, GROUP, z.wide), F32)],
        compiler_params=params(),
        cost_estimate=cost(16 * 10**6, 10**10),
    )(taps, x)
    return conv, jnp.sum(total, axis=1)[: z.chan], jnp.sum(square, axis=1)[: z.chan]


def pack_normed(z, lengths, conv, columns):
    def kernel(columns_ref, conv_ref, *outs):
        channel = lax.broadcasted_iota(jnp.int32, (z.pad, LANES), 0)
        filler = jnp.where(channel == z.chan, 1.0, 0.0)
        mean, factor, offset = columns_ref[0], columns_ref[1], columns_ref[2]
        bands = []
        for band in range(PAIR):
            rows = []
            for row in range(z.rows * band, z.rows * (band + 1)):
                tiles = [conv_ref[row, :, LANES * j : LANES * (j + 1)] for j in range(z.tiles)]
                rows.append(
                    [
                        jnp.where(channel < z.chan, (tile - mean) * factor + offset, filler)
                        for tile in tiles
                    ]
                )
            bands.append(pack_rows(z, rows))
        write_pair(z, outs, bands)

    return pl.pallas_call(
        kernel,
        grid=(z.bands // PAIR,),
        in_specs=[whole(columns.shape), pair_wide(z)],
        out_specs=[pair_packed(z, n) for n in lengths],
        out_shape=[jax.ShapeDtypeStruct((z.packed_rows, n), BF16) for n in lengths],
        compiler_params=params(),
        cost_estimate=cost(12 * 10**6),
    )(columns, conv)


def norm_sums(z, parts, conv, columns):
    count = len(parts)

    def kernel(columns_ref, conv_ref, *rest):
        ins, (shift_ref, gain_ref) = rest[:count], rest[count:]

        @pl.when(pl.program_id(0) == 0)
        def _():
            shift_ref[...] = jnp.zeros_like(shift_ref)
            gain_ref[...] = jnp.zeros_like(gain_ref)

        mean = columns_ref[0]
        tiles = packed_tiles(ins, lambda ref, lanes: ref[:, lanes].astype(F32))
        shift = jnp.zeros((z.pad, LANES), F32)
        gain = jnp.zeros((z.pad, LANES), F32)
        for band in range(PAIR):
            rows = unpack_rows(z, [tile[z.pad * band : z.pad * (band + 1)] for tile in tiles])
            for row, grads in enumerate(rows):
                for j, grad in enumerate(grads):
                    value = conv_ref[z.rows * band + row, :, LANES * j : LANES * (j + 1)]
                    shift = shift + grad
                    gain = gain + grad * (value - mean)
        shift_ref[...] += shift
        gain_ref[...] += gain * columns_ref[1]

    lane_shape = jax.ShapeDtypeStruct((z.pad, LANES), F32)
    shift, gain = pl.pallas_call(
        kernel,
        grid=(z.bands // PAIR,),
        in_specs=[whole(columns.shape), pair_wide(z)] + [pair_packed(z, p.shape[1]) for p in parts],
        out_specs=[whole((z.pad, LANES))] * 2,
        out_shape=[lane_shape, lane_shape],
        compiler_params=params(),
        cost_estimate=cost(12 * 10**6),
    )(columns, conv, *parts)
    return jnp.sum(shift, axis=1)[: z.chan], jnp.sum(gain, axis=1)[: z.chan]


def conv_gradient(z, columns, parts, conv, x, ntaps):
    count = len(parts)
    parts = [part.reshape(z.bands, z.pad, part.shape[1]) for part in parts]
    steps = 4

    def kernel(columns_ref, conv_ref, x_ref, *rest):
        ins, (grad_ref, product_ref, grads, source) = rest[:count], rest[count:]
        mean, scale, factor, shift, gain = (columns_ref[k] for k in range(5))

        def band_body(band, carry):
            tiles = packed_tiles(ins, lambda ref, lanes: ref[band, :, lanes].astype(F32))
            for row, values in enumerate(unpack_rows(z, tiles)):
                h = band * z.rows + row
                made = []
                for j, value in enumerate(values):
                    centred = (conv_ref[h, :, LANES * j : LANES * (j + 1)] - mean) * scale
                    made.append(factor * (value - (shift + centred * gain)))
                for j, tile in enumerate(wrap_tiles(z, made)):
                    at = slice(LANES * j, LANES * (j + 1))
                    grads[h, :, at] = tile
                    grad_ref[h, :, at] = tile.astype(BF16)
            return carry

        lax.fori_loop(0, z.bands, band_body, 0)
        fill_rows(z, source, lambda h: x_ref[h].astype(F32), False)
        for part in range(GROUP // SUBL):
            at = slice(SUBL * part, SUBL * (part + 1))

            @pl.when(pl.program_id(0) * GROUP + SUBL * part < z.chan)
            def _():
                for b in range(z.side):

                    def body(block, totals):
                        h0 = block * steps
                        rows = [
                            [source[h0 + m, at, LANES * j : LANES * (j + 1)] for j in range(z.tiles)]
                            for m in range(steps + 2 * z.margin)
                        ]
                        totals = list(totals)
                        for r in range(steps):
                            moved = roll_tiles(
                                z,
                                [grads[h0 + r, at, LANES * j : LANES * (j + 1)] for j in range(z.tiles)],
                                b - z.margin,
                            )
                            for a in range(z.side):
                                for m, tile in zip(moved, rows[r + a]):
                                    totals[a] = totals[a] + m * tile
                        return tuple(totals)

                    zero = jnp.zeros((SUBL, LANES), F32)
                    totals = lax.fori_loop(0, z.height // steps, body, (zero,) * z.side, unroll=4)
                    for a in range(z.side):
                        product_ref[z.side * a + b, at, :] = totals[a]

    grad, products = pl.pallas_call(
        kernel,
        grid=(pl.cdiv(z.chan, GROUP),),
        in_specs=[group_lanes(5), group_wide(z), group_rows(z)]
        + [pl.BlockSpec((z.bands, GROUP, p.shape[2]), lambda c: (0, c, 0)) for p in parts],
        out_specs=[group_wide(z), group_lanes(ntaps)],
        out_shape=[
            jax.ShapeDtypeStruct((z.height, z.pad, z.wide), BF16),
            jax.ShapeDtypeStruct((ntaps, z.pad, LANES), F32),
        ],
        scratch_shapes=[
            pltpu.VMEM((z.height, GROUP, z.wide), F32),
            pltpu.VMEM((z.height + 2 * z.margin, GROUP, z.wide), F32),
        ],
        compiler_params=params(),
        cost_estimate=cost(20 * 10**6, 10**10),
    )(columns, conv, x, *parts)
    return grad, jnp.sum(products, axis=2)[:, : z.chan]


def conv_backward(z, taps, grad, cot, land):
    def kernel(taps_ref, grad_ref, cot_ref, land_ref, out_ref, source, result):
        zeros = jnp.zeros(source.shape[1:], F32)
        for k in range(z.margin):
            source[k] = zeros
            source[z.margin + z.height + k] = zeros

        def fill(h, carry):
            source[z.margin + h] = grad_ref[h].astype(F32)
            return carry

        lax.fori_loop(0, z.height, fill, 0, unroll=8)
        for part in range(GROUP // SUBL):
            at = slice(SUBL * part, SUBL * (part + 1))

            def put(h, tiles, carry):
                for j, tile in enumerate(tiles):
                    result[h, at, LANES * j : LANES * (j + 1)] = tile
                return carry

            @pl.when(pl.program_id(0) * GROUP + SUBL * part < z.chan)
            def _():
                convolve(z, 4, at, taps_ref, source, True, put, 0)

        def finish(h, carry):
            direct = cot_ref[h].astype(F32) * land_ref[h].astype(F32)
            out_ref[h] = (direct + result[h][:, : z.width]).astype(BF16)
            return carry

        lax.fori_loop(0, z.height, finish, 0, unroll=8)

    return pl.pallas_call(
        kernel,
        grid=(pl.cdiv(z.chan, GROUP),),
        in_specs=[
            group_lanes(taps.shape[0]), group_wide(z), group_rows(z),
            whole((z.height, 1, z.width)),
        ],
        out_specs=group_rows(z),
        out_shape=jax.ShapeDtypeStruct((z.height, z.chan, z.width), BF16),
        scratch_shapes=[
            pltpu.VMEM((z.height + 2 * z.margin, GROUP, z.wide), F32),
            pltpu.VMEM((z.height, GROUP, z.wide), F32),
        ],
        compiler_params=params(),
        cost_estimate=cost(16 * 10**6, 10**10),
    )(taps, grad, cot, land)


def mix_branch(z, branch, x, land):
    def kernel(x_ref, land_ref, branch_ref, out_ref):
        tiles = packed_tiles([branch_ref], lambda ref, lanes: ref[:, lanes].astype(F32))
        for band in range(PAIR):
            rows = unpack_rows(z, [tile[z.pad * band : z.pad * (band + 1)] for tile in tiles])
            for k, row in enumerate(rows):
                h = z.rows * band + k
                value = jnp.concatenate(row, axis=1)[:, : z.width]
                value = land_ref[h].astype(F32) * (x_ref[h].astype(F32) + value)
                out_ref[h] = value.astype(BF16)

    return pl.pallas_call(
        kernel,
        grid=(z.bands // PAIR,),
        in_specs=[pair_rows(z), pair_land(z), pair_packed(z, branch.shape[1])],
        out_specs=pair_rows(z),
        out_shape=jax.ShapeDtypeStruct((z.height, z.chan, z.width), BF16),
        compiler_params=params(),
        cost_estimate=cost(12 * 10**6),
    )(x, land, branch)


def gelu_parts(h):
    span = 1.0 + (0.3275911 * math.sqrt(0.5)) * jnp.abs(h)
    t = pl.reciprocal(span, approx=True)
    t = t * (2.0 - span * t)
    bell = jnp.exp2((-0.5 / math.log(2.0)) * (h * h))
    poly = t * (
        0.5 * 0.254829592
        + t
        * (
            0.5 * -0.284496736
            + t * (0.5 * 1.421413741 + t * (0.5 * -1.453152027 + t * (0.5 * 1.061405429)))
        )
    )
    tail = poly * bell
    phi = jnp.where(h >= 0, 1.0 - tail, tail)
    return h * phi, phi + h * ((1.0 / math.sqrt(2.0 * math.pi)) * bell)


def pad_weight(z, matrix):
    groups, hidden = matrix.shape[0] // z.chan, matrix.shape[1]
    block = block_of(hidden, 640)
    rows = groups * z.pad

    def kernel(in_ref, out_ref, transposed_ref, wide):
        value = in_ref[...].astype(F32)
        zeros = jnp.zeros((z.pad - z.chan, block), F32)
        for k in range(groups):
            wide[z.pad * k : z.pad * (k + 1), :] = jnp.concatenate(
                [value[z.chan * k : z.chan * (k + 1), :], zeros], axis=0
            )
        padded = wide[...]
        out_ref[...] = padded.astype(BF16)
        transposed_ref[...] = padded.T.astype(BF16)

    return pl.pallas_call(
        kernel,
        grid=(hidden // block,),
        in_specs=[pl.BlockSpec((groups * z.chan, block), lambda f: (0, f))],
        out_specs=[
            pl.BlockSpec((rows, block), lambda f: (0, f)),
            pl.BlockSpec((block, rows), lambda f: (f, 0)),
        ],
        out_shape=[
            jax.ShapeDtypeStruct((rows, hidden), BF16),
            jax.ShapeDtypeStruct((hidden, rows), BF16),
        ],
        scratch_shapes=[pltpu.VMEM((rows, block), F32)],
        compiler_params=params(),
        cost_estimate=cost(16 * 10**6),
    )(matrix)


def lane_block(rows, cells, part):
    return pl.BlockSpec((rows, cells), lambda *_: (0, part))


def row_step(rows, most):
    return max(n for n in range(16, most + 1, 16) if rows % n == 0)


def mlp(part, length, normed, out_grad, w_in_t, w_in, w_out, w_out_t, b_in, b_out, branch_all):
    packed, cells = normed.shape
    hidden = w_in_t.shape[0]
    block = block_of(hidden, 640)
    inner = row_step(block, 320)
    blocks = hidden // block
    pairs = block // inner // 2
    rows = row_step(packed, 416)
    outs = packed // rows

    def kernel(
        n_ref, g_ref, w_in_t_ref, w_in_ref, w_out_ref, w_out_t_ref, b_in_ref, b_out_ref, *rest
    ):
        (
            branch_ref, norm_ref, active_out, hidden_out,
            h_0, h_1, back_0, back_1, active, grads, sems,
        ) = rest[-11:]
        step = pl.program_id(0)

        def products(k, h, back):
            at = pl.ds(k * inner, inner)
            h[...] = (
                jnp.dot(w_in_t_ref[at, :], n_ref[...], preferred_element_type=F32) + b_in_ref[at, :]
            )
            back[...] = jnp.dot(w_out_ref[at, :], g_ref[:, :cells], preferred_element_type=F32)

        def gelu(k, h, back):
            at = pl.ds(pl.multiple_of(jnp.maximum(k, 0) * inner, inner), inner)
            value, slope = gelu_parts(h[...])
            active[at, :] = value.astype(BF16)
            grads[at, :] = (back[...] * slope).astype(BF16)

        @pl.when(step < blocks)
        def _():
            first = step * (2 * pairs)

            def body(i, carry):
                products(2 * i, h_0, back_0)
                gelu(first + 2 * i - 1, h_1, back_1)
                products(2 * i + 1, h_1, back_1)
                gelu(first + 2 * i, h_0, back_0)
                return carry

            lax.fori_loop(0, pairs, body, 0)

        copies = [
            pltpu.make_async_copy(active, active_out, sems.at[0]),
            pltpu.make_async_copy(grads, hidden_out, sems.at[1]),
        ]

        @pl.when(step == blocks)
        def _():
            gelu(2 * pairs * blocks - 1, h_1, back_1)
            for copy in copies:
                copy.start()

        @pl.when(step >= blocks)
        def _():
            branch = jnp.dot(w_out_t_ref[...], active[...], preferred_element_type=F32)
            branch_ref[:, :cells] = (branch + b_out_ref[...]).astype(BF16)
            norm = jnp.dot(w_in_ref[...], grads[...], preferred_element_type=F32)
            norm_ref[...] = norm.astype(BF16)

        @pl.when(step == blocks + outs - 1)
        def _():
            for copy in copies:
                copy.wait()

    def at_in(f):
        return jnp.minimum(f, blocks - 1)

    def at_out(f):
        return jnp.maximum(f - blocks, 0)

    tall_block = pl.BlockSpec((block, packed), lambda f: (at_in(f), 0))
    wide_block = pl.BlockSpec((rows, hidden), lambda f: (at_out(f), 0))
    anywhere = pl.BlockSpec(memory_space=pl.ANY)
    operands = [normed, out_grad, w_in_t, w_in, w_out, w_out_t, b_in, b_out]
    in_specs = [
        whole((packed, cells)), lane_block(packed, length, part),
        tall_block, wide_block, tall_block, wide_block,
        pl.BlockSpec((block, 1), lambda f: (at_in(f), 0)),
        pl.BlockSpec((rows, 1), lambda f: (at_out(f), 0)),
    ]
    aliases = {}
    if branch_all is not None:
        aliases = {len(operands): 0}
        operands.append(branch_all)
        in_specs.append(anywhere)
    buffer = pltpu.VMEM((inner, cells), F32)
    return pl.pallas_call(
        kernel,
        grid=(blocks + outs,),
        in_specs=in_specs,
        out_specs=[
            pl.BlockSpec((rows, length), lambda f: (at_out(f), part)),
            pl.BlockSpec((rows, cells), lambda f: (at_out(f), 0)),
            anywhere, anywhere,
        ],
        out_shape=[
            jax.ShapeDtypeStruct(out_grad.shape, BF16),
            jax.ShapeDtypeStruct((packed, cells), BF16),
            jax.ShapeDtypeStruct((hidden, cells), BF16),
            jax.ShapeDtypeStruct((hidden, cells), BF16),
        ],
        scratch_shapes=[buffer] * 4
        + [pltpu.VMEM((hidden, cells), BF16)] * 2
        + [pltpu.SemaphoreType.DMA((2,))],
        input_output_aliases=aliases,
        compiler_params=params(),
        cost_estimate=pl.CostEstimate(
            flops=8 * packed * cells * hidden, bytes_accessed=4 * 10**7, transcendentals=cells * hidden
        ),
    )(*operands)


def weight_grad(lefts, rights):
    rows, hidden = lefts[0][0].shape[0], rights[0].shape[0]
    block = block_of(hidden, 640)
    inner = row_step(rows, 832)
    arrays = []
    for array, _ in lefts:
        if not any(array is known for known in arrays):
            arrays.append(array)
    which = [next(k for k, known in enumerate(arrays) if known is array) for array, _ in lefts]

    def kernel(*refs):
        def body(m, carry):
            at = pl.ds(pl.multiple_of(m * inner, inner), inner)
            total = None
            for k, (_, start), right in zip(which, lefts, refs[len(arrays) : -1]):
                part = lax.dot_general(
                    refs[k][at, start : start + right.shape[1]], right[...],
                    (((1,), (1,)), ((), ())), preferred_element_type=F32,
                )
                total = part if total is None else total + part
            refs[-1][at, :] = total.astype(BF16)
            return carry

        lax.fori_loop(0, rows // inner, body, 0)

    cells = sum(right.shape[1] for right in rights)
    return pl.pallas_call(
        kernel,
        grid=(hidden // block,),
        in_specs=[whole(array.shape) for array in arrays]
        + [pl.BlockSpec((block, right.shape[1]), lambda f: (f, 0)) for right in rights],
        out_specs=pl.BlockSpec((rows, block), lambda f: (0, f)),
        out_shape=jax.ShapeDtypeStruct((rows, hidden), BF16),
        compiler_params=params(),
        cost_estimate=cost(24 * 10**6, 2 * rows * cells * hidden),
    )(*arrays, *rights)


def unpad_rows(z, matrix):
    groups, hidden = matrix.shape[0] // z.pad, matrix.shape[1]
    several = next(k for k in range(2, groups + 1, 2) if groups % k == 0 and k * z.chan % SUBL == 0)

    def kernel(in_ref, out_ref):
        value = in_ref[...].astype(F32)
        for k in range(several):
            out_ref[z.chan * k : z.chan * (k + 1), :] = value[z.pad * k : z.pad * k + z.chan, :]

    return pl.pallas_call(
        kernel,
        grid=(groups // several,),
        in_specs=[pl.BlockSpec((several * z.pad, hidden), lambda g: (g, 0))],
        out_specs=pl.BlockSpec((several * z.chan, hidden), lambda g: (g, 0)),
        out_shape=jax.ShapeDtypeStruct((groups * z.chan, hidden), F32),
        compiler_params=params(),
        cost_estimate=cost(16 * 10**6),
    )(matrix)


def exchange(value):
    return lax.all_to_all(value, CHAN, split_axis=0, concat_axis=0, tiled=True)


def after(value, *others):
    return lax.optimization_barrier((value, *others))[0]


def dp_sum(value):
    ways = lax.axis_size("dp")
    total = value
    for turn in range(1, ways):
        total = total + lax.ppermute(value, "dp", [(i, i ^ turn) for i in range(ways)])
    return total


def per_device(
    x_in, cotangent, land, grid_res, dw_kernel, gain, shift, res_bias, w_in, b_in, w_out, b_out
):
    samples, height, columns, chan = x_in.shape
    groups = lax.axis_size("pair") * CORES
    first = (lax.axis_index("pair") * CORES + lax.axis_index("core")) * chan
    width = chan * groups
    ntaps = dw_kernel.shape[0]
    z = Sizes(chan, height, columns, groups, ntaps)
    pixels = float(samples * lax.axis_size("dp") * height * columns)
    part = (z.units + 1) // 2 * LANES
    lengths = [part, z.units * LANES - part]
    starts = [0, part]

    def own(values, axis=0):
        return lax.dynamic_slice_in_dim(values, first, chan, axis)

    def over_lanes(rows):
        rows = jnp.pad(rows, ((0, 0), (0, z.pad - chan)))
        return jnp.broadcast_to(rows[:, :, None], rows.shape + (LANES,))

    x = jnp.transpose(x_in[0], (0, 2, 1))
    cot = jnp.transpose(cotangent[0], (0, 2, 1))
    land3 = land[0][:, None, :]

    grad_packed, part_b_out = pack_out_grad(z, sum(lengths), cot, land3)
    grad_band = exchange(grad_packed)

    taps = over_lanes(own(dw_kernel, 1).astype(F32))
    conv, total, square = conv_forward(z, taps, after(x, grad_packed))
    total, square = lax.psum((total, square), "dp")
    mean = total / pixels
    var = square / pixels - mean * mean
    scale = lax.rsqrt(var + 1e-05)
    own_gain = own(gain)
    chooser = (grid_res[:, None] == jnp.arange(2, dtype=jnp.int32)[None, :]).astype(F32)
    sample_bias = jnp.sum(chooser[0][:, None] * own(res_bias, 1), axis=0)
    affine = over_lanes(jnp.stack([mean, own_gain * scale, own(shift) + sample_bias]))
    packed = pack_normed(z, lengths, conv, affine)

    w_in_p, w_in_t = pad_weight(z, after(w_in, packed[0]))
    w_out_t, w_out_p = pad_weight(z, after(w_out.T, packed[0]))
    b_out_p = jnp.pad(b_out.reshape(groups, chan), ((0, 0), (0, z.pad - chan))).reshape(-1, 1)
    weights = (w_in_t, w_in_p, w_out_p, w_out_t, b_in[:, None], b_out_p)

    normed = [exchange(after(packed[0], grad_band))]
    normed.append(exchange(after(packed[1], normed[0], w_in_t, w_out_p)))
    branch, norm1, active1, hidden1 = mlp(0, part, normed[0], grad_band, *weights, None)
    norm_parts = [exchange(after(norm1, normed[1]))]
    branch, norm2, active2, hidden2 = mlp(1, part, normed[1], grad_band, *weights, branch)
    norm_parts.append(exchange(after(norm2, norm_parts[0])))
    g_w_out_t = weight_grad(
        [(grad_band, start) for start in starts], [active1, after(active2, norm_parts[0])]
    )
    g_w_in = weight_grad(
        [(value, 0) for value in normed], [hidden1, after(hidden2, g_w_out_t)]
    )
    branch = exchange(after(branch, norm_parts[1], g_w_in))
    g_w_out_t = lax.psum(g_w_out_t, ("dp",) + CHAN)
    g_w_in = lax.psum(g_w_in, CHAN + ("dp",))

    part_shift, part_gain = norm_sums(z, norm_parts, conv, over_lanes(jnp.stack([mean, scale])))
    small = jnp.concatenate(
        [part_shift[None], part_gain[None], chooser[0][:, None] * part_shift[None], part_b_out[None]],
        axis=0,
    )
    small = lax.psum(small, "dp")
    terms = over_lanes(
        jnp.stack([mean, scale, own_gain * scale, small[0] / pixels, small[1] / pixels])
    )
    conv_grad, g_kernel = conv_gradient(z, terms, norm_parts, conv, x, ntaps)
    g_kernel = dp_sum(g_kernel)
    x_grad = conv_backward(z, taps, conv_grad, cot, land3)
    rows = jnp.concatenate([after(g_kernel, x_grad), small], axis=0)
    gathered = lax.all_gather(rows, CHAN)
    placed = jnp.transpose(gathered, (1, 0, 2)).reshape(rows.shape[0], width)
    mixed = mix_branch(z, branch, after(x, x_grad), land3)
    g_w_out_t, g_w_in = after(g_w_out_t, mixed), after(g_w_in, mixed)

    return (
        jnp.transpose(mixed, (0, 2, 1))[None],
        jnp.transpose(x_grad, (0, 2, 1))[None],
        placed[:ntaps],
        placed[ntaps + 1],
        placed[ntaps],
        placed[ntaps + 2 : ntaps + 4],
        unpad_rows(z, g_w_in),
        g_w_in[chan].astype(F32),
        unpad_rows(z, g_w_out_t).T,
        placed[ntaps + 4],
    )


def solution(mesh):
    shape = mesh.shape
    mesh = jax.sharding.Mesh(
        mesh.devices.reshape(shape["dp"], shape["chan"] // CORES, CORES), ("dp",) + CHAN
    )
    cells = P("dp", None, None, CHAN)
    return jax.shard_map(
        per_device,
        mesh=mesh,
        in_specs=(cells, cells, P("dp", None, None), P("dp")) + (P(),) * 8,
        out_specs=(cells, cells) + (P(),) * 8,
        check_vma=False,
    )
```

```python
from functools import partial
import math

import jax
import jax.numpy as jnp
from jax import lax
from jax.experimental import pallas as pl
from jax.experimental.pallas import tpu as pltpu
from jax.sharding import PartitionSpec as P

LANES = 128
SUBL = 8
VMEM_LIMIT = 56 * 1024 * 1024
CHAN = ("pair", "core")
CORES = 2
F32 = jnp.float32
BF16 = jnp.bfloat16


def round_up(value, step):
    return (value + step - 1) // step * step


def block_of(total, most):
    return max(size for size in range(1, most + 1) if total % size == 0)


class Sizes:
    def __init__(self, chan, height, width, bands, taps):
        self.chan, self.height, self.width, self.bands = chan, height, width, bands
        self.side = math.isqrt(taps)
        self.margin = self.side // 2
        self.rows = height // bands
        self.wide = round_up(width + 2 * self.margin, LANES)
        self.tiles = self.wide // LANES
        self.tail = width - (self.tiles - 1) * LANES
        self.pad = round_up(chan + 1, SUBL)
        self.packed_rows = bands * self.pad
        self.tail_units = round_up(self.rows * self.tail, LANES) // LANES
        self.units = self.rows * (self.tiles - 1) + self.tail_units


def params(semantics=("arbitrary",)):
    return pltpu.CompilerParams(dimension_semantics=semantics, vmem_limit_bytes=VMEM_LIMIT)


def roll_tiles(z, tiles, shift):
    jump, low = divmod(shift % z.wide, LANES)
    count = z.tiles
    if low == 0:
        return [tiles[(j - jump) % count] for j in range(count)]
    lane = lax.broadcasted_iota(jnp.int32, tiles[0].shape, 1)
    moved = [pltpu.roll(tile, low, 1) for tile in tiles]
    return [
        jnp.where(lane < low, moved[(j - jump - 1) % count], moved[(j - jump) % count])
        for j in range(count)
    ]


def wrap_tiles(z, tiles):
    last = tiles[-1]
    lane = lax.broadcasted_iota(jnp.int32, last.shape, 1)
    ahead = pltpu.roll(tiles[0], z.tail, 1)
    behind = pltpu.roll(last, LANES - z.tail, 1)
    last = jnp.where(lane < z.tail, last, jnp.where(lane < z.tail + z.margin, ahead, behind))
    return tiles[:-1] + [last]


def row_tiles(z, value):
    tiles = [value[:, LANES * j : LANES * (j + 1)] for j in range(z.tiles - 1)]
    tail = value[:, LANES * (z.tiles - 1) :]
    zeros = jnp.zeros((value.shape[0], LANES - z.tail), F32)
    return tiles + [jnp.concatenate([tail, zeros], axis=1)]


def pack_tails(z, tails):
    lane = lax.broadcasted_iota(jnp.int32, tails[0].shape, 1)
    tiles = []
    for t in range(z.tail_units):
        begin, tile = LANES * t, None
        for row, tail in enumerate(tails):
            low = z.tail * row - begin
            if low >= LANES or low + z.tail <= 0:
                continue
            moved = pltpu.roll(tail, low % LANES, 1) if low % LANES else tail
            tile = moved if tile is None else jnp.where(lane >= low, moved, tile)
        end = z.tail * z.rows - begin
        tiles.append(jnp.where(lane < end, tile, 0.0) if end < LANES else tile)
    return tiles


def unpack_tails(z, tiles):
    lane = lax.broadcasted_iota(jnp.int32, tiles[0].shape, 1)
    tails = []
    for row in range(z.rows):
        t, low = divmod(z.tail * row, LANES)
        tail = pltpu.roll(tiles[t], LANES - low, 1) if low else tiles[t]
        if LANES - low < z.tail:
            tail = jnp.where(lane < LANES - low, tail, pltpu.roll(tiles[t + 1], LANES - low, 1))
        tails.append(jnp.where(lane < z.tail, tail, 0.0))
    return tails


def pack_rows(z, rows):
    full = z.tiles - 1
    return [row[j] for row in rows for j in range(full)] + pack_tails(z, [row[full] for row in rows])


def unpack_rows(z, tiles):
    full = z.tiles - 1
    tails = unpack_tails(z, tiles[z.rows * full :])
    return [tiles[row * full : (row + 1) * full] + [tails[row]] for row in range(z.rows)]


def packed_tiles(refs, read):
    return [
        read(ref, slice(LANES * k, LANES * (k + 1)))
        for ref in refs
        for k in range(ref.shape[-1] // LANES)
    ]


def whole(shape):
    return pl.BlockSpec(shape, lambda *_: (0,) * len(shape))


def smem():
    return pl.BlockSpec(memory_space=pltpu.SMEM)


def cost(bytes_accessed, flops=10**7):
    return pl.CostEstimate(flops=flops, bytes_accessed=bytes_accessed, transcendentals=0)


PAIR = 2
GROUP = 16


def pair_rows(z):
    return pl.BlockSpec((PAIR * z.rows, z.pad, z.width), lambda g: (g, 0, 0))


def pair_wide(z):
    return pl.BlockSpec((PAIR * z.rows, z.pad, z.wide), lambda g: (g, 0, 0))


def pair_land(z):
    return pl.BlockSpec((PAIR * z.rows, 1, z.width), lambda g: (g, 0, 0))


def pair_packed(z, cells):
    return pl.BlockSpec((PAIR * z.pad, cells), lambda g: (g, 0))


def group_rows(z):
    return pl.BlockSpec((z.height, GROUP, z.width), lambda c: (0, c, 0))


def group_wide(z):
    return pl.BlockSpec((z.height, GROUP, z.wide), lambda c: (0, c, 0))


def group_lanes(count):
    return pl.BlockSpec((count, GROUP, LANES), lambda c: (0, c, 0))


def write_pair(z, refs, bands):
    tiles = [jnp.concatenate(both, axis=0).astype(BF16) for both in zip(*bands)]
    unit = 0
    for ref in refs:
        for k in range(ref.shape[1] // LANES):
            ref[:, LANES * k : LANES * (k + 1)] = tiles[unit]
            unit += 1


def pack_out_grad(z, cells, cot, land):
    def kernel(cot_ref, land_ref, out_ref, sum_ref):
        @pl.when(pl.program_id(0) == 0)
        def _():
            sum_ref[...] = jnp.zeros_like(sum_ref)

        channel = lax.broadcasted_iota(jnp.int32, (z.pad, z.width), 0)
        total = jnp.zeros((z.pad, LANES), F32)
        bands = []
        for band in range(PAIR):
            rows = []
            for row in range(z.rows * band, z.rows * (band + 1)):
                value = cot_ref[row].astype(F32) * land_ref[row].astype(F32)
                rows.append(row_tiles(z, jnp.where(channel < z.chan, value, 0.0)))
                total = total + sum(rows[-1])
            bands.append(pack_rows(z, rows))
        sum_ref[...] += total
        write_pair(z, [out_ref], bands)

    out, sums = pl.pallas_call(
        kernel,
        grid=(z.bands // PAIR,),
        in_specs=[pair_rows(z), pair_land(z)],
        out_specs=[pair_packed(z, cells), whole((z.pad, LANES))],
        out_shape=[
            jax.ShapeDtypeStruct((z.packed_rows, cells), BF16),
            jax.ShapeDtypeStruct((z.pad, LANES), F32),
        ],
        compiler_params=params(),
        cost_estimate=cost(8 * 10**6),
    )(cot, land)
    return out, jnp.sum(sums, axis=1)[: z.chan]


def fill_rows(z, target, read, wrap):
    zeros = jnp.zeros(target.shape[1:], F32)
    for k in range(z.margin):
        target[k] = zeros
        target[z.margin + z.height + k] = zeros

    def body(h, carry):
        tiles = row_tiles(z, read(h))
        if wrap:
            tiles = wrap_tiles(z, tiles)
        for j, tile in enumerate(tiles):
            target[z.margin + h, :, LANES * j : LANES * (j + 1)] = tile
        return carry

    lax.fori_loop(0, z.height, body, 0, unroll=8)


def convolve(z, steps, at, taps_ref, source, flip, put, carry):
    span = steps + 2 * z.margin

    def body(block, carry):
        h0 = block * steps
        rows = [
            [source[h0 + m, at, LANES * j : LANES * (j + 1)] for j in range(z.tiles)]
            for m in range(span)
        ]
        sums = [None] * steps
        for b in range(z.side):
            weights = [taps_ref[z.side * a + b, at, :] for a in range(z.side)]
            for r in range(steps):
                part = None
                for a in range(z.side):
                    row = rows[r + 2 * z.margin - a] if flip else rows[r + a]
                    terms = [weights[a] * tile for tile in row]
                    part = terms if part is None else [p + t for p, t in zip(part, terms)]
                part = roll_tiles(z, part, b - z.margin if flip else z.margin - b)
                sums[r] = part if b == 0 else [s + p for s, p in zip(sums[r], part)]
        for r in range(steps):
            carry = put(h0 + r, sums[r], carry)
        return carry

    return lax.fori_loop(0, z.height // steps, body, carry, unroll=2)


def conv_forward(z, taps, x):
    def kernel(taps_ref, x_ref, conv_ref, sum_ref, square_ref, source):
        fill_rows(z, source, lambda h: x_ref[h].astype(F32), True)
        lane = lax.broadcasted_iota(jnp.int32, (SUBL, LANES), 1)
        for part in range(GROUP // SUBL):
            at = slice(SUBL * part, SUBL * (part + 1))

            def put(h, tiles, carry):
                for j, tile in enumerate(tiles):
                    conv_ref[h, at, LANES * j : LANES * (j + 1)] = tile
                tiles = tiles[:-1] + [jnp.where(lane < z.tail, tiles[-1], 0.0)]
                return carry[0] + sum(tiles), carry[1] + sum(t * t for t in tiles)

            @pl.when(pl.program_id(0) * GROUP + SUBL * part < z.chan)
            def _():
                zero = jnp.zeros((SUBL, LANES), F32)
                total, square = convolve(z, 4, at, taps_ref, source, False, put, (zero, zero))
                sum_ref[at, :] = total
                square_ref[at, :] = square

    lane_spec = pl.BlockSpec((GROUP, LANES), lambda c: (c, 0))
    lane_shape = jax.ShapeDtypeStruct((z.pad, LANES), F32)
    conv, total, square = pl.pallas_call(
        kernel,
        grid=(pl.cdiv(z.chan, GROUP),),
        in_specs=[group_lanes(taps.shape[0]), group_rows(z)],
        out_specs=[group_wide(z), lane_spec, lane_spec],
        out_shape=[
            jax.ShapeDtypeStruct((z.height, z.pad, z.wide), F32), lane_shape, lane_shape,
        ],
        scratch_shapes=[pltpu.VMEM((z.height + 2 * z.margin, GROUP, z.wide), F32)],
        compiler_params=params(),
        cost_estimate=cost(16 * 10**6, 10**10),
    )(taps, x)
    return conv, jnp.sum(total, axis=1)[: z.chan], jnp.sum(square, axis=1)[: z.chan]


def pack_normed(z, lengths, conv, columns):
    def kernel(columns_ref, conv_ref, *outs):
        channel = lax.broadcasted_iota(jnp.int32, (z.pad, LANES), 0)
        filler = jnp.where(channel == z.chan, 1.0, 0.0)
        mean, factor, offset = columns_ref[0], columns_ref[1], columns_ref[2]
        bands = []
        for band in range(PAIR):
            rows = []
            for row in range(z.rows * band, z.rows * (band + 1)):
                tiles = [conv_ref[row, :, LANES * j : LANES * (j + 1)] for j in range(z.tiles)]
                rows.append(
                    [
                        jnp.where(channel < z.chan, (tile - mean) * factor + offset, filler)
                        for tile in tiles
                    ]
                )
            bands.append(pack_rows(z, rows))
        write_pair(z, outs, bands)

    return pl.pallas_call(
        kernel,
        grid=(z.bands // PAIR,),
        in_specs=[whole(columns.shape), pair_wide(z)],
        out_specs=[pair_packed(z, n) for n in lengths],
        out_shape=[jax.ShapeDtypeStruct((z.packed_rows, n), BF16) for n in lengths],
        compiler_params=params(),
        cost_estimate=cost(12 * 10**6),
    )(columns, conv)


def norm_sums(z, parts, conv, columns):
    count = len(parts)

    def kernel(columns_ref, conv_ref, *rest):
        ins, (shift_ref, gain_ref) = rest[:count], rest[count:]

        @pl.when(pl.program_id(0) == 0)
        def _():
            shift_ref[...] = jnp.zeros_like(shift_ref)
            gain_ref[...] = jnp.zeros_like(gain_ref)

        mean = columns_ref[0]
        tiles = packed_tiles(ins, lambda ref, lanes: ref[:, lanes].astype(F32))
        shift = jnp.zeros((z.pad, LANES), F32)
        gain = jnp.zeros((z.pad, LANES), F32)
        for band in range(PAIR):
            rows = unpack_rows(z, [tile[z.pad * band : z.pad * (band + 1)] for tile in tiles])
            for row, grads in enumerate(rows):
                for j, grad in enumerate(grads):
                    value = conv_ref[z.rows * band + row, :, LANES * j : LANES * (j + 1)]
                    shift = shift + grad
                    gain = gain + grad * (value - mean)
        shift_ref[...] += shift
        gain_ref[...] += gain * columns_ref[1]

    lane_shape = jax.ShapeDtypeStruct((z.pad, LANES), F32)
    shift, gain = pl.pallas_call(
        kernel,
        grid=(z.bands // PAIR,),
        in_specs=[whole(columns.shape), pair_wide(z)] + [pair_packed(z, p.shape[1]) for p in parts],
        out_specs=[whole((z.pad, LANES))] * 2,
        out_shape=[lane_shape, lane_shape],
        compiler_params=params(),
        cost_estimate=cost(12 * 10**6),
    )(columns, conv, *parts)
    return jnp.sum(shift, axis=1)[: z.chan], jnp.sum(gain, axis=1)[: z.chan]


def conv_gradient(z, begin, end, columns, parts, conv, x, ntaps, before):
    count = len(parts)
    parts = [part.reshape(z.bands, z.pad, part.shape[1]) for part in parts]
    steps = 4
    before = [] if before is None else list(before)

    def kernel(columns_ref, conv_ref, x_ref, *rest):
        ins, (grad_ref, product_ref, grads, source) = rest[:count], rest[-4:]
        mean, scale, factor, shift, gain = (columns_ref[k] for k in range(5))

        def band_body(band, carry):
            tiles = packed_tiles(ins, lambda ref, lanes: ref[band, :, lanes].astype(F32))
            for row, values in enumerate(unpack_rows(z, tiles)):
                h = band * z.rows + row
                made = []
                for j, value in enumerate(values):
                    centred = (conv_ref[h, :, LANES * j : LANES * (j + 1)] - mean) * scale
                    made.append(factor * (value - (shift + centred * gain)))
                for j, tile in enumerate(wrap_tiles(z, made)):
                    at = slice(LANES * j, LANES * (j + 1))
                    grads[h, :, at] = tile
                    grad_ref[h, :, at] = tile.astype(BF16)
            return carry

        lax.fori_loop(0, z.bands, band_body, 0)
        fill_rows(z, source, lambda h: x_ref[h].astype(F32), False)
        for part in range(GROUP // SUBL):
            at = slice(SUBL * part, SUBL * (part + 1))

            @pl.when((begin + pl.program_id(0)) * GROUP + SUBL * part < z.chan)
            def _():
                for b in range(z.side):

                    def body(block, totals):
                        h0 = block * steps
                        rows = [
                            [source[h0 + m, at, LANES * j : LANES * (j + 1)] for j in range(z.tiles)]
                            for m in range(steps + 2 * z.margin)
                        ]
                        totals = list(totals)
                        for r in range(steps):
                            moved = roll_tiles(
                                z,
                                [grads[h0 + r, at, LANES * j : LANES * (j + 1)] for j in range(z.tiles)],
                                b - z.margin,
                            )
                            for a in range(z.side):
                                for m, tile in zip(moved, rows[r + a]):
                                    totals[a] = totals[a] + m * tile
                        return tuple(totals)

                    zero = jnp.zeros((SUBL, LANES), F32)
                    totals = lax.fori_loop(0, z.height // steps, body, (zero,) * z.side, unroll=4)
                    for a in range(z.side):
                        product_ref[z.side * a + b, at, :] = totals[a]

    def group(shape):
        return pl.BlockSpec(shape, lambda c: (0, begin + c, 0))

    operands = [columns, conv, x, *parts, *before]
    return pl.pallas_call(
        kernel,
        grid=(end - begin,),
        in_specs=[
            group((5, GROUP, LANES)), group((z.height, GROUP, z.wide)),
            group((z.height, GROUP, z.width)),
        ]
        + [group((z.bands, GROUP, p.shape[2])) for p in parts]
        + [pl.BlockSpec(memory_space=pl.ANY)] * len(before),
        out_specs=[group((z.height, GROUP, z.wide)), group((ntaps, GROUP, LANES))],
        out_shape=[
            jax.ShapeDtypeStruct((z.height, z.pad, z.wide), BF16),
            jax.ShapeDtypeStruct((ntaps, z.pad, LANES), F32),
        ],
        scratch_shapes=[
            pltpu.VMEM((z.height, GROUP, z.wide), F32),
            pltpu.VMEM((z.height + 2 * z.margin, GROUP, z.wide), F32),
        ],
        input_output_aliases={len(operands) - 2 + k: k for k in range(len(before))},
        compiler_params=params(),
        cost_estimate=cost(10 * 10**6, 4 * 10**9),
    )(*operands)


def conv_backward(z, taps, grad, cot, land):
    def kernel(taps_ref, grad_ref, cot_ref, land_ref, out_ref, source, result):
        zeros = jnp.zeros(source.shape[1:], F32)
        for k in range(z.margin):
            source[k] = zeros
            source[z.margin + z.height + k] = zeros

        def fill(h, carry):
            source[z.margin + h] = grad_ref[h].astype(F32)
            return carry

        lax.fori_loop(0, z.height, fill, 0, unroll=8)
        for part in range(GROUP // SUBL):
            at = slice(SUBL * part, SUBL * (part + 1))

            def put(h, tiles, carry):
                for j, tile in enumerate(tiles):
                    result[h, at, LANES * j : LANES * (j + 1)] = tile
                return carry

            @pl.when(pl.program_id(0) * GROUP + SUBL * part < z.chan)
            def _():
                convolve(z, 4, at, taps_ref, source, True, put, 0)

        def finish(h, carry):
            direct = cot_ref[h].astype(F32) * land_ref[h].astype(F32)
            out_ref[h] = (direct + result[h][:, : z.width]).astype(BF16)
            return carry

        lax.fori_loop(0, z.height, finish, 0, unroll=8)

    return pl.pallas_call(
        kernel,
        grid=(pl.cdiv(z.chan, GROUP),),
        in_specs=[
            group_lanes(taps.shape[0]), group_wide(z), group_rows(z),
            whole((z.height, 1, z.width)),
        ],
        out_specs=group_rows(z),
        out_shape=jax.ShapeDtypeStruct((z.height, z.chan, z.width), BF16),
        scratch_shapes=[
            pltpu.VMEM((z.height + 2 * z.margin, GROUP, z.wide), F32),
            pltpu.VMEM((z.height, GROUP, z.wide), F32),
        ],
        compiler_params=params(),
        cost_estimate=cost(16 * 10**6, 10**10),
    )(taps, grad, cot, land)


def mix_branch(z, branch, x, land):
    def kernel(x_ref, land_ref, branch_ref, out_ref):
        tiles = packed_tiles([branch_ref], lambda ref, lanes: ref[:, lanes].astype(F32))
        for band in range(PAIR):
            rows = unpack_rows(z, [tile[z.pad * band : z.pad * (band + 1)] for tile in tiles])
            for k, row in enumerate(rows):
                h = z.rows * band + k
                value = jnp.concatenate(row, axis=1)[:, : z.width]
                value = land_ref[h].astype(F32) * (x_ref[h].astype(F32) + value)
                out_ref[h] = value.astype(BF16)

    return pl.pallas_call(
        kernel,
        grid=(z.bands // PAIR,),
        in_specs=[pair_rows(z), pair_land(z), pair_packed(z, branch.shape[1])],
        out_specs=pair_rows(z),
        out_shape=jax.ShapeDtypeStruct((z.height, z.chan, z.width), BF16),
        compiler_params=params(),
        cost_estimate=cost(12 * 10**6),
    )(x, land, branch)


def gelu_parts(h):
    span = 1.0 + (0.3275911 * math.sqrt(0.5)) * jnp.abs(h)
    t = pl.reciprocal(span, approx=True)
    t = t * (2.0 - span * t)
    bell = jnp.exp2((-0.5 / math.log(2.0)) * (h * h))
    poly = t * (
        0.5 * 0.254829592
        + t
        * (
            0.5 * -0.284496736
            + t * (0.5 * 1.421413741 + t * (0.5 * -1.453152027 + t * (0.5 * 1.061405429)))
        )
    )
    tail = poly * bell
    phi = jnp.where(h >= 0, 1.0 - tail, tail)
    return h * phi, phi + h * ((1.0 / math.sqrt(2.0 * math.pi)) * bell)


def pad_weight(z, matrix):
    groups, hidden = matrix.shape[0] // z.chan, matrix.shape[1]
    block = block_of(hidden, 640)
    rows = groups * z.pad

    def kernel(in_ref, out_ref, transposed_ref, wide):
        value = in_ref[...].astype(F32)
        zeros = jnp.zeros((z.pad - z.chan, block), F32)
        for k in range(groups):
            wide[z.pad * k : z.pad * (k + 1), :] = jnp.concatenate(
                [value[z.chan * k : z.chan * (k + 1), :], zeros], axis=0
            )
        padded = wide[...]
        out_ref[...] = padded.astype(BF16)
        transposed_ref[...] = padded.T.astype(BF16)

    return pl.pallas_call(
        kernel,
        grid=(hidden // block,),
        in_specs=[pl.BlockSpec((groups * z.chan, block), lambda f: (0, f))],
        out_specs=[
            pl.BlockSpec((rows, block), lambda f: (0, f)),
            pl.BlockSpec((block, rows), lambda f: (f, 0)),
        ],
        out_shape=[
            jax.ShapeDtypeStruct((rows, hidden), BF16),
            jax.ShapeDtypeStruct((hidden, rows), BF16),
        ],
        scratch_shapes=[pltpu.VMEM((rows, block), F32)],
        compiler_params=params(),
        cost_estimate=cost(16 * 10**6),
    )(matrix)


def lane_block(rows, cells, part):
    return pl.BlockSpec((rows, cells), lambda *_: (0, part))


def row_step(rows, most):
    return max(n for n in range(16, most + 1, 16) if rows % n == 0)


def mlp(part, length, normed, out_grad, w_in_t, w_in, w_out, w_out_t, b_in, b_out, branch_all):
    packed, cells = normed.shape
    hidden = w_in_t.shape[0]
    block = block_of(hidden, 640)
    inner = row_step(block, 320)
    blocks = hidden // block
    pairs = block // inner // 2
    rows = row_step(packed, 416)
    outs = packed // rows

    def kernel(
        n_ref, g_ref, w_in_t_ref, w_in_ref, w_out_ref, w_out_t_ref, b_in_ref, b_out_ref, *rest
    ):
        (
            branch_ref, norm_ref, active_out, hidden_out,
            h_0, h_1, back_0, back_1, active, grads, sems,
        ) = rest[-11:]
        step = pl.program_id(0)

        def products(k, h, back):
            at = pl.ds(k * inner, inner)
            h[...] = (
                jnp.dot(w_in_t_ref[at, :], n_ref[...], preferred_element_type=F32) + b_in_ref[at, :]
            )
            back[...] = jnp.dot(w_out_ref[at, :], g_ref[:, :cells], preferred_element_type=F32)

        def gelu(k, h, back):
            at = pl.ds(pl.multiple_of(jnp.maximum(k, 0) * inner, inner), inner)
            value, slope = gelu_parts(h[...])
            active[at, :] = value.astype(BF16)
            grads[at, :] = (back[...] * slope).astype(BF16)

        @pl.when(step < blocks)
        def _():
            first = step * (2 * pairs)

            def body(i, carry):
                products(2 * i, h_0, back_0)
                gelu(first + 2 * i - 1, h_1, back_1)
                products(2 * i + 1, h_1, back_1)
                gelu(first + 2 * i, h_0, back_0)
                return carry

            lax.fori_loop(0, pairs, body, 0)

        copies = [
            pltpu.make_async_copy(active, active_out, sems.at[0]),
            pltpu.make_async_copy(grads, hidden_out, sems.at[1]),
        ]

        @pl.when(step == blocks)
        def _():
            gelu(2 * pairs * blocks - 1, h_1, back_1)
            for copy in copies:
                copy.start()

        @pl.when(step >= blocks)
        def _():
            branch = jnp.dot(w_out_t_ref[...], active[...], preferred_element_type=F32)
            branch_ref[:, :cells] = (branch + b_out_ref[...]).astype(BF16)
            norm = jnp.dot(w_in_ref[...], grads[...], preferred_element_type=F32)
            norm_ref[...] = norm.astype(BF16)

        @pl.when(step == blocks + outs - 1)
        def _():
            for copy in copies:
                copy.wait()

    def at_in(f):
        return jnp.minimum(f, blocks - 1)

    def at_out(f):
        return jnp.maximum(f - blocks, 0)

    tall_block = pl.BlockSpec((block, packed), lambda f: (at_in(f), 0))
    wide_block = pl.BlockSpec((rows, hidden), lambda f: (at_out(f), 0))
    anywhere = pl.BlockSpec(memory_space=pl.ANY)
    operands = [normed, out_grad, w_in_t, w_in, w_out, w_out_t, b_in, b_out]
    in_specs = [
        whole((packed, cells)), lane_block(packed, length, part),
        tall_block, wide_block, tall_block, wide_block,
        pl.BlockSpec((block, 1), lambda f: (at_in(f), 0)),
        pl.BlockSpec((rows, 1), lambda f: (at_out(f), 0)),
    ]
    aliases = {}
    if branch_all is not None:
        aliases = {len(operands): 0}
        operands.append(branch_all)
        in_specs.append(anywhere)
    buffer = pltpu.VMEM((inner, cells), F32)
    return pl.pallas_call(
        kernel,
        grid=(blocks + outs,),
        in_specs=in_specs,
        out_specs=[
            pl.BlockSpec((rows, length), lambda f: (at_out(f), part)),
            pl.BlockSpec((rows, cells), lambda f: (at_out(f), 0)),
            anywhere, anywhere,
        ],
        out_shape=[
            jax.ShapeDtypeStruct(out_grad.shape, BF16),
            jax.ShapeDtypeStruct((packed, cells), BF16),
            jax.ShapeDtypeStruct((hidden, cells), BF16),
            jax.ShapeDtypeStruct((hidden, cells), BF16),
        ],
        scratch_shapes=[buffer] * 4
        + [pltpu.VMEM((hidden, cells), BF16)] * 2
        + [pltpu.SemaphoreType.DMA((2,))],
        input_output_aliases=aliases,
        compiler_params=params(),
        cost_estimate=pl.CostEstimate(
            flops=8 * packed * cells * hidden, bytes_accessed=4 * 10**7, transcendentals=cells * hidden
        ),
    )(*operands)


def weight_grad(core, lefts, rights):
    rows, hidden = lefts[0][0].shape[0], rights[0].shape[0]
    half = rows // CORES
    block = block_of(hidden, 640)
    arrays = []
    for array, _ in lefts:
        if not any(array is known for known in arrays):
            arrays.append(array)
    which = [next(k for k, known in enumerate(arrays) if known is array) for array, _ in lefts]

    def kernel(core_ref, *refs):
        mine_ref, sent_ref, both = refs[-3:]
        total = None
        for k, (_, start), right in zip(which, lefts, refs[len(arrays) : -3]):
            part = lax.dot_general(
                refs[k][:, start : start + right.shape[1]], right[...],
                (((1,), (1,)), ((), ())), preferred_element_type=F32,
            )
            total = part if total is None else total + part
        both[0] = total[:half].astype(BF16)
        both[1] = total[half:].astype(BF16)
        mine_ref[...] = both[core_ref[0]]
        sent_ref[...] = both[1 - core_ref[0]]

    cells = sum(right.shape[1] for right in rights)
    out = jax.ShapeDtypeStruct((half, hidden), BF16)
    return pl.pallas_call(
        kernel,
        grid=(hidden // block,),
        in_specs=[smem()] + [whole(array.shape) for array in arrays]
        + [pl.BlockSpec((block, right.shape[1]), lambda f: (f, 0)) for right in rights],
        out_specs=[pl.BlockSpec((half, block), lambda f: (0, f))] * 2,
        out_shape=[out, out],
        scratch_shapes=[pltpu.VMEM((CORES, half, block), BF16)],
        compiler_params=params(),
        cost_estimate=cost(24 * 10**6, 2 * rows * cells * hidden),
    )(core[None], *arrays, *rights)


def unpad_rows(z, place, pieces):
    groups, hidden = pieces[0].shape[0] // z.pad, pieces[0].shape[1]

    def kernel(place_ref, *refs):
        out_ref = refs[-1]

        def put(ref):
            value = ref[...].astype(F32)
            for k in range(groups):
                out_ref[z.chan * k : z.chan * (k + 1), :] = value[z.pad * k : z.pad * k + z.chan, :]

        wanted = jnp.bitwise_xor(pl.program_id(0), place_ref[0])
        for k, ref in enumerate(refs[:-1]):
            pl.when(wanted == k)(partial(put, ref))

    return pl.pallas_call(
        kernel,
        grid=(4,),
        in_specs=[smem()] + [whole(pieces[0].shape)] * 4,
        out_specs=pl.BlockSpec((groups * z.chan, hidden), lambda q: (q, 0)),
        out_shape=jax.ShapeDtypeStruct((4 * groups * z.chan, hidden), F32),
        compiler_params=params(),
        cost_estimate=cost(16 * 10**6),
    )(place[None], *pieces)


def exchange(value):
    return lax.all_to_all(value, CHAN, split_axis=0, concat_axis=0, tiled=True)


def after(value, *others):
    return lax.optimization_barrier((value, *others))[0]


def dp_sum(value):
    ways = lax.axis_size("dp")
    total = value
    for turn in range(1, ways):
        total = total + lax.ppermute(value, "dp", [(i, i ^ turn) for i in range(ways)])
    return total


def swap_cores(value):
    return lax.ppermute(value, "core", [(0, 1), (1, 0)])


class HalvingSum:
    def __init__(self, turns, mine, sent):
        place = lax.axis_index("dp")
        self.turns = turns
        self.bits = [jnp.bitwise_and(place // turn, 1) for turn in turns]
        self.core = lax.axis_index("core")
        self.mine, self.other = mine, swap_cores(sent)

    def meet(self, value, turn):
        ways = lax.axis_size("dp")
        return lax.ppermute(value, "dp", [(i, i ^ turn) for i in range(ways)])

    def pair(self, half):
        rows = self.mine.shape[0] // 2
        at = half * rows
        return lax.dynamic_slice_in_dim(self.mine, at, rows, 0).astype(
            F32
        ) + lax.dynamic_slice_in_dim(self.other, at, rows, 0).astype(F32)

    def first(self):
        self.arrived = self.meet(self.pair(1 - self.bits[0]).astype(BF16), self.turns[0])

    def second(self, ready):
        arrived = after(self.arrived, ready)
        total = self.pair(self.bits[0]) + arrived.astype(F32)
        rows = total.shape[0] // 2
        send = lax.dynamic_slice_in_dim(total, (1 - self.bits[1]) * rows, rows, 0).astype(BF16)
        self.kept = lax.dynamic_slice_in_dim(total, self.bits[1] * rows, rows, 0)
        self.sent = send
        self.arrived = self.meet(send, self.turns[1])

    def share(self, ready):
        return (self.kept + after(self.arrived, ready).astype(F32)).astype(BF16)

    def back_first(self, share):
        self.own = share
        self.arrived = self.meet(share, self.turns[1])

    def back_second(self, ready):
        other = after(self.arrived, ready)
        low = self.bits[1] == 0
        self.own = jnp.concatenate(
            [jnp.where(low, self.own, other), jnp.where(low, other, self.own)], axis=0
        )
        self.arrived = self.meet(self.own, self.turns[0])
        self.swapped = swap_cores(self.own)

    def finish(self, z, ready):
        other = after(self.arrived, ready)
        pieces = [self.own, other, self.swapped, swap_cores(other)]
        return unpad_rows(z, self.core * 2 + self.bits[0], pieces), pieces

    def first_row(self, pieces, row):
        place = self.core * 2 + self.bits[0]
        found = pieces[0][row]
        for k in range(1, 4):
            found = jnp.where(place == k, pieces[k][row], found)
        return found.astype(F32)


def per_device(
    x_in, cotangent, land, grid_res, dw_kernel, gain, shift, res_bias, w_in, b_in, w_out, b_out
):
    samples, height, columns, chan = x_in.shape
    groups = lax.axis_size("pair") * CORES
    first = (lax.axis_index("pair") * CORES + lax.axis_index("core")) * chan
    width = chan * groups
    ntaps = dw_kernel.shape[0]
    z = Sizes(chan, height, columns, groups, ntaps)
    pixels = float(samples * lax.axis_size("dp") * height * columns)
    part = (z.units + 1) // 2 * LANES
    lengths = [part, z.units * LANES - part]
    starts = [0, part]

    def own(values, axis=0):
        return lax.dynamic_slice_in_dim(values, first, chan, axis)

    def over_lanes(rows):
        rows = jnp.pad(rows, ((0, 0), (0, z.pad - chan)))
        return jnp.broadcast_to(rows[:, :, None], rows.shape + (LANES,))

    x = jnp.transpose(x_in[0], (0, 2, 1))
    cot = jnp.transpose(cotangent[0], (0, 2, 1))
    land3 = land[0][:, None, :]

    grad_packed, part_b_out = pack_out_grad(z, sum(lengths), cot, land3)
    grad_band = exchange(grad_packed)

    taps = over_lanes(own(dw_kernel, 1).astype(F32))
    conv, total, square = conv_forward(z, taps, after(x, grad_packed))
    total, square = lax.psum((total, square), "dp")
    mean = total / pixels
    var = square / pixels - mean * mean
    scale = lax.rsqrt(var + 1e-05)
    own_gain = own(gain)
    chooser = (grid_res[:, None] == jnp.arange(2, dtype=jnp.int32)[None, :]).astype(F32)
    sample_bias = jnp.sum(chooser[0][:, None] * own(res_bias, 1), axis=0)
    affine = over_lanes(jnp.stack([mean, own_gain * scale, own(shift) + sample_bias]))
    packed = pack_normed(z, lengths, conv, affine)

    w_in_p, w_in_t = pad_weight(z, after(w_in, packed[0]))
    w_out_t, w_out_p = pad_weight(z, after(w_out.T, packed[0]))
    b_out_p = jnp.pad(b_out.reshape(groups, chan), ((0, 0), (0, z.pad - chan))).reshape(-1, 1)
    weights = (w_in_t, w_in_p, w_out_p, w_out_t, b_in[:, None], b_out_p)

    normed = [exchange(after(packed[0], grad_band))]
    normed.append(exchange(after(packed[1], normed[0], w_in_t, w_out_p)))
    branch, norm1, active1, hidden1 = mlp(0, part, normed[0], grad_band, *weights, None)
    norm_parts = [exchange(after(norm1, normed[1]))]
    branch, norm2, active2, hidden2 = mlp(1, part, normed[1], grad_band, *weights, branch)
    norm_parts.append(exchange(after(norm2, norm_parts[0])))
    core = lax.axis_index("core")
    mine, sent_out = weight_grad(
        core, [(grad_band, start) for start in starts], [active1, after(active2, norm_parts[0])]
    )
    sum_out = HalvingSum((1, 2), mine, sent_out)
    mine, sent_in = weight_grad(
        core, [(value, 0) for value in normed], [hidden1, after(hidden2, sent_out)]
    )
    sum_in = HalvingSum((2, 1), mine, sent_in)
    branch = exchange(after(branch, norm_parts[1], sent_in))
    sum_out.first()
    sum_in.first()

    part_shift, part_gain = norm_sums(z, norm_parts, conv, over_lanes(jnp.stack([mean, scale])))
    small = jnp.concatenate(
        [part_shift[None], part_gain[None], chooser[0][:, None] * part_shift[None], part_b_out[None]],
        axis=0,
    )
    small = lax.psum(small, "dp")
    terms = over_lanes(
        jnp.stack([mean, scale, own_gain * scale, small[0] / pixels, small[1] / pixels])
    )
    calls = pl.cdiv(chan, GROUP)
    cuts = [0, min(2, calls), min(4, calls), calls]
    cuts = [cut for k, cut in enumerate(cuts) if k == 0 or cut > cuts[k - 1]]
    made = conv_gradient(z, cuts[0], cuts[1], terms, norm_parts, conv, x, ntaps, None)
    sum_out.second(made[1])
    sum_in.second(made[1])
    if len(cuts) > 2:
        made = conv_gradient(
            z, cuts[1], cuts[2], after(terms, sum_out.sent, sum_in.sent), norm_parts, conv, x, ntaps, made
        )
    shares = sum_out.share(made[1]), sum_in.share(made[1])
    if len(cuts) > 3:
        made = conv_gradient(
            z, cuts[2], cuts[3], after(terms, *shares), norm_parts, conv, x, ntaps, made
        )
    conv_grad, products = made
    shares = lax.psum(shares, "pair")
    g_kernel = dp_sum(jnp.sum(products, axis=2)[:, :chan])
    x_grad = conv_backward(z, taps, conv_grad, cot, land3)
    sum_out.back_first(after(shares[0], x_grad))
    sum_in.back_first(after(shares[1], x_grad))
    mixed = mix_branch(z, branch, after(x, sum_out.own, sum_in.own), land3)
    sum_out.back_second(mixed)
    sum_in.back_second(mixed)
    rows = jnp.concatenate([after(g_kernel, x_grad, sum_out.own, sum_in.own), small], axis=0)
    gathered = lax.all_gather(rows, CHAN)
    placed = jnp.transpose(gathered, (1, 0, 2)).reshape(rows.shape[0], width)
    g_w_out_t, _ = sum_out.finish(z, placed)
    g_w_in, pieces = sum_in.finish(z, placed)

    return (
        jnp.transpose(mixed, (0, 2, 1))[None],
        jnp.transpose(x_grad, (0, 2, 1))[None],
        placed[:ntaps],
        placed[ntaps + 1],
        placed[ntaps],
        placed[ntaps + 2 : ntaps + 4],
        g_w_in,
        sum_in.first_row(pieces, chan),
        g_w_out_t.T,
        placed[ntaps + 4],
    )


def solution(mesh):
    shape = mesh.shape
    mesh = jax.sharding.Mesh(
        mesh.devices.reshape(shape["dp"], shape["chan"] // CORES, CORES), ("dp",) + CHAN
    )
    cells = P("dp", None, None, CHAN)
    return jax.shard_map(
        per_device,
        mesh=mesh,
        in_specs=(cells, cells, P("dp", None, None), P("dp")) + (P(),) * 8,
        out_specs=(cells, cells) + (P(),) * 8,
        check_vma=False,
    )
```

```python
from functools import partial
import math

import jax
import jax.numpy as jnp
from jax import lax
from jax.experimental import pallas as pl
from jax.experimental.pallas import tpu as pltpu
from jax.sharding import PartitionSpec as P

LANES = 128
SUBL = 8
VMEM_LIMIT = 56 * 1024 * 1024
CHAN = ("pair", "core")
CORES = 2
F32 = jnp.float32
BF16 = jnp.bfloat16


def round_up(value, step):
    return (value + step - 1) // step * step


def block_of(total, most):
    return max(size for size in range(1, most + 1) if total % size == 0)


class Sizes:
    def __init__(self, chan, height, width, bands, taps):
        self.chan, self.height, self.width, self.bands = chan, height, width, bands
        self.side = math.isqrt(taps)
        self.margin = self.side // 2
        self.rows = height // bands
        self.wide = round_up(width + 2 * self.margin, LANES)
        self.tiles = self.wide // LANES
        self.tail = width - (self.tiles - 1) * LANES
        self.pad = round_up(chan + 1, SUBL)
        self.packed_rows = bands * self.pad
        self.tail_units = round_up(self.rows * self.tail, LANES) // LANES
        self.units = self.rows * (self.tiles - 1) + self.tail_units


def params(semantics=("arbitrary",)):
    return pltpu.CompilerParams(dimension_semantics=semantics, vmem_limit_bytes=VMEM_LIMIT)


def roll_tiles(z, tiles, shift):
    jump, low = divmod(shift % z.wide, LANES)
    count = z.tiles
    if low == 0:
        return [tiles[(j - jump) % count] for j in range(count)]
    lane = lax.broadcasted_iota(jnp.int32, tiles[0].shape, 1)
    moved = [pltpu.roll(tile, low, 1) for tile in tiles]
    return [
        jnp.where(lane < low, moved[(j - jump - 1) % count], moved[(j - jump) % count])
        for j in range(count)
    ]


def wrap_tiles(z, tiles):
    last = tiles[-1]
    lane = lax.broadcasted_iota(jnp.int32, last.shape, 1)
    ahead = pltpu.roll(tiles[0], z.tail, 1)
    behind = pltpu.roll(last, LANES - z.tail, 1)
    last = jnp.where(lane < z.tail, last, jnp.where(lane < z.tail + z.margin, ahead, behind))
    return tiles[:-1] + [last]


def row_tiles(z, value):
    tiles = [value[:, LANES * j : LANES * (j + 1)] for j in range(z.tiles - 1)]
    tail = value[:, LANES * (z.tiles - 1) :]
    zeros = jnp.zeros((value.shape[0], LANES - z.tail), F32)
    return tiles + [jnp.concatenate([tail, zeros], axis=1)]


def pack_tails(z, tails):
    lane = lax.broadcasted_iota(jnp.int32, tails[0].shape, 1)
    tiles = []
    for t in range(z.tail_units):
        begin, tile = LANES * t, None
        for row, tail in enumerate(tails):
            low = z.tail * row - begin
            if low >= LANES or low + z.tail <= 0:
                continue
            moved = pltpu.roll(tail, low % LANES, 1) if low % LANES else tail
            tile = moved if tile is None else jnp.where(lane >= low, moved, tile)
        end = z.tail * z.rows - begin
        tiles.append(jnp.where(lane < end, tile, 0.0) if end < LANES else tile)
    return tiles


def unpack_tails(z, tiles):
    lane = lax.broadcasted_iota(jnp.int32, tiles[0].shape, 1)
    tails = []
    for row in range(z.rows):
        t, low = divmod(z.tail * row, LANES)
        tail = pltpu.roll(tiles[t], LANES - low, 1) if low else tiles[t]
        if LANES - low < z.tail:
            tail = jnp.where(lane < LANES - low, tail, pltpu.roll(tiles[t + 1], LANES - low, 1))
        tails.append(jnp.where(lane < z.tail, tail, 0.0))
    return tails


def pack_rows(z, rows):
    full = z.tiles - 1
    return [row[j] for row in rows for j in range(full)] + pack_tails(z, [row[full] for row in rows])


def unpack_rows(z, tiles):
    full = z.tiles - 1
    tails = unpack_tails(z, tiles[z.rows * full :])
    return [tiles[row * full : (row + 1) * full] + [tails[row]] for row in range(z.rows)]


def packed_tiles(refs, read):
    return [
        read(ref, slice(LANES * k, LANES * (k + 1)))
        for ref in refs
        for k in range(ref.shape[-1] // LANES)
    ]


def whole(shape):
    return pl.BlockSpec(shape, lambda *_: (0,) * len(shape))


def smem():
    return pl.BlockSpec(memory_space=pltpu.SMEM)


def cost(bytes_accessed, flops=10**7):
    return pl.CostEstimate(flops=flops, bytes_accessed=bytes_accessed, transcendentals=0)


PAIR = 2
GROUP = 16


def pair_rows(z):
    return pl.BlockSpec((PAIR * z.rows, z.pad, z.width), lambda g: (g, 0, 0))


def pair_wide(z):
    return pl.BlockSpec((PAIR * z.rows, z.pad, z.wide), lambda g: (g, 0, 0))


def pair_land(z):
    return pl.BlockSpec((PAIR * z.rows, 1, z.width), lambda g: (g, 0, 0))


def pair_packed(z, cells):
    return pl.BlockSpec((PAIR * z.pad, cells), lambda g: (g, 0))


def group_rows(z):
    return pl.BlockSpec((z.height, GROUP, z.width), lambda c: (0, c, 0))


def group_wide(z):
    return pl.BlockSpec((z.height, GROUP, z.wide), lambda c: (0, c, 0))


def group_lanes(count):
    return pl.BlockSpec((count, GROUP, LANES), lambda c: (0, c, 0))


def write_pair(z, refs, bands):
    tiles = [jnp.concatenate(both, axis=0).astype(BF16) for both in zip(*bands)]
    unit = 0
    for ref in refs:
        for k in range(ref.shape[1] // LANES):
            ref[:, LANES * k : LANES * (k + 1)] = tiles[unit]
            unit += 1


def pack_out_grad(z, cells, cot, land):
    def kernel(cot_ref, land_ref, out_ref, sum_ref):
        @pl.when(pl.program_id(0) == 0)
        def _():
            sum_ref[...] = jnp.zeros_like(sum_ref)

        channel = lax.broadcasted_iota(jnp.int32, (z.pad, z.width), 0)
        total = jnp.zeros((z.pad, LANES), F32)
        bands = []
        for band in range(PAIR):
            rows = []
            for row in range(z.rows * band, z.rows * (band + 1)):
                value = cot_ref[row].astype(F32) * land_ref[row].astype(F32)
                rows.append(row_tiles(z, jnp.where(channel < z.chan, value, 0.0)))
                total = total + sum(rows[-1])
            bands.append(pack_rows(z, rows))
        sum_ref[...] += total
        write_pair(z, [out_ref], bands)

    out, sums = pl.pallas_call(
        kernel,
        grid=(z.bands // PAIR,),
        in_specs=[pair_rows(z), pair_land(z)],
        out_specs=[pair_packed(z, cells), whole((z.pad, LANES))],
        out_shape=[
            jax.ShapeDtypeStruct((z.packed_rows, cells), BF16),
            jax.ShapeDtypeStruct((z.pad, LANES), F32),
        ],
        compiler_params=params(),
        cost_estimate=cost(8 * 10**6),
    )(cot, land)
    return out, jnp.sum(sums, axis=1)[: z.chan]


def fill_rows(z, target, read, wrap):
    zeros = jnp.zeros(target.shape[1:], F32)
    for k in range(z.margin):
        target[k] = zeros
        target[z.margin + z.height + k] = zeros

    def body(h, carry):
        tiles = row_tiles(z, read(h))
        if wrap:
            tiles = wrap_tiles(z, tiles)
        for j, tile in enumerate(tiles):
            target[z.margin + h, :, LANES * j : LANES * (j + 1)] = tile
        return carry

    lax.fori_loop(0, z.height, body, 0, unroll=8)


def convolve(z, steps, at, taps_ref, source, flip, put, carry):
    span = steps + 2 * z.margin

    def body(block, carry):
        h0 = block * steps
        rows = [
            [source[h0 + m, at, LANES * j : LANES * (j + 1)] for j in range(z.tiles)]
            for m in range(span)
        ]
        sums = [None] * steps
        for b in range(z.side):
            weights = [taps_ref[z.side * a + b, at, :] for a in range(z.side)]
            for r in range(steps):
                part = None
                for a in range(z.side):
                    row = rows[r + 2 * z.margin - a] if flip else rows[r + a]
                    terms = [weights[a] * tile for tile in row]
                    part = terms if part is None else [p + t for p, t in zip(part, terms)]
                part = roll_tiles(z, part, b - z.margin if flip else z.margin - b)
                sums[r] = part if b == 0 else [s + p for s, p in zip(sums[r], part)]
        for r in range(steps):
            carry = put(h0 + r, sums[r], carry)
        return carry

    return lax.fori_loop(0, z.height // steps, body, carry, unroll=2)


def conv_forward(z, taps, x):
    def kernel(taps_ref, x_ref, conv_ref, sum_ref, square_ref, source):
        fill_rows(z, source, lambda h: x_ref[h].astype(F32), True)
        lane = lax.broadcasted_iota(jnp.int32, (SUBL, LANES), 1)
        for part in range(GROUP // SUBL):
            at = slice(SUBL * part, SUBL * (part + 1))

            def put(h, tiles, carry):
                for j, tile in enumerate(tiles):
                    conv_ref[h, at, LANES * j : LANES * (j + 1)] = tile
                tiles = tiles[:-1] + [jnp.where(lane < z.tail, tiles[-1], 0.0)]
                return carry[0] + sum(tiles), carry[1] + sum(t * t for t in tiles)

            @pl.when(pl.program_id(0) * GROUP + SUBL * part < z.chan)
            def _():
                zero = jnp.zeros((SUBL, LANES), F32)
                total, square = convolve(z, 4, at, taps_ref, source, False, put, (zero, zero))
                sum_ref[at, :] = total
                square_ref[at, :] = square

    lane_spec = pl.BlockSpec((GROUP, LANES), lambda c: (c, 0))
    lane_shape = jax.ShapeDtypeStruct((z.pad, LANES), F32)
    conv, total, square = pl.pallas_call(
        kernel,
        grid=(pl.cdiv(z.chan, GROUP),),
        in_specs=[group_lanes(taps.shape[0]), group_rows(z)],
        out_specs=[group_wide(z), lane_spec, lane_spec],
        out_shape=[
            jax.ShapeDtypeStruct((z.height, z.pad, z.wide), F32), lane_shape, lane_shape,
        ],
        scratch_shapes=[pltpu.VMEM((z.height + 2 * z.margin, GROUP, z.wide), F32)],
        compiler_params=params(),
        cost_estimate=cost(16 * 10**6, 10**10),
    )(taps, x)
    return conv, jnp.sum(total, axis=1)[: z.chan], jnp.sum(square, axis=1)[: z.chan]


def pack_normed(z, lengths, conv, columns):
    def kernel(columns_ref, conv_ref, *outs):
        channel = lax.broadcasted_iota(jnp.int32, (z.pad, LANES), 0)
        filler = jnp.where(channel == z.chan, 1.0, 0.0)
        mean, factor, offset = columns_ref[0], columns_ref[1], columns_ref[2]
        bands = []
        for band in range(PAIR):
            rows = []
            for row in range(z.rows * band, z.rows * (band + 1)):
                tiles = [conv_ref[row, :, LANES * j : LANES * (j + 1)] for j in range(z.tiles)]
                rows.append(
                    [
                        jnp.where(channel < z.chan, (tile - mean) * factor + offset, filler)
                        for tile in tiles
                    ]
                )
            bands.append(pack_rows(z, rows))
        write_pair(z, outs, bands)

    return pl.pallas_call(
        kernel,
        grid=(z.bands // PAIR,),
        in_specs=[whole(columns.shape), pair_wide(z)],
        out_specs=[pair_packed(z, n) for n in lengths],
        out_shape=[jax.ShapeDtypeStruct((z.packed_rows, n), BF16) for n in lengths],
        compiler_params=params(),
        cost_estimate=cost(12 * 10**6),
    )(columns, conv)


def norm_sums(z, parts, conv, columns):
    count = len(parts)

    def kernel(columns_ref, conv_ref, *rest):
        ins, (shift_ref, gain_ref) = rest[:count], rest[count:]

        @pl.when(pl.program_id(0) == 0)
        def _():
            shift_ref[...] = jnp.zeros_like(shift_ref)
            gain_ref[...] = jnp.zeros_like(gain_ref)

        mean = columns_ref[0]
        tiles = packed_tiles(ins, lambda ref, lanes: ref[:, lanes].astype(F32))
        shift = jnp.zeros((z.pad, LANES), F32)
        gain = jnp.zeros((z.pad, LANES), F32)
        for band in range(PAIR):
            rows = unpack_rows(z, [tile[z.pad * band : z.pad * (band + 1)] for tile in tiles])
            for row, grads in enumerate(rows):
                for j, grad in enumerate(grads):
                    value = conv_ref[z.rows * band + row, :, LANES * j : LANES * (j + 1)]
                    shift = shift + grad
                    gain = gain + grad * (value - mean)
        shift_ref[...] += shift
        gain_ref[...] += gain * columns_ref[1]

    lane_shape = jax.ShapeDtypeStruct((z.pad, LANES), F32)
    shift, gain = pl.pallas_call(
        kernel,
        grid=(z.bands // PAIR,),
        in_specs=[whole(columns.shape), pair_wide(z)] + [pair_packed(z, p.shape[1]) for p in parts],
        out_specs=[whole((z.pad, LANES))] * 2,
        out_shape=[lane_shape, lane_shape],
        compiler_params=params(),
        cost_estimate=cost(12 * 10**6),
    )(columns, conv, *parts)
    return jnp.sum(shift, axis=1)[: z.chan], jnp.sum(gain, axis=1)[: z.chan]


def conv_gradient(z, begin, end, columns, parts, conv, x, ntaps, before):
    count = len(parts)
    parts = [part.reshape(z.bands, z.pad, part.shape[1]) for part in parts]
    steps = 4
    before = [] if before is None else list(before)

    def kernel(columns_ref, conv_ref, x_ref, *rest):
        ins, (grad_ref, product_ref, grads, source) = rest[:count], rest[-4:]
        mean, scale, factor, shift, gain = (columns_ref[k] for k in range(5))

        def band_body(band, carry):
            tiles = packed_tiles(ins, lambda ref, lanes: ref[band, :, lanes].astype(F32))
            for row, values in enumerate(unpack_rows(z, tiles)):
                h = band * z.rows + row
                made = []
                for j, value in enumerate(values):
                    centred = (conv_ref[h, :, LANES * j : LANES * (j + 1)] - mean) * scale
                    made.append(factor * (value - (shift + centred * gain)))
                for j, tile in enumerate(wrap_tiles(z, made)):
                    at = slice(LANES * j, LANES * (j + 1))
                    grads[h, :, at] = tile
                    grad_ref[h, :, at] = tile.astype(BF16)
            return carry

        lax.fori_loop(0, z.bands, band_body, 0)
        fill_rows(z, source, lambda h: x_ref[h].astype(F32), False)
        for part in range(GROUP // SUBL):
            at = slice(SUBL * part, SUBL * (part + 1))

            @pl.when((begin + pl.program_id(0)) * GROUP + SUBL * part < z.chan)
            def _():
                for b in range(z.side):

                    def body(block, totals):
                        h0 = block * steps
                        rows = [
                            [source[h0 + m, at, LANES * j : LANES * (j + 1)] for j in range(z.tiles)]
                            for m in range(steps + 2 * z.margin)
                        ]
                        totals = list(totals)
                        for r in range(steps):
                            moved = roll_tiles(
                                z,
                                [grads[h0 + r, at, LANES * j : LANES * (j + 1)] for j in range(z.tiles)],
                                b - z.margin,
                            )
                            for a in range(z.side):
                                for m, tile in zip(moved, rows[r + a]):
                                    totals[a] = totals[a] + m * tile
                        return tuple(totals)

                    zero = jnp.zeros((SUBL, LANES), F32)
                    totals = lax.fori_loop(0, z.height // steps, body, (zero,) * z.side, unroll=4)
                    for a in range(z.side):
                        product_ref[z.side * a + b, at, :] = totals[a]

    def group(shape):
        return pl.BlockSpec(shape, lambda c: (0, begin + c, 0))

    operands = [columns, conv, x, *parts, *before]
    return pl.pallas_call(
        kernel,
        grid=(end - begin,),
        in_specs=[
            group((5, GROUP, LANES)), group((z.height, GROUP, z.wide)),
            group((z.height, GROUP, z.width)),
        ]
        + [group((z.bands, GROUP, p.shape[2])) for p in parts]
        + [pl.BlockSpec(memory_space=pl.ANY)] * len(before),
        out_specs=[group((z.height, GROUP, z.wide)), group((ntaps, GROUP, LANES))],
        out_shape=[
            jax.ShapeDtypeStruct((z.height, z.pad, z.wide), BF16),
            jax.ShapeDtypeStruct((ntaps, z.pad, LANES), F32),
        ],
        scratch_shapes=[
            pltpu.VMEM((z.height, GROUP, z.wide), F32),
            pltpu.VMEM((z.height + 2 * z.margin, GROUP, z.wide), F32),
        ],
        input_output_aliases={len(operands) - 2 + k: k for k in range(len(before))},
        compiler_params=params(),
        cost_estimate=cost(10 * 10**6, 4 * 10**9),
    )(*operands)


def conv_backward(z, taps, grad, cot, land):
    def kernel(taps_ref, grad_ref, cot_ref, land_ref, out_ref, source, result):
        zeros = jnp.zeros(source.shape[1:], F32)
        for k in range(z.margin):
            source[k] = zeros
            source[z.margin + z.height + k] = zeros

        def fill(h, carry):
            source[z.margin + h] = grad_ref[h].astype(F32)
            return carry

        lax.fori_loop(0, z.height, fill, 0, unroll=8)
        for part in range(GROUP // SUBL):
            at = slice(SUBL * part, SUBL * (part + 1))

            def put(h, tiles, carry):
                for j, tile in enumerate(tiles):
                    result[h, at, LANES * j : LANES * (j + 1)] = tile
                return carry

            @pl.when(pl.program_id(0) * GROUP + SUBL * part < z.chan)
            def _():
                convolve(z, 4, at, taps_ref, source, True, put, 0)

        def finish(h, carry):
            direct = cot_ref[h].astype(F32) * land_ref[h].astype(F32)
            out_ref[h] = (direct + result[h][:, : z.width]).astype(BF16)
            return carry

        lax.fori_loop(0, z.height, finish, 0, unroll=8)

    return pl.pallas_call(
        kernel,
        grid=(pl.cdiv(z.chan, GROUP),),
        in_specs=[
            group_lanes(taps.shape[0]), group_wide(z), group_rows(z),
            whole((z.height, 1, z.width)),
        ],
        out_specs=group_rows(z),
        out_shape=jax.ShapeDtypeStruct((z.height, z.chan, z.width), BF16),
        scratch_shapes=[
            pltpu.VMEM((z.height + 2 * z.margin, GROUP, z.wide), F32),
            pltpu.VMEM((z.height, GROUP, z.wide), F32),
        ],
        compiler_params=params(),
        cost_estimate=cost(16 * 10**6, 10**10),
    )(taps, grad, cot, land)


def mix_branch(z, branch, x, land):
    def kernel(x_ref, land_ref, branch_ref, out_ref):
        tiles = packed_tiles([branch_ref], lambda ref, lanes: ref[:, lanes].astype(F32))
        for band in range(PAIR):
            rows = unpack_rows(z, [tile[z.pad * band : z.pad * (band + 1)] for tile in tiles])
            for k, row in enumerate(rows):
                h = z.rows * band + k
                value = jnp.concatenate(row, axis=1)[:, : z.width]
                value = land_ref[h].astype(F32) * (x_ref[h].astype(F32) + value)
                out_ref[h] = value.astype(BF16)

    return pl.pallas_call(
        kernel,
        grid=(z.bands // PAIR,),
        in_specs=[pair_rows(z), pair_land(z), pair_packed(z, branch.shape[1])],
        out_specs=pair_rows(z),
        out_shape=jax.ShapeDtypeStruct((z.height, z.chan, z.width), BF16),
        compiler_params=params(),
        cost_estimate=cost(12 * 10**6),
    )(x, land, branch)


def gelu_parts(h):
    span = 1.0 + (0.3275911 * math.sqrt(0.5)) * jnp.abs(h)
    t = pl.reciprocal(span, approx=True)
    t = t * (2.0 - span * t)
    bell = jnp.exp2((-0.5 / math.log(2.0)) * (h * h))
    poly = t * (
        0.5 * 0.254829592
        + t
        * (
            0.5 * -0.284496736
            + t * (0.5 * 1.421413741 + t * (0.5 * -1.453152027 + t * (0.5 * 1.061405429)))
        )
    )
    tail = poly * bell
    phi = jnp.where(h >= 0, 1.0 - tail, tail)
    return h * phi, phi + h * ((1.0 / math.sqrt(2.0 * math.pi)) * bell)


def pad_weight(z, matrix):
    groups, hidden = matrix.shape[0] // z.chan, matrix.shape[1]
    block = block_of(hidden, 640)
    rows = groups * z.pad

    def kernel(in_ref, out_ref, transposed_ref, wide):
        value = in_ref[...].astype(F32)
        zeros = jnp.zeros((z.pad - z.chan, block), F32)
        for k in range(groups):
            wide[z.pad * k : z.pad * (k + 1), :] = jnp.concatenate(
                [value[z.chan * k : z.chan * (k + 1), :], zeros], axis=0
            )
        padded = wide[...]
        out_ref[...] = padded.astype(BF16)
        transposed_ref[...] = padded.T.astype(BF16)

    return pl.pallas_call(
        kernel,
        grid=(hidden // block,),
        in_specs=[pl.BlockSpec((groups * z.chan, block), lambda f: (0, f))],
        out_specs=[
            pl.BlockSpec((rows, block), lambda f: (0, f)),
            pl.BlockSpec((block, rows), lambda f: (f, 0)),
        ],
        out_shape=[
            jax.ShapeDtypeStruct((rows, hidden), BF16),
            jax.ShapeDtypeStruct((hidden, rows), BF16),
        ],
        scratch_shapes=[pltpu.VMEM((rows, block), F32)],
        compiler_params=params(),
        cost_estimate=cost(16 * 10**6),
    )(matrix)


def lane_block(rows, cells, part):
    return pl.BlockSpec((rows, cells), lambda *_: (0, part))


def row_step(rows, most):
    return max(n for n in range(16, most + 1, 16) if rows % n == 0)


def mlp(part, length, normed, out_grad, w_in_t, w_in, w_out, w_out_t, b_in, b_out, branch_all):
    packed, cells = normed.shape
    hidden = w_in_t.shape[0]
    block = block_of(hidden, 640)
    slices = 4
    inner, rows = block // slices, packed // slices
    blocks = hidden // block

    def kernel(
        n_ref, g_ref, w_in_t_ref, w_in_ref, w_out_ref, w_out_t_ref, b_in_ref, b_out_ref, *rest
    ):
        (
            branch_ref, norm_ref, active_out, hidden_out,
            h_0, h_1, back_0, back_1, active, grads, branch_acc, norm_acc, sems,
        ) = rest[-13:]
        step = pl.program_id(0)
        buffers = ((h_0, back_0), (h_1, back_1))

        def products_in(q, h, back):
            at = pl.ds(pl.multiple_of(q * inner, inner), inner)
            h[...] = (
                jnp.dot(w_in_t_ref[at, :], n_ref[...], preferred_element_type=F32) + b_in_ref[at, :]
            )
            back[...] = jnp.dot(w_out_ref[at, :], g_ref[:, :cells], preferred_element_type=F32)

        def gelu(k, h, back):
            at = pl.ds(pl.multiple_of(jnp.maximum(k, 0) * inner, inner), inner)
            value, slope = gelu_parts(h[...])
            active[at, :] = value.astype(BF16)
            grads[at, :] = (back[...] * slope).astype(BF16)

        def products_out(q):
            at = pl.ds(pl.multiple_of(q * rows, rows), rows)
            block_at = pl.ds(pl.multiple_of((step - 2) * block, block), block)
            branch_acc[at, :] += jnp.dot(
                w_out_t_ref[at, :], active[block_at, :], preferred_element_type=F32
            )
            norm_acc[at, :] += jnp.dot(
                w_in_ref[at, :], grads[block_at, :], preferred_element_type=F32
            )

        def loop(enter, leave):
            def body(i, carry):
                for turn in range(2):
                    q = 2 * i + turn
                    if leave:
                        products_out(q)
                    if enter:
                        products_in(q, *buffers[turn])
                        gelu(step * slices + q - 1, *buffers[1 - turn])
                return carry

            lax.fori_loop(0, slices // 2, body, 0)

        @pl.when(step == 0)
        def _():
            branch_acc[...] = jnp.broadcast_to(b_out_ref[...], branch_acc.shape)
            norm_acc[...] = jnp.zeros_like(norm_acc)

        copies = [
            pltpu.make_async_copy(active, active_out, sems.at[0]),
            pltpu.make_async_copy(grads, hidden_out, sems.at[1]),
        ]
        pl.when(step < 2)(lambda: loop(True, False))
        pl.when((step >= 2) & (step < blocks))(lambda: loop(True, True))

        @pl.when(step == blocks)
        def _():
            gelu(slices * blocks - 1, *buffers[1])
            for copy in copies:
                copy.start()

        pl.when(step >= blocks)(lambda: loop(False, True))

        @pl.when(step == blocks + 1)
        def _():
            branch_ref[:, :cells] = branch_acc[...].astype(BF16)
            norm_ref[...] = norm_acc[...].astype(BF16)
            for copy in copies:
                copy.wait()

    def at_in(f):
        return jnp.minimum(f, blocks - 1)

    def at_out(f):
        return jnp.maximum(f - 2, 0)

    tall_block = pl.BlockSpec((block, packed), lambda f: (at_in(f), 0))
    wide_block = pl.BlockSpec((packed, block), lambda f: (0, at_out(f)))
    anywhere = pl.BlockSpec(memory_space=pl.ANY)
    operands = [normed, out_grad, w_in_t, w_in, w_out, w_out_t, b_in, b_out]
    in_specs = [
        whole((packed, cells)), lane_block(packed, length, part),
        tall_block, wide_block, tall_block, wide_block,
        pl.BlockSpec((block, 1), lambda f: (at_in(f), 0)), whole((packed, 1)),
    ]
    aliases = {}
    if branch_all is not None:
        aliases = {len(operands): 0}
        operands.append(branch_all)
        in_specs.append(anywhere)
    return pl.pallas_call(
        kernel,
        grid=(blocks + 2,),
        in_specs=in_specs,
        out_specs=[lane_block(packed, length, part), whole((packed, cells)), anywhere, anywhere],
        out_shape=[
            jax.ShapeDtypeStruct(out_grad.shape, BF16),
            jax.ShapeDtypeStruct((packed, cells), BF16),
            jax.ShapeDtypeStruct((hidden, cells), BF16),
            jax.ShapeDtypeStruct((hidden, cells), BF16),
        ],
        scratch_shapes=[pltpu.VMEM((inner, cells), F32)] * 4
        + [pltpu.VMEM((hidden, cells), BF16)] * 2
        + [pltpu.VMEM((packed, cells), F32)] * 2
        + [pltpu.SemaphoreType.DMA((2,))],
        input_output_aliases=aliases,
        compiler_params=params(),
        cost_estimate=pl.CostEstimate(
            flops=8 * packed * cells * hidden, bytes_accessed=4 * 10**7, transcendentals=cells * hidden
        ),
    )(*operands)


def weight_grad(core, lefts, rights):
    rows, hidden = lefts[0][0].shape[0], rights[0].shape[0]
    half = rows // CORES
    block = block_of(hidden, 640)
    arrays = []
    for array, _ in lefts:
        if not any(array is known for known in arrays):
            arrays.append(array)
    which = [next(k for k, known in enumerate(arrays) if known is array) for array, _ in lefts]

    def kernel(core_ref, *refs):
        mine_ref, sent_ref, both = refs[-3:]
        total = None
        for k, (_, start), right in zip(which, lefts, refs[len(arrays) : -3]):
            part = lax.dot_general(
                refs[k][:, start : start + right.shape[1]], right[...],
                (((1,), (1,)), ((), ())), preferred_element_type=F32,
            )
            total = part if total is None else total + part
        both[0] = total[:half].astype(BF16)
        both[1] = total[half:].astype(BF16)
        mine_ref[...] = both[core_ref[0]]
        sent_ref[...] = both[1 - core_ref[0]]

    cells = sum(right.shape[1] for right in rights)
    out = jax.ShapeDtypeStruct((half, hidden), BF16)
    return pl.pallas_call(
        kernel,
        grid=(hidden // block,),
        in_specs=[smem()] + [whole(array.shape) for array in arrays]
        + [pl.BlockSpec((block, right.shape[1]), lambda f: (f, 0)) for right in rights],
        out_specs=[pl.BlockSpec((half, block), lambda f: (0, f))] * 2,
        out_shape=[out, out],
        scratch_shapes=[pltpu.VMEM((CORES, half, block), BF16)],
        compiler_params=params(),
        cost_estimate=cost(24 * 10**6, 2 * rows * cells * hidden),
    )(core[None], *arrays, *rights)


def unpad_rows(z, place, pieces):
    groups, hidden = pieces[0].shape[0] // z.pad, pieces[0].shape[1]

    def kernel(place_ref, *refs):
        out_ref = refs[-1]

        def put(ref):
            value = ref[...].astype(F32)
            for k in range(groups):
                out_ref[z.chan * k : z.chan * (k + 1), :] = value[z.pad * k : z.pad * k + z.chan, :]

        wanted = jnp.bitwise_xor(pl.program_id(0), place_ref[0])
        for k, ref in enumerate(refs[:-1]):
            pl.when(wanted == k)(partial(put, ref))

    return pl.pallas_call(
        kernel,
        grid=(4,),
        in_specs=[smem()] + [whole(pieces[0].shape)] * 4,
        out_specs=pl.BlockSpec((groups * z.chan, hidden), lambda q: (q, 0)),
        out_shape=jax.ShapeDtypeStruct((4 * groups * z.chan, hidden), F32),
        compiler_params=params(),
        cost_estimate=cost(16 * 10**6),
    )(place[None], *pieces)


def exchange(value):
    return lax.all_to_all(value, CHAN, split_axis=0, concat_axis=0, tiled=True)


def after(value, *others):
    return lax.optimization_barrier((value, *others))[0]


def dp_sum(value):
    ways = lax.axis_size("dp")
    total = value
    for turn in range(1, ways):
        total = total + lax.ppermute(value, "dp", [(i, i ^ turn) for i in range(ways)])
    return total


def swap_cores(value):
    return lax.ppermute(value, "core", [(0, 1), (1, 0)])


class HalvingSum:
    def __init__(self, turns, mine, sent):
        place = lax.axis_index("dp")
        self.turns = turns
        self.bits = [jnp.bitwise_and(place // turn, 1) for turn in turns]
        self.core = lax.axis_index("core")
        self.mine, self.other = mine, swap_cores(sent)

    def meet(self, value, turn):
        ways = lax.axis_size("dp")
        return lax.ppermute(value, "dp", [(i, i ^ turn) for i in range(ways)])

    def pair(self, half):
        rows = self.mine.shape[0] // 2
        at = half * rows
        return lax.dynamic_slice_in_dim(self.mine, at, rows, 0).astype(
            F32
        ) + lax.dynamic_slice_in_dim(self.other, at, rows, 0).astype(F32)

    def first(self, ready):
        self.mine = after(self.mine, ready)
        self.arrived = self.meet(self.pair(1 - self.bits[0]).astype(BF16), self.turns[0])

    def second(self, ready):
        arrived = after(self.arrived, ready)
        total = self.pair(self.bits[0]) + arrived.astype(F32)
        rows = total.shape[0] // 2
        send = lax.dynamic_slice_in_dim(total, (1 - self.bits[1]) * rows, rows, 0).astype(BF16)
        self.kept = lax.dynamic_slice_in_dim(total, self.bits[1] * rows, rows, 0)
        self.sent = send
        self.arrived = self.meet(send, self.turns[1])

    def share(self, ready):
        return (self.kept + after(self.arrived, ready).astype(F32)).astype(BF16)

    def back_first(self, share):
        self.own = share
        self.arrived = self.meet(share, self.turns[1])

    def back_second(self, ready):
        other = after(self.arrived, ready)
        low = self.bits[1] == 0
        self.own = jnp.concatenate(
            [jnp.where(low, self.own, other), jnp.where(low, other, self.own)], axis=0
        )
        self.arrived = self.meet(self.own, self.turns[0])
        self.swapped = swap_cores(self.own)

    def finish(self, z, ready):
        other = after(self.arrived, ready)
        pieces = [self.own, other, self.swapped, swap_cores(other)]
        return unpad_rows(z, self.core * 2 + self.bits[0], pieces), pieces

    def first_row(self, pieces, row):
        place = self.core * 2 + self.bits[0]
        found = pieces[0][row]
        for k in range(1, 4):
            found = jnp.where(place == k, pieces[k][row], found)
        return found.astype(F32)


def per_device(
    x_in, cotangent, land, grid_res, dw_kernel, gain, shift, res_bias, w_in, b_in, w_out, b_out
):
    samples, height, columns, chan = x_in.shape
    groups = lax.axis_size("pair") * CORES
    first = (lax.axis_index("pair") * CORES + lax.axis_index("core")) * chan
    width = chan * groups
    ntaps = dw_kernel.shape[0]
    z = Sizes(chan, height, columns, groups, ntaps)
    pixels = float(samples * lax.axis_size("dp") * height * columns)
    part = (z.units + 1) // 2 * LANES
    lengths = [part, z.units * LANES - part]
    starts = [0, part]

    def own(values, axis=0):
        return lax.dynamic_slice_in_dim(values, first, chan, axis)

    def over_lanes(rows):
        rows = jnp.pad(rows, ((0, 0), (0, z.pad - chan)))
        return jnp.broadcast_to(rows[:, :, None], rows.shape + (LANES,))

    x = jnp.transpose(x_in[0], (0, 2, 1))
    cot = jnp.transpose(cotangent[0], (0, 2, 1))
    land3 = land[0][:, None, :]

    grad_packed, part_b_out = pack_out_grad(z, sum(lengths), cot, land3)
    grad_band = exchange(grad_packed)

    taps = over_lanes(own(dw_kernel, 1).astype(F32))
    conv, total, square = conv_forward(z, taps, after(x, grad_packed))
    total, square = lax.psum((total, square), "dp")
    mean = total / pixels
    var = square / pixels - mean * mean
    scale = lax.rsqrt(var + 1e-05)
    own_gain = own(gain)
    chooser = (grid_res[:, None] == jnp.arange(2, dtype=jnp.int32)[None, :]).astype(F32)
    sample_bias = jnp.sum(chooser[0][:, None] * own(res_bias, 1), axis=0)
    affine = over_lanes(jnp.stack([mean, own_gain * scale, own(shift) + sample_bias]))
    packed = pack_normed(z, lengths, conv, affine)

    w_in_p, w_in_t = pad_weight(z, after(w_in, packed[0]))
    w_out_t, w_out_p = pad_weight(z, after(w_out.T, packed[0]))
    b_out_p = jnp.pad(b_out.reshape(groups, chan), ((0, 0), (0, z.pad - chan))).reshape(-1, 1)
    weights = (w_in_t, w_in_p, w_out_p, w_out_t, b_in[:, None], b_out_p)

    normed = [exchange(after(packed[0], grad_band))]
    normed.append(exchange(after(packed[1], normed[0], w_in_t, w_out_p)))
    branch, norm1, active1, hidden1 = mlp(0, part, normed[0], grad_band, *weights, None)
    norm_parts = [exchange(after(norm1, normed[1]))]
    branch, norm2, active2, hidden2 = mlp(1, part, normed[1], grad_band, *weights, branch)
    norm_parts.append(exchange(after(norm2, norm_parts[0])))
    core = lax.axis_index("core")
    mine, sent_out = weight_grad(
        core, [(grad_band, start) for start in starts], [active1, after(active2, norm_parts[0])]
    )
    sum_out = HalvingSum((1, 2), mine, sent_out)
    mine, sent_in = weight_grad(
        core, [(value, 0) for value in normed], [hidden1, after(hidden2, sent_out)]
    )
    sum_in = HalvingSum((2, 1), mine, sent_in)
    branch = exchange(after(branch, norm_parts[1], sent_in))
    sum_out.first(norm_parts[1])
    sum_in.first(norm_parts[1])

    part_shift, part_gain = norm_sums(z, norm_parts, conv, over_lanes(jnp.stack([mean, scale])))
    small = jnp.concatenate(
        [part_shift[None], part_gain[None], chooser[0][:, None] * part_shift[None], part_b_out[None]],
        axis=0,
    )
    small = lax.psum(small, "dp")
    terms = over_lanes(
        jnp.stack([mean, scale, own_gain * scale, small[0] / pixels, small[1] / pixels])
    )
    calls = pl.cdiv(chan, GROUP)
    cuts = [0, min(2, calls), min(4, calls), calls]
    cuts = [cut for k, cut in enumerate(cuts) if k == 0 or cut > cuts[k - 1]]
    made = conv_gradient(z, cuts[0], cuts[1], terms, norm_parts, conv, x, ntaps, None)
    sum_out.second(made[1])
    sum_in.second(made[1])
    if len(cuts) > 2:
        made = conv_gradient(
            z, cuts[1], cuts[2], after(terms, sum_out.sent, sum_in.sent), norm_parts, conv, x, ntaps, made
        )
    shares = sum_out.share(made[1]), sum_in.share(made[1])
    if len(cuts) > 3:
        made = conv_gradient(
            z, cuts[2], cuts[3], after(terms, *shares), norm_parts, conv, x, ntaps, made
        )
    conv_grad, products = made
    shares = lax.psum(shares, "pair")
    g_kernel = dp_sum(jnp.sum(products, axis=2)[:, :chan])
    x_grad = conv_backward(z, taps, conv_grad, cot, land3)
    sum_out.back_first(after(shares[0], x_grad))
    sum_in.back_first(after(shares[1], x_grad))
    rows = jnp.concatenate([after(g_kernel, sum_out.own, sum_in.own), small], axis=0)
    gathered = lax.all_gather(rows, CHAN)
    placed = jnp.transpose(gathered, (1, 0, 2)).reshape(rows.shape[0], width)
    sum_out.back_second(gathered)
    sum_in.back_second(gathered)
    mixed = mix_branch(z, branch, after(x, sum_out.own, sum_in.own), land3)
    mixed_out = jnp.transpose(mixed, (0, 2, 1))[None]
    x_grad_out = jnp.transpose(after(x_grad, sum_out.own, sum_in.own), (0, 2, 1))[None]
    g_w_out_t, _ = sum_out.finish(z, mixed)
    g_w_in, pieces = sum_in.finish(z, mixed)

    return (
        mixed_out,
        x_grad_out,
        placed[:ntaps],
        placed[ntaps + 1],
        placed[ntaps],
        placed[ntaps + 2 : ntaps + 4],
        g_w_in,
        sum_in.first_row(pieces, chan),
        g_w_out_t.T,
        placed[ntaps + 4],
    )


def solution(mesh):
    shape = mesh.shape
    mesh = jax.sharding.Mesh(
        mesh.devices.reshape(shape["dp"], shape["chan"] // CORES, CORES), ("dp",) + CHAN
    )
    cells = P("dp", None, None, CHAN)
    return jax.shard_map(
        per_device,
        mesh=mesh,
        in_specs=(cells, cells, P("dp", None, None), P("dp")) + (P(),) * 8,
        out_specs=(cells, cells) + (P(),) * 8,
        check_vma=False,
    )
```

```python
from functools import partial
import math

import jax
import jax.numpy as jnp
from jax import lax
from jax.experimental import pallas as pl
from jax.experimental.pallas import tpu as pltpu
from jax.sharding import PartitionSpec as P

LANES = 128
SUBL = 8
VMEM_LIMIT = 56 * 1024 * 1024
CHAN = ("pair", "core")
CORES = 2
F32 = jnp.float32
BF16 = jnp.bfloat16


def round_up(value, step):
    return (value + step - 1) // step * step


def block_of(total, most):
    return max(size for size in range(1, most + 1) if total % size == 0)


class Sizes:
    def __init__(self, chan, height, width, bands, taps):
        self.chan, self.height, self.width, self.bands = chan, height, width, bands
        self.side = math.isqrt(taps)
        self.margin = self.side // 2
        self.rows = height // bands
        self.wide = round_up(width + 2 * self.margin, LANES)
        self.tiles = self.wide // LANES
        self.tail = width - (self.tiles - 1) * LANES
        self.pad = round_up(chan + 1, SUBL)
        self.packed_rows = bands * self.pad
        self.tail_units = round_up(self.rows * self.tail, LANES) // LANES
        self.units = self.rows * (self.tiles - 1) + self.tail_units


def params(semantics=("arbitrary",)):
    return pltpu.CompilerParams(dimension_semantics=semantics, vmem_limit_bytes=VMEM_LIMIT)


def roll_tiles(z, tiles, shift):
    jump, low = divmod(shift % z.wide, LANES)
    count = z.tiles
    if low == 0:
        return [tiles[(j - jump) % count] for j in range(count)]
    lane = lax.broadcasted_iota(jnp.int32, tiles[0].shape, 1)
    moved = [pltpu.roll(tile, low, 1) for tile in tiles]
    return [
        jnp.where(lane < low, moved[(j - jump - 1) % count], moved[(j - jump) % count])
        for j in range(count)
    ]


def wrap_tiles(z, tiles):
    last = tiles[-1]
    lane = lax.broadcasted_iota(jnp.int32, last.shape, 1)
    ahead = pltpu.roll(tiles[0], z.tail, 1)
    behind = pltpu.roll(last, LANES - z.tail, 1)
    last = jnp.where(lane < z.tail, last, jnp.where(lane < z.tail + z.margin, ahead, behind))
    return tiles[:-1] + [last]


def row_tiles(z, value):
    tiles = [value[:, LANES * j : LANES * (j + 1)] for j in range(z.tiles - 1)]
    tail = value[:, LANES * (z.tiles - 1) :]
    zeros = jnp.zeros((value.shape[0], LANES - z.tail), F32)
    return tiles + [jnp.concatenate([tail, zeros], axis=1)]


def pack_tails(z, tails):
    lane = lax.broadcasted_iota(jnp.int32, tails[0].shape, 1)
    tiles = []
    for t in range(z.tail_units):
        begin, tile = LANES * t, None
        for row, tail in enumerate(tails):
            low = z.tail * row - begin
            if low >= LANES or low + z.tail <= 0:
                continue
            moved = pltpu.roll(tail, low % LANES, 1) if low % LANES else tail
            tile = moved if tile is None else jnp.where(lane >= low, moved, tile)
        end = z.tail * z.rows - begin
        tiles.append(jnp.where(lane < end, tile, 0.0) if end < LANES else tile)
    return tiles


def unpack_tails(z, tiles):
    lane = lax.broadcasted_iota(jnp.int32, tiles[0].shape, 1)
    tails = []
    for row in range(z.rows):
        t, low = divmod(z.tail * row, LANES)
        tail = pltpu.roll(tiles[t], LANES - low, 1) if low else tiles[t]
        if LANES - low < z.tail:
            tail = jnp.where(lane < LANES - low, tail, pltpu.roll(tiles[t + 1], LANES - low, 1))
        tails.append(jnp.where(lane < z.tail, tail, 0.0))
    return tails


def pack_rows(z, rows):
    full = z.tiles - 1
    return [row[j] for row in rows for j in range(full)] + pack_tails(z, [row[full] for row in rows])


def unpack_rows(z, tiles):
    full = z.tiles - 1
    tails = unpack_tails(z, tiles[z.rows * full :])
    return [tiles[row * full : (row + 1) * full] + [tails[row]] for row in range(z.rows)]


def packed_tiles(refs, read):
    return [
        read(ref, slice(LANES * k, LANES * (k + 1)))
        for ref in refs
        for k in range(ref.shape[-1] // LANES)
    ]


def whole(shape):
    return pl.BlockSpec(shape, lambda *_: (0,) * len(shape))


def smem():
    return pl.BlockSpec(memory_space=pltpu.SMEM)


def cost():
    return pl.CostEstimate(flops=1000, bytes_accessed=1000, transcendentals=0)


PAIR = 2
GROUP = 16


def pair_rows(z):
    return pl.BlockSpec((PAIR * z.rows, z.pad, z.width), lambda g: (g, 0, 0))


def pair_wide(z):
    return pl.BlockSpec((PAIR * z.rows, z.pad, z.wide), lambda g: (g, 0, 0))


def pair_land(z):
    return pl.BlockSpec((PAIR * z.rows, 1, z.width), lambda g: (g, 0, 0))


def pair_packed(z, cells):
    return pl.BlockSpec((PAIR * z.pad, cells), lambda g: (g, 0))


def group_rows(z):
    return pl.BlockSpec((z.height, GROUP, z.width), lambda c: (0, c, 0))


def group_wide(z):
    return pl.BlockSpec((z.height, GROUP, z.wide), lambda c: (0, c, 0))


def group_lanes(count):
    return pl.BlockSpec((count, GROUP, LANES), lambda c: (0, c, 0))


def write_pair(z, refs, bands):
    tiles = [jnp.concatenate(both, axis=0).astype(BF16) for both in zip(*bands)]
    unit = 0
    for ref in refs:
        for k in range(ref.shape[1] // LANES):
            ref[:, LANES * k : LANES * (k + 1)] = tiles[unit]
            unit += 1


def pack_out_grad(z, cells, cot, land):
    def kernel(cot_ref, land_ref, out_ref, sum_ref):
        @pl.when(pl.program_id(0) == 0)
        def _():
            sum_ref[...] = jnp.zeros_like(sum_ref)

        channel = lax.broadcasted_iota(jnp.int32, (z.pad, z.width), 0)
        total = jnp.zeros((z.pad, LANES), F32)
        bands = []
        for band in range(PAIR):
            rows = []
            for row in range(z.rows * band, z.rows * (band + 1)):
                value = cot_ref[row].astype(F32) * land_ref[row].astype(F32)
                rows.append(row_tiles(z, jnp.where(channel < z.chan, value, 0.0)))
                total = total + sum(rows[-1])
            bands.append(pack_rows(z, rows))
        sum_ref[...] += total
        write_pair(z, [out_ref], bands)

    out, sums = pl.pallas_call(
        kernel,
        grid=(z.bands // PAIR,),
        in_specs=[pair_rows(z), pair_land(z)],
        out_specs=[pair_packed(z, cells), whole((z.pad, LANES))],
        out_shape=[
            jax.ShapeDtypeStruct((z.packed_rows, cells), BF16),
            jax.ShapeDtypeStruct((z.pad, LANES), F32),
        ],
        compiler_params=params(),
        cost_estimate=cost(),
    )(cot, land)
    return out, jnp.sum(sums, axis=1)[: z.chan]


def fill_rows(z, target, read, wrap):
    zeros = jnp.zeros(target.shape[1:], F32)
    for k in range(z.margin):
        target[k] = zeros
        target[z.margin + z.height + k] = zeros

    def body(h, carry):
        tiles = row_tiles(z, read(h))
        if wrap:
            tiles = wrap_tiles(z, tiles)
        for j, tile in enumerate(tiles):
            target[z.margin + h, :, LANES * j : LANES * (j + 1)] = tile
        return carry

    lax.fori_loop(0, z.height, body, 0, unroll=8)


def convolve(z, steps, at, taps_ref, source, flip, put, carry):
    span = steps + 2 * z.margin

    def body(block, carry):
        h0 = block * steps
        rows = [
            [source[h0 + m, at, LANES * j : LANES * (j + 1)] for j in range(z.tiles)]
            for m in range(span)
        ]
        sums = [None] * steps
        for b in range(z.side):
            weights = [taps_ref[z.side * a + b, at, :] for a in range(z.side)]
            for r in range(steps):
                part = None
                for a in range(z.side):
                    row = rows[r + 2 * z.margin - a] if flip else rows[r + a]
                    terms = [weights[a] * tile for tile in row]
                    part = terms if part is None else [p + t for p, t in zip(part, terms)]
                part = roll_tiles(z, part, b - z.margin if flip else z.margin - b)
                sums[r] = part if b == 0 else [s + p for s, p in zip(sums[r], part)]
        for r in range(steps):
            carry = put(h0 + r, sums[r], carry)
        return carry

    return lax.fori_loop(0, z.height // steps, body, carry, unroll=2)


def conv_forward(z, taps, x):
    def kernel(taps_ref, x_ref, conv_ref, sum_ref, square_ref, source):
        fill_rows(z, source, lambda h: x_ref[h].astype(F32), True)
        lane = lax.broadcasted_iota(jnp.int32, (SUBL, LANES), 1)
        for part in range(GROUP // SUBL):
            at = slice(SUBL * part, SUBL * (part + 1))

            def put(h, tiles, carry):
                for j, tile in enumerate(tiles):
                    conv_ref[h, at, LANES * j : LANES * (j + 1)] = tile
                tiles = tiles[:-1] + [jnp.where(lane < z.tail, tiles[-1], 0.0)]
                return carry[0] + sum(tiles), carry[1] + sum(t * t for t in tiles)

            @pl.when(pl.program_id(0) * GROUP + SUBL * part < z.chan)
            def _():
                zero = jnp.zeros((SUBL, LANES), F32)
                total, square = convolve(z, 4, at, taps_ref, source, False, put, (zero, zero))
                sum_ref[at, :] = total
                square_ref[at, :] = square

    lane_spec = pl.BlockSpec((GROUP, LANES), lambda c: (c, 0))
    lane_shape = jax.ShapeDtypeStruct((z.pad, LANES), F32)
    conv, total, square = pl.pallas_call(
        kernel,
        grid=(pl.cdiv(z.chan, GROUP),),
        in_specs=[group_lanes(taps.shape[0]), group_rows(z)],
        out_specs=[group_wide(z), lane_spec, lane_spec],
        out_shape=[
            jax.ShapeDtypeStruct((z.height, z.pad, z.wide), F32), lane_shape, lane_shape,
        ],
        scratch_shapes=[pltpu.VMEM((z.height + 2 * z.margin, GROUP, z.wide), F32)],
        compiler_params=params(),
        cost_estimate=cost(),
    )(taps, x)
    return conv, jnp.sum(total, axis=1)[: z.chan], jnp.sum(square, axis=1)[: z.chan]


def pack_normed(z, lengths, conv, columns):
    def kernel(columns_ref, conv_ref, *outs):
        channel = lax.broadcasted_iota(jnp.int32, (z.pad, LANES), 0)
        filler = jnp.where(channel == z.chan, 1.0, 0.0)
        mean, factor, offset = columns_ref[0], columns_ref[1], columns_ref[2]
        bands = []
        for band in range(PAIR):
            rows = []
            for row in range(z.rows * band, z.rows * (band + 1)):
                tiles = [conv_ref[row, :, LANES * j : LANES * (j + 1)] for j in range(z.tiles)]
                rows.append(
                    [
                        jnp.where(channel < z.chan, (tile - mean) * factor + offset, filler)
                        for tile in tiles
                    ]
                )
            bands.append(pack_rows(z, rows))
        write_pair(z, outs, bands)

    return pl.pallas_call(
        kernel,
        grid=(z.bands // PAIR,),
        in_specs=[whole(columns.shape), pair_wide(z)],
        out_specs=[pair_packed(z, n) for n in lengths],
        out_shape=[jax.ShapeDtypeStruct((z.packed_rows, n), BF16) for n in lengths],
        compiler_params=params(),
        cost_estimate=cost(),
    )(columns, conv)


def norm_sums(z, parts, conv, columns):
    count = len(parts)

    def kernel(columns_ref, conv_ref, *rest):
        ins, (shift_ref, gain_ref) = rest[:count], rest[count:]

        @pl.when(pl.program_id(0) == 0)
        def _():
            shift_ref[...] = jnp.zeros_like(shift_ref)
            gain_ref[...] = jnp.zeros_like(gain_ref)

        mean = columns_ref[0]
        tiles = packed_tiles(ins, lambda ref, lanes: ref[:, lanes].astype(F32))
        shift = jnp.zeros((z.pad, LANES), F32)
        gain = jnp.zeros((z.pad, LANES), F32)
        for band in range(PAIR):
            rows = unpack_rows(z, [tile[z.pad * band : z.pad * (band + 1)] for tile in tiles])
            for row, grads in enumerate(rows):
                for j, grad in enumerate(grads):
                    value = conv_ref[z.rows * band + row, :, LANES * j : LANES * (j + 1)]
                    shift = shift + grad
                    gain = gain + grad * (value - mean)
        shift_ref[...] += shift
        gain_ref[...] += gain * columns_ref[1]

    lane_shape = jax.ShapeDtypeStruct((z.pad, LANES), F32)
    shift, gain = pl.pallas_call(
        kernel,
        grid=(z.bands // PAIR,),
        in_specs=[whole(columns.shape), pair_wide(z)] + [pair_packed(z, p.shape[1]) for p in parts],
        out_specs=[whole((z.pad, LANES))] * 2,
        out_shape=[lane_shape, lane_shape],
        compiler_params=params(),
        cost_estimate=cost(),
    )(columns, conv, *parts)
    return jnp.sum(shift, axis=1)[: z.chan], jnp.sum(gain, axis=1)[: z.chan]


def conv_gradient(z, begin, end, columns, parts, conv, x, ntaps, before):
    count = len(parts)
    parts = [part.reshape(z.bands, z.pad, part.shape[1]) for part in parts]
    steps = 4
    before = [] if before is None else list(before)

    def kernel(columns_ref, conv_ref, x_ref, *rest):
        ins, (grad_ref, product_ref, grads, source) = rest[:count], rest[-4:]
        mean, scale, factor, shift, gain = (columns_ref[k] for k in range(5))

        def band_body(band, carry):
            tiles = packed_tiles(ins, lambda ref, lanes: ref[band, :, lanes].astype(F32))
            for row, values in enumerate(unpack_rows(z, tiles)):
                h = band * z.rows + row
                made = []
                for j, value in enumerate(values):
                    centred = (conv_ref[h, :, LANES * j : LANES * (j + 1)] - mean) * scale
                    made.append(factor * (value - (shift + centred * gain)))
                for j, tile in enumerate(wrap_tiles(z, made)):
                    at = slice(LANES * j, LANES * (j + 1))
                    grads[h, :, at] = tile
                    grad_ref[h, :, at] = tile.astype(BF16)
            return carry

        lax.fori_loop(0, z.bands, band_body, 0)
        fill_rows(z, source, lambda h: x_ref[h].astype(F32), False)
        for part in range(GROUP // SUBL):
            at = slice(SUBL * part, SUBL * (part + 1))

            @pl.when((begin + pl.program_id(0)) * GROUP + SUBL * part < z.chan)
            def _():
                for b in range(z.side):

                    def body(block, totals):
                        h0 = block * steps
                        rows = [
                            [source[h0 + m, at, LANES * j : LANES * (j + 1)] for j in range(z.tiles)]
                            for m in range(steps + 2 * z.margin)
                        ]
                        totals = list(totals)
                        for r in range(steps):
                            moved = roll_tiles(
                                z,
                                [grads[h0 + r, at, LANES * j : LANES * (j + 1)] for j in range(z.tiles)],
                                b - z.margin,
                            )
                            for a in range(z.side):
                                for m, tile in zip(moved, rows[r + a]):
                                    totals[a] = totals[a] + m * tile
                        return tuple(totals)

                    zero = jnp.zeros((SUBL, LANES), F32)
                    totals = lax.fori_loop(0, z.height // steps, body, (zero,) * z.side, unroll=4)
                    for a in range(z.side):
                        product_ref[z.side * a + b, at, :] = totals[a]

    def group(shape):
        return pl.BlockSpec(shape, lambda c: (0, begin + c, 0))

    operands = [columns, conv, x, *parts, *before]
    return pl.pallas_call(
        kernel,
        grid=(end - begin,),
        in_specs=[
            group((5, GROUP, LANES)), group((z.height, GROUP, z.wide)),
            group((z.height, GROUP, z.width)),
        ]
        + [group((z.bands, GROUP, p.shape[2])) for p in parts]
        + [pl.BlockSpec(memory_space=pl.ANY)] * len(before),
        out_specs=[group((z.height, GROUP, z.wide)), group((ntaps, GROUP, LANES))],
        out_shape=[
            jax.ShapeDtypeStruct((z.height, z.pad, z.wide), BF16),
            jax.ShapeDtypeStruct((ntaps, z.pad, LANES), F32),
        ],
        scratch_shapes=[
            pltpu.VMEM((z.height, GROUP, z.wide), F32),
            pltpu.VMEM((z.height + 2 * z.margin, GROUP, z.wide), F32),
        ],
        input_output_aliases={len(operands) - 2 + k: k for k in range(len(before))},
        compiler_params=params(),
        cost_estimate=cost(),
    )(*operands)


def conv_backward(z, taps, grad, cot, land):
    def kernel(taps_ref, grad_ref, cot_ref, land_ref, out_ref, source, result):
        zeros = jnp.zeros(source.shape[1:], F32)
        for k in range(z.margin):
            source[k] = zeros
            source[z.margin + z.height + k] = zeros

        def fill(h, carry):
            source[z.margin + h] = grad_ref[h].astype(F32)
            return carry

        lax.fori_loop(0, z.height, fill, 0, unroll=8)
        for part in range(GROUP // SUBL):
            at = slice(SUBL * part, SUBL * (part + 1))

            def put(h, tiles, carry):
                for j, tile in enumerate(tiles):
                    result[h, at, LANES * j : LANES * (j + 1)] = tile
                return carry

            @pl.when(pl.program_id(0) * GROUP + SUBL * part < z.chan)
            def _():
                convolve(z, 4, at, taps_ref, source, True, put, 0)

        def finish(h, carry):
            direct = cot_ref[h].astype(F32) * land_ref[h].astype(F32)
            out_ref[h] = (direct + result[h][:, : z.width]).astype(BF16)
            return carry

        lax.fori_loop(0, z.height, finish, 0, unroll=8)

    return pl.pallas_call(
        kernel,
        grid=(pl.cdiv(z.chan, GROUP),),
        in_specs=[
            group_lanes(taps.shape[0]), group_wide(z), group_rows(z),
            whole((z.height, 1, z.width)),
        ],
        out_specs=group_rows(z),
        out_shape=jax.ShapeDtypeStruct((z.height, z.chan, z.width), BF16),
        scratch_shapes=[
            pltpu.VMEM((z.height + 2 * z.margin, GROUP, z.wide), F32),
            pltpu.VMEM((z.height, GROUP, z.wide), F32),
        ],
        compiler_params=params(),
        cost_estimate=cost(),
    )(taps, grad, cot, land)


def mix_branch(z, branch, x, land):
    def kernel(x_ref, land_ref, branch_ref, out_ref):
        tiles = packed_tiles([branch_ref], lambda ref, lanes: ref[:, lanes].astype(F32))
        for band in range(PAIR):
            rows = unpack_rows(z, [tile[z.pad * band : z.pad * (band + 1)] for tile in tiles])
            for k, row in enumerate(rows):
                h = z.rows * band + k
                value = jnp.concatenate(row, axis=1)[:, : z.width]
                value = land_ref[h].astype(F32) * (x_ref[h].astype(F32) + value)
                out_ref[h] = value.astype(BF16)

    return pl.pallas_call(
        kernel,
        grid=(z.bands // PAIR,),
        in_specs=[pair_rows(z), pair_land(z), pair_packed(z, branch.shape[1])],
        out_specs=pair_rows(z),
        out_shape=jax.ShapeDtypeStruct((z.height, z.chan, z.width), BF16),
        compiler_params=params(),
        cost_estimate=cost(),
    )(x, land, branch)


def gelu_parts(h):
    span = 1.0 + (0.3275911 * math.sqrt(0.5)) * jnp.abs(h)
    t = pl.reciprocal(span, approx=True)
    t = t * (2.0 - span * t)
    bell = jnp.exp2((-0.5 / math.log(2.0)) * (h * h))
    poly = t * (
        0.5 * 0.254829592
        + t
        * (
            0.5 * -0.284496736
            + t * (0.5 * 1.421413741 + t * (0.5 * -1.453152027 + t * (0.5 * 1.061405429)))
        )
    )
    tail = poly * bell
    phi = jnp.where(h >= 0, 1.0 - tail, tail)
    return h * phi, phi + h * ((1.0 / math.sqrt(2.0 * math.pi)) * bell)


def pad_weight(z, matrix):
    groups, hidden = matrix.shape[0] // z.chan, matrix.shape[1]
    block = block_of(hidden, 640)
    rows = groups * z.pad

    def kernel(in_ref, out_ref, transposed_ref, wide):
        value = in_ref[...].astype(F32)
        zeros = jnp.zeros((z.pad - z.chan, block), F32)
        for k in range(groups):
            wide[z.pad * k : z.pad * (k + 1), :] = jnp.concatenate(
                [value[z.chan * k : z.chan * (k + 1), :], zeros], axis=0
            )
        padded = wide[...]
        out_ref[...] = padded.astype(BF16)
        transposed_ref[...] = padded.T.astype(BF16)

    return pl.pallas_call(
        kernel,
        grid=(hidden // block,),
        in_specs=[pl.BlockSpec((groups * z.chan, block), lambda f: (0, f))],
        out_specs=[
            pl.BlockSpec((rows, block), lambda f: (0, f)),
            pl.BlockSpec((block, rows), lambda f: (f, 0)),
        ],
        out_shape=[
            jax.ShapeDtypeStruct((rows, hidden), BF16),
            jax.ShapeDtypeStruct((hidden, rows), BF16),
        ],
        scratch_shapes=[pltpu.VMEM((rows, block), F32)],
        compiler_params=params(),
        cost_estimate=cost(),
    )(matrix)


def lane_block(rows, cells, part):
    return pl.BlockSpec((rows, cells), lambda *_: (0, part))


def row_step(rows, most):
    return max(n for n in range(16, most + 1, 16) if rows % n == 0)


def mlp(part, length, normed, out_grad, w_in_t, w_in, w_out, w_out_t, b_in, b_out, branch_all):
    packed, cells = normed.shape
    hidden = w_in_t.shape[0]
    block = block_of(hidden, 640)
    inner = row_step(block, 320)
    blocks = hidden // block
    pairs = block // inner // 2
    rows = row_step(packed, 416)
    outs = packed // rows

    def kernel(
        n_ref, g_ref, w_in_t_ref, w_in_ref, w_out_ref, w_out_t_ref, b_in_ref, b_out_ref, *rest
    ):
        (
            branch_ref, norm_ref, active_out, hidden_out,
            h_0, h_1, back_0, back_1, active, grads, sems,
        ) = rest[-11:]
        step = pl.program_id(0)

        def products(k, h, back):
            at = pl.ds(k * inner, inner)
            h[...] = (
                jnp.dot(w_in_t_ref[at, :], n_ref[...], preferred_element_type=F32) + b_in_ref[at, :]
            )
            back[...] = jnp.dot(w_out_ref[at, :], g_ref[:, :cells], preferred_element_type=F32)

        def gelu(k, h, back):
            at = pl.ds(pl.multiple_of(jnp.maximum(k, 0) * inner, inner), inner)
            value, slope = gelu_parts(h[...])
            active[at, :] = value.astype(BF16)
            grads[at, :] = (back[...] * slope).astype(BF16)

        @pl.when(step < blocks)
        def _():
            first = step * (2 * pairs)

            def body(i, carry):
                products(2 * i, h_0, back_0)
                gelu(first + 2 * i - 1, h_1, back_1)
                products(2 * i + 1, h_1, back_1)
                gelu(first + 2 * i, h_0, back_0)
                return carry

            lax.fori_loop(0, pairs, body, 0)

        copies = [
            pltpu.make_async_copy(active, active_out, sems.at[0]),
            pltpu.make_async_copy(grads, hidden_out, sems.at[1]),
        ]

        @pl.when(step == blocks)
        def _():
            gelu(2 * pairs * blocks - 1, h_1, back_1)
            for copy in copies:
                copy.start()

        @pl.when(step >= blocks)
        def _():
            branch = jnp.dot(w_out_t_ref[...], active[...], preferred_element_type=F32)
            branch_ref[:, :cells] = (branch + b_out_ref[...]).astype(BF16)
            norm = jnp.dot(w_in_ref[...], grads[...], preferred_element_type=F32)
            norm_ref[...] = norm.astype(BF16)

        @pl.when(step == blocks + outs - 1)
        def _():
            for copy in copies:
                copy.wait()

    def at_in(f):
        return jnp.minimum(f, blocks - 1)

    def at_out(f):
        return jnp.maximum(f - blocks, 0)

    tall_block = pl.BlockSpec((block, packed), lambda f: (at_in(f), 0))
    wide_block = pl.BlockSpec((rows, hidden), lambda f: (at_out(f), 0))
    anywhere = pl.BlockSpec(memory_space=pl.ANY)
    operands = [normed, out_grad, w_in_t, w_in, w_out, w_out_t, b_in, b_out]
    in_specs = [
        whole((packed, cells)), lane_block(packed, length, part),
        tall_block, wide_block, tall_block, wide_block,
        pl.BlockSpec((block, 1), lambda f: (at_in(f), 0)),
        pl.BlockSpec((rows, 1), lambda f: (at_out(f), 0)),
    ]
    aliases = {}
    if branch_all is not None:
        aliases = {len(operands): 0}
        operands.append(branch_all)
        in_specs.append(anywhere)
    buffer = pltpu.VMEM((inner, cells), F32)
    return pl.pallas_call(
        kernel,
        grid=(blocks + outs,),
        in_specs=in_specs,
        out_specs=[
            pl.BlockSpec((rows, length), lambda f: (at_out(f), part)),
            pl.BlockSpec((rows, cells), lambda f: (at_out(f), 0)),
            anywhere, anywhere,
        ],
        out_shape=[
            jax.ShapeDtypeStruct(out_grad.shape, BF16),
            jax.ShapeDtypeStruct((packed, cells), BF16),
            jax.ShapeDtypeStruct((hidden, cells), BF16),
            jax.ShapeDtypeStruct((hidden, cells), BF16),
        ],
        scratch_shapes=[buffer] * 4
        + [pltpu.VMEM((hidden, cells), BF16)] * 2
        + [pltpu.SemaphoreType.DMA((2,))],
        input_output_aliases=aliases,
        compiler_params=params(),
        cost_estimate=cost(),
    )(*operands)


def weight_grad(core, lefts, rights):
    rows, hidden = lefts[0][0].shape[0], rights[0].shape[0]
    half = rows // CORES
    block = block_of(hidden, 640)
    arrays = []
    for array, _ in lefts:
        if not any(array is known for known in arrays):
            arrays.append(array)
    which = [next(k for k, known in enumerate(arrays) if known is array) for array, _ in lefts]

    def kernel(core_ref, *refs):
        mine_ref, sent_ref, both = refs[-3:]
        total = None
        for k, (_, start), right in zip(which, lefts, refs[len(arrays) : -3]):
            part = lax.dot_general(
                refs[k][:, start : start + right.shape[1]], right[...],
                (((1,), (1,)), ((), ())), preferred_element_type=F32,
            )
            total = part if total is None else total + part
        both[0] = total[:half].astype(BF16)
        both[1] = total[half:].astype(BF16)
        mine_ref[...] = both[core_ref[0]]
        sent_ref[...] = both[1 - core_ref[0]]

    out = jax.ShapeDtypeStruct((half, hidden), BF16)
    return pl.pallas_call(
        kernel,
        grid=(hidden // block,),
        in_specs=[smem()] + [whole(array.shape) for array in arrays]
        + [pl.BlockSpec((block, right.shape[1]), lambda f: (f, 0)) for right in rights],
        out_specs=[pl.BlockSpec((half, block), lambda f: (0, f))] * 2,
        out_shape=[out, out],
        scratch_shapes=[pltpu.VMEM((CORES, half, block), BF16)],
        compiler_params=params(),
        cost_estimate=cost(),
    )(core[None], *arrays, *rights)


def unpad_rows(z, place, pieces):
    groups, hidden = pieces[0].shape[0] // z.pad, pieces[0].shape[1]

    def kernel(place_ref, *refs):
        out_ref = refs[-1]

        def put(ref):
            value = ref[...].astype(F32)
            for k in range(groups):
                out_ref[z.chan * k : z.chan * (k + 1), :] = value[z.pad * k : z.pad * k + z.chan, :]

        wanted = jnp.bitwise_xor(pl.program_id(0), place_ref[0])
        for k, ref in enumerate(refs[:-1]):
            pl.when(wanted == k)(partial(put, ref))

    return pl.pallas_call(
        kernel,
        grid=(4,),
        in_specs=[smem()] + [whole(pieces[0].shape)] * 4,
        out_specs=pl.BlockSpec((groups * z.chan, hidden), lambda q: (q, 0)),
        out_shape=jax.ShapeDtypeStruct((4 * groups * z.chan, hidden), F32),
        compiler_params=params(),
        cost_estimate=cost(),
    )(place[None], *pieces)


def exchange(value):
    return lax.all_to_all(value, CHAN, split_axis=0, concat_axis=0, tiled=True)


def after(value, *others):
    return lax.optimization_barrier((value, *others))[0]


def dp_sum(value):
    ways = lax.axis_size("dp")
    total = value
    for turn in range(1, ways):
        total = total + lax.ppermute(value, "dp", [(i, i ^ turn) for i in range(ways)])
    return total


def swap_cores(value):
    return lax.ppermute(value, "core", [(0, 1), (1, 0)])


class HalvingSum:
    def __init__(self, turns, mine, sent):
        place = lax.axis_index("dp")
        self.turns = turns
        self.bits = [jnp.bitwise_and(place // turn, 1) for turn in turns]
        self.core = lax.axis_index("core")
        self.mine, self.other = mine, swap_cores(sent)

    def meet(self, value, turn):
        ways = lax.axis_size("dp")
        return lax.ppermute(value, "dp", [(i, i ^ turn) for i in range(ways)])

    def pair(self, half):
        rows = self.mine.shape[0] // 2
        at = half * rows
        return lax.dynamic_slice_in_dim(self.mine, at, rows, 0).astype(
            F32
        ) + lax.dynamic_slice_in_dim(self.other, at, rows, 0).astype(F32)

    def first(self, ready):
        self.mine = after(self.mine, ready)
        self.arrived = self.meet(self.pair(1 - self.bits[0]).astype(BF16), self.turns[0])

    def second(self, ready):
        arrived = after(self.arrived, ready)
        total = self.pair(self.bits[0]) + arrived.astype(F32)
        rows = total.shape[0] // 2
        send = lax.dynamic_slice_in_dim(total, (1 - self.bits[1]) * rows, rows, 0).astype(BF16)
        self.kept = lax.dynamic_slice_in_dim(total, self.bits[1] * rows, rows, 0)
        self.sent = send
        self.arrived = self.meet(send, self.turns[1])

    def share(self, ready):
        return (self.kept + after(self.arrived, ready).astype(F32)).astype(BF16)

    def back_first(self, share):
        self.own = share
        self.arrived = self.meet(share, self.turns[1])

    def back_second(self, ready):
        other = after(self.arrived, ready)
        low = self.bits[1] == 0
        self.own = jnp.concatenate(
            [jnp.where(low, self.own, other), jnp.where(low, other, self.own)], axis=0
        )
        self.arrived = self.meet(self.own, self.turns[0])
        self.swapped = swap_cores(self.own)

    def finish(self, z, ready):
        other = after(self.arrived, ready)
        pieces = [self.own, other, self.swapped, swap_cores(other)]
        return unpad_rows(z, self.core * 2 + self.bits[0], pieces), pieces

    def first_row(self, pieces, row):
        place = self.core * 2 + self.bits[0]
        found = pieces[0][row]
        for k in range(1, 4):
            found = jnp.where(place == k, pieces[k][row], found)
        return found.astype(F32)


def per_device(
    x_in, cotangent, land, grid_res, dw_kernel, gain, shift, res_bias, w_in, b_in, w_out, b_out
):
    samples, height, columns, chan = x_in.shape
    groups = lax.axis_size("pair") * CORES
    first = (lax.axis_index("pair") * CORES + lax.axis_index("core")) * chan
    width = chan * groups
    ntaps = dw_kernel.shape[0]
    z = Sizes(chan, height, columns, groups, ntaps)
    pixels = float(samples * lax.axis_size("dp") * height * columns)
    part = (z.units + 1) // 2 * LANES
    lengths = [part, z.units * LANES - part]
    starts = [0, part]

    def own(values, axis=0):
        return lax.dynamic_slice_in_dim(values, first, chan, axis)

    def over_lanes(rows):
        rows = jnp.pad(rows, ((0, 0), (0, z.pad - chan)))
        return jnp.broadcast_to(rows[:, :, None], rows.shape + (LANES,))

    x = jnp.transpose(x_in[0], (0, 2, 1))
    cot = jnp.transpose(cotangent[0], (0, 2, 1))
    land3 = land[0][:, None, :]

    grad_packed, part_b_out = pack_out_grad(z, sum(lengths), cot, land3)
    grad_band = exchange(grad_packed)

    taps = over_lanes(own(dw_kernel, 1).astype(F32))
    conv, total, square = conv_forward(z, taps, after(x, grad_packed))
    total, square = lax.psum((total, square), "dp")
    mean = total / pixels
    var = square / pixels - mean * mean
    scale = lax.rsqrt(var + 1e-05)
    own_gain = own(gain)
    chooser = (grid_res[:, None] == jnp.arange(2, dtype=jnp.int32)[None, :]).astype(F32)
    sample_bias = jnp.sum(chooser[0][:, None] * own(res_bias, 1), axis=0)
    affine = over_lanes(jnp.stack([mean, own_gain * scale, own(shift) + sample_bias]))
    packed = pack_normed(z, lengths, conv, affine)

    w_in_p, w_in_t = pad_weight(z, after(w_in, packed[0]))
    w_out_t, w_out_p = pad_weight(z, after(w_out.T, packed[0]))
    b_out_p = jnp.pad(b_out.reshape(groups, chan), ((0, 0), (0, z.pad - chan))).reshape(-1, 1)
    weights = (w_in_t, w_in_p, w_out_p, w_out_t, b_in[:, None], b_out_p)

    normed = [exchange(after(packed[0], grad_band))]
    normed.append(exchange(after(packed[1], normed[0], w_in_t, w_out_p)))
    branch, norm1, active1, hidden1 = mlp(0, part, normed[0], grad_band, *weights, None)
    norm_parts = [exchange(after(norm1, normed[1]))]
    branch, norm2, active2, hidden2 = mlp(1, part, normed[1], grad_band, *weights, branch)
    norm_parts.append(exchange(after(norm2, norm_parts[0])))
    core = lax.axis_index("core")
    mine, sent_out = weight_grad(
        core, [(grad_band, start) for start in starts], [active1, after(active2, norm_parts[0])]
    )
    sum_out = HalvingSum((1, 2), mine, sent_out)
    mine, sent_in = weight_grad(
        core, [(value, 0) for value in normed], [hidden1, after(hidden2, sent_out)]
    )
    sum_in = HalvingSum((2, 1), mine, sent_in)
    branch = exchange(after(branch, norm_parts[1], sent_in))
    sum_out.first(norm_parts[1])
    sum_in.first(norm_parts[1])

    part_shift, part_gain = norm_sums(z, norm_parts, conv, over_lanes(jnp.stack([mean, scale])))
    small = jnp.concatenate(
        [part_shift[None], part_gain[None], chooser[0][:, None] * part_shift[None], part_b_out[None]],
        axis=0,
    )
    small = lax.psum(small, "dp")
    terms = over_lanes(
        jnp.stack([mean, scale, own_gain * scale, small[0] / pixels, small[1] / pixels])
    )
    calls = pl.cdiv(chan, GROUP)
    cuts = [0, min(2, calls), min(4, calls), calls]
    cuts = [cut for k, cut in enumerate(cuts) if k == 0 or cut > cuts[k - 1]]
    made = conv_gradient(z, cuts[0], cuts[1], terms, norm_parts, conv, x, ntaps, None)
    sum_out.second(made[1])
    sum_in.second(made[1])
    if len(cuts) > 2:
        made = conv_gradient(
            z, cuts[1], cuts[2], after(terms, sum_out.sent, sum_in.sent), norm_parts, conv, x, ntaps, made
        )
    shares = sum_out.share(made[1]), sum_in.share(made[1])
    if len(cuts) > 3:
        made = conv_gradient(
            z, cuts[2], cuts[3], after(terms, *shares), norm_parts, conv, x, ntaps, made
        )
    conv_grad, products = made
    shares = lax.psum(shares, "pair")
    g_kernel = dp_sum(jnp.sum(products, axis=2)[:, :chan])
    x_grad = conv_backward(z, taps, conv_grad, cot, land3)
    rows = jnp.concatenate([after(g_kernel, x_grad), small], axis=0)
    gathered = lax.all_gather(rows, CHAN)
    placed = jnp.transpose(gathered, (1, 0, 2)).reshape(rows.shape[0], width)
    sum_out.back_first(after(shares[0], gathered))
    sum_in.back_first(after(shares[1], gathered))
    mixed = mix_branch(z, branch, after(x, sum_out.own, sum_in.own), land3)
    sum_out.back_second(mixed)
    sum_in.back_second(mixed)
    mixed = after(mixed, sum_out.own, sum_in.own)
    mixed_out = jnp.transpose(mixed, (0, 2, 1))[None]
    x_grad_out = jnp.transpose(after(x_grad, sum_out.own, sum_in.own), (0, 2, 1))[None]
    g_w_out_t, _ = sum_out.finish(z, x_grad_out)
    g_w_in, pieces = sum_in.finish(z, x_grad_out)

    return (
        mixed_out,
        x_grad_out,
        placed[:ntaps],
        placed[ntaps + 1],
        placed[ntaps],
        placed[ntaps + 2 : ntaps + 4],
        g_w_in,
        sum_in.first_row(pieces, chan),
        g_w_out_t.T,
        placed[ntaps + 4],
    )


def solution(mesh):
    shape = mesh.shape
    mesh = jax.sharding.Mesh(
        mesh.devices.reshape(shape["dp"], shape["chan"] // CORES, CORES), ("dp",) + CHAN
    )
    cells = P("dp", None, None, CHAN)
    return jax.shard_map(
        per_device,
        mesh=mesh,
        in_specs=(cells, cells, P("dp", None, None), P("dp")) + (P(),) * 8,
        out_specs=(cells, cells) + (P(),) * 8,
        check_vma=False,
    )
```

```python
from functools import partial
import math

import jax
import jax.numpy as jnp
from jax import lax
from jax.experimental import pallas as pl
from jax.experimental.layout import Layout, with_layout_constraint
from jax.experimental.pallas import tpu as pltpu
from jax.sharding import PartitionSpec as P

LANES = 128
SUBL = 8
VMEM_LIMIT = 56 * 1024 * 1024
CHAN = ("pair", "core")
CORES = 2
F32 = jnp.float32
BF16 = jnp.bfloat16


def round_up(value, step):
    return (value + step - 1) // step * step


def block_of(total, most):
    return max(size for size in range(1, most + 1) if total % size == 0)


class Sizes:
    def __init__(self, chan, height, width, bands, taps):
        self.chan, self.height, self.width, self.bands = chan, height, width, bands
        self.side = math.isqrt(taps)
        self.margin = self.side // 2
        self.rows = height // bands
        self.wide = round_up(width + 2 * self.margin, LANES)
        self.tiles = self.wide // LANES
        self.tail = width - (self.tiles - 1) * LANES
        self.pad = round_up(chan + 1, SUBL)
        self.packed_rows = bands * self.pad
        self.tail_units = round_up(self.rows * self.tail, LANES) // LANES
        self.units = self.rows * (self.tiles - 1) + self.tail_units


def params(semantics=("arbitrary",)):
    return pltpu.CompilerParams(dimension_semantics=semantics, vmem_limit_bytes=VMEM_LIMIT)


def roll_tiles(z, tiles, shift):
    jump, low = divmod(shift % z.wide, LANES)
    count = z.tiles
    if low == 0:
        return [tiles[(j - jump) % count] for j in range(count)]
    lane = lax.broadcasted_iota(jnp.int32, tiles[0].shape, 1)
    moved = [pltpu.roll(tile, low, 1) for tile in tiles]
    return [
        jnp.where(lane < low, moved[(j - jump - 1) % count], moved[(j - jump) % count])
        for j in range(count)
    ]


def wrap_tiles(z, tiles):
    last = tiles[-1]
    lane = lax.broadcasted_iota(jnp.int32, last.shape, 1)
    ahead = pltpu.roll(tiles[0], z.tail, 1)
    behind = pltpu.roll(last, LANES - z.tail, 1)
    last = jnp.where(lane < z.tail, last, jnp.where(lane < z.tail + z.margin, ahead, behind))
    return tiles[:-1] + [last]


def row_tiles(z, value):
    tiles = [value[:, LANES * j : LANES * (j + 1)] for j in range(z.tiles - 1)]
    tail = value[:, LANES * (z.tiles - 1) :]
    zeros = jnp.zeros((value.shape[0], LANES - z.tail), F32)
    return tiles + [jnp.concatenate([tail, zeros], axis=1)]


def pack_tails(z, tails):
    lane = lax.broadcasted_iota(jnp.int32, tails[0].shape, 1)
    tiles = []
    for t in range(z.tail_units):
        begin, tile = LANES * t, None
        for row, tail in enumerate(tails):
            low = z.tail * row - begin
            if low >= LANES or low + z.tail <= 0:
                continue
            moved = pltpu.roll(tail, low % LANES, 1) if low % LANES else tail
            tile = moved if tile is None else jnp.where(lane >= low, moved, tile)
        end = z.tail * z.rows - begin
        tiles.append(jnp.where(lane < end, tile, 0.0) if end < LANES else tile)
    return tiles


def unpack_tails(z, tiles):
    lane = lax.broadcasted_iota(jnp.int32, tiles[0].shape, 1)
    tails = []
    for row in range(z.rows):
        t, low = divmod(z.tail * row, LANES)
        tail = pltpu.roll(tiles[t], LANES - low, 1) if low else tiles[t]
        if LANES - low < z.tail:
            tail = jnp.where(lane < LANES - low, tail, pltpu.roll(tiles[t + 1], LANES - low, 1))
        tails.append(jnp.where(lane < z.tail, tail, 0.0))
    return tails


def pack_rows(z, rows):
    full = z.tiles - 1
    return [row[j] for row in rows for j in range(full)] + pack_tails(z, [row[full] for row in rows])


def unpack_rows(z, tiles):
    full = z.tiles - 1
    tails = unpack_tails(z, tiles[z.rows * full :])
    return [tiles[row * full : (row + 1) * full] + [tails[row]] for row in range(z.rows)]


def packed_tiles(refs, read):
    return [
        read(ref, slice(LANES * k, LANES * (k + 1)))
        for ref in refs
        for k in range(ref.shape[-1] // LANES)
    ]


def whole(shape):
    return pl.BlockSpec(shape, lambda *_: (0,) * len(shape))


def smem():
    return pl.BlockSpec(memory_space=pltpu.SMEM)


def cost():
    return pl.CostEstimate(flops=1000, bytes_accessed=1000, transcendentals=0)


PAIR = 2
GROUP = 16


def pair_rows(z):
    return pl.BlockSpec((PAIR * z.rows, z.pad, z.width), lambda g: (g, 0, 0))


def pair_wide(z):
    return pl.BlockSpec((PAIR * z.rows, z.pad, z.wide), lambda g: (g, 0, 0))


def pair_land(z):
    return pl.BlockSpec((PAIR * z.rows, 1, z.width), lambda g: (g, 0, 0))


def pair_packed(z, cells):
    return pl.BlockSpec((PAIR * z.pad, cells), lambda g: (g, 0))


def group_rows(z):
    return pl.BlockSpec((z.height, GROUP, z.width), lambda c: (0, c, 0))


def group_wide(z):
    return pl.BlockSpec((z.height, GROUP, z.wide), lambda c: (0, c, 0))


def group_lanes(count):
    return pl.BlockSpec((count, GROUP, LANES), lambda c: (0, c, 0))


def write_pair(z, refs, bands):
    tiles = [jnp.concatenate(both, axis=0).astype(BF16) for both in zip(*bands)]
    unit = 0
    for ref in refs:
        for k in range(ref.shape[1] // LANES):
            ref[:, LANES * k : LANES * (k + 1)] = tiles[unit]
            unit += 1


def pack_out_grad(z, cells, cot, land):
    def kernel(cot_ref, land_ref, out_ref, sum_ref):
        @pl.when(pl.program_id(0) == 0)
        def _():
            sum_ref[...] = jnp.zeros_like(sum_ref)

        channel = lax.broadcasted_iota(jnp.int32, (z.pad, z.width), 0)
        total = jnp.zeros((z.pad, LANES), F32)
        bands = []
        for band in range(PAIR):
            rows = []
            for row in range(z.rows * band, z.rows * (band + 1)):
                value = cot_ref[row].astype(F32) * land_ref[row].astype(F32)
                rows.append(row_tiles(z, jnp.where(channel < z.chan, value, 0.0)))
                total = total + sum(rows[-1])
            bands.append(pack_rows(z, rows))
        sum_ref[...] += total
        write_pair(z, [out_ref], bands)

    out, sums = pl.pallas_call(
        kernel,
        grid=(z.bands // PAIR,),
        in_specs=[pair_rows(z), pair_land(z)],
        out_specs=[pair_packed(z, cells), whole((z.pad, LANES))],
        out_shape=[
            jax.ShapeDtypeStruct((z.packed_rows, cells), BF16),
            jax.ShapeDtypeStruct((z.pad, LANES), F32),
        ],
        compiler_params=params(),
        cost_estimate=cost(),
    )(cot, land)
    return out, jnp.sum(sums, axis=1)[: z.chan]


def fill_rows(z, target, read, wrap):
    zeros = jnp.zeros(target.shape[1:], F32)
    for k in range(z.margin):
        target[k] = zeros
        target[z.margin + z.height + k] = zeros

    def body(h, carry):
        tiles = row_tiles(z, read(h))
        if wrap:
            tiles = wrap_tiles(z, tiles)
        for j, tile in enumerate(tiles):
            target[z.margin + h, :, LANES * j : LANES * (j + 1)] = tile
        return carry

    lax.fori_loop(0, z.height, body, 0, unroll=8)


def convolve(z, steps, at, taps_ref, source, flip, put, carry):
    span = steps + 2 * z.margin

    def body(block, carry):
        h0 = block * steps
        rows = [
            [source[h0 + m, at, LANES * j : LANES * (j + 1)] for j in range(z.tiles)]
            for m in range(span)
        ]
        sums = [None] * steps
        for b in range(z.side):
            weights = [taps_ref[z.side * a + b, at, :] for a in range(z.side)]
            for r in range(steps):
                part = None
                for a in range(z.side):
                    row = rows[r + 2 * z.margin - a] if flip else rows[r + a]
                    terms = [weights[a] * tile for tile in row]
                    part = terms if part is None else [p + t for p, t in zip(part, terms)]
                part = roll_tiles(z, part, b - z.margin if flip else z.margin - b)
                sums[r] = part if b == 0 else [s + p for s, p in zip(sums[r], part)]
        for r in range(steps):
            carry = put(h0 + r, sums[r], carry)
        return carry

    return lax.fori_loop(0, z.height // steps, body, carry, unroll=2)


def conv_forward(z, taps, x):
    def kernel(taps_ref, x_ref, conv_ref, sum_ref, square_ref, source):
        fill_rows(z, source, lambda h: x_ref[h].astype(F32), True)
        lane = lax.broadcasted_iota(jnp.int32, (SUBL, LANES), 1)
        for part in range(GROUP // SUBL):
            at = slice(SUBL * part, SUBL * (part + 1))

            def put(h, tiles, carry):
                for j, tile in enumerate(tiles):
                    conv_ref[h, at, LANES * j : LANES * (j + 1)] = tile
                tiles = tiles[:-1] + [jnp.where(lane < z.tail, tiles[-1], 0.0)]
                return carry[0] + sum(tiles), carry[1] + sum(t * t for t in tiles)

            @pl.when(pl.program_id(0) * GROUP + SUBL * part < z.chan)
            def _():
                zero = jnp.zeros((SUBL, LANES), F32)
                total, square = convolve(z, 4, at, taps_ref, source, False, put, (zero, zero))
                sum_ref[at, :] = total
                square_ref[at, :] = square

    lane_spec = pl.BlockSpec((GROUP, LANES), lambda c: (c, 0))
    lane_shape = jax.ShapeDtypeStruct((z.pad, LANES), F32)
    conv, total, square = pl.pallas_call(
        kernel,
        grid=(pl.cdiv(z.chan, GROUP),),
        in_specs=[group_lanes(taps.shape[0]), group_rows(z)],
        out_specs=[group_wide(z), lane_spec, lane_spec],
        out_shape=[
            jax.ShapeDtypeStruct((z.height, z.pad, z.wide), F32), lane_shape, lane_shape,
        ],
        scratch_shapes=[pltpu.VMEM((z.height + 2 * z.margin, GROUP, z.wide), F32)],
        compiler_params=params(),
        cost_estimate=cost(),
    )(taps, x)
    return conv, jnp.sum(total, axis=1)[: z.chan], jnp.sum(square, axis=1)[: z.chan]


def pack_normed(z, lengths, conv, columns):
    def kernel(columns_ref, conv_ref, *outs):
        channel = lax.broadcasted_iota(jnp.int32, (z.pad, LANES), 0)
        filler = jnp.where(channel == z.chan, 1.0, 0.0)
        mean, factor, offset = columns_ref[0], columns_ref[1], columns_ref[2]
        bands = []
        for band in range(PAIR):
            rows = []
            for row in range(z.rows * band, z.rows * (band + 1)):
                tiles = [conv_ref[row, :, LANES * j : LANES * (j + 1)] for j in range(z.tiles)]
                rows.append(
                    [
                        jnp.where(channel < z.chan, (tile - mean) * factor + offset, filler)
                        for tile in tiles
                    ]
                )
            bands.append(pack_rows(z, rows))
        write_pair(z, outs, bands)

    return pl.pallas_call(
        kernel,
        grid=(z.bands // PAIR,),
        in_specs=[whole(columns.shape), pair_wide(z)],
        out_specs=[pair_packed(z, n) for n in lengths],
        out_shape=[jax.ShapeDtypeStruct((z.packed_rows, n), BF16) for n in lengths],
        compiler_params=params(),
        cost_estimate=cost(),
    )(columns, conv)


def norm_sums(z, parts, conv, columns):
    count = len(parts)

    def kernel(columns_ref, conv_ref, *rest):
        ins, (shift_ref, gain_ref) = rest[:count], rest[count:]

        @pl.when(pl.program_id(0) == 0)
        def _():
            shift_ref[...] = jnp.zeros_like(shift_ref)
            gain_ref[...] = jnp.zeros_like(gain_ref)

        mean = columns_ref[0]
        tiles = packed_tiles(ins, lambda ref, lanes: ref[:, lanes].astype(F32))
        shift = jnp.zeros((z.pad, LANES), F32)
        gain = jnp.zeros((z.pad, LANES), F32)
        for band in range(PAIR):
            rows = unpack_rows(z, [tile[z.pad * band : z.pad * (band + 1)] for tile in tiles])
            for row, grads in enumerate(rows):
                for j, grad in enumerate(grads):
                    value = conv_ref[z.rows * band + row, :, LANES * j : LANES * (j + 1)]
                    shift = shift + grad
                    gain = gain + grad * (value - mean)
        shift_ref[...] += shift
        gain_ref[...] += gain * columns_ref[1]

    lane_shape = jax.ShapeDtypeStruct((z.pad, LANES), F32)
    shift, gain = pl.pallas_call(
        kernel,
        grid=(z.bands // PAIR,),
        in_specs=[whole(columns.shape), pair_wide(z)] + [pair_packed(z, p.shape[1]) for p in parts],
        out_specs=[whole((z.pad, LANES))] * 2,
        out_shape=[lane_shape, lane_shape],
        compiler_params=params(),
        cost_estimate=cost(),
    )(columns, conv, *parts)
    return jnp.sum(shift, axis=1)[: z.chan], jnp.sum(gain, axis=1)[: z.chan]


def conv_gradient(z, begin, end, columns, parts, conv, x, ntaps, before):
    count = len(parts)
    parts = [part.reshape(z.bands, z.pad, part.shape[1]) for part in parts]
    steps = 4
    before = [] if before is None else list(before)

    def kernel(columns_ref, conv_ref, x_ref, *rest):
        ins, (grad_ref, product_ref, grads, source) = rest[:count], rest[-4:]
        mean, scale, factor, shift, gain = (columns_ref[k] for k in range(5))

        def band_body(band, carry):
            tiles = packed_tiles(ins, lambda ref, lanes: ref[band, :, lanes].astype(F32))
            for row, values in enumerate(unpack_rows(z, tiles)):
                h = band * z.rows + row
                made = []
                for j, value in enumerate(values):
                    centred = (conv_ref[h, :, LANES * j : LANES * (j + 1)] - mean) * scale
                    made.append(factor * (value - (shift + centred * gain)))
                for j, tile in enumerate(wrap_tiles(z, made)):
                    at = slice(LANES * j, LANES * (j + 1))
                    grads[h, :, at] = tile
                    grad_ref[h, :, at] = tile.astype(BF16)
            return carry

        lax.fori_loop(0, z.bands, band_body, 0)
        fill_rows(z, source, lambda h: x_ref[h].astype(F32), False)
        for part in range(GROUP // SUBL):
            at = slice(SUBL * part, SUBL * (part + 1))

            @pl.when((begin + pl.program_id(0)) * GROUP + SUBL * part < z.chan)
            def _():
                for b in range(z.side):

                    def body(block, totals):
                        h0 = block * steps
                        rows = [
                            [source[h0 + m, at, LANES * j : LANES * (j + 1)] for j in range(z.tiles)]
                            for m in range(steps + 2 * z.margin)
                        ]
                        totals = list(totals)
                        for r in range(steps):
                            moved = roll_tiles(
                                z,
                                [grads[h0 + r, at, LANES * j : LANES * (j + 1)] for j in range(z.tiles)],
                                b - z.margin,
                            )
                            for a in range(z.side):
                                for m, tile in zip(moved, rows[r + a]):
                                    totals[a] = totals[a] + m * tile
                        return tuple(totals)

                    zero = jnp.zeros((SUBL, LANES), F32)
                    totals = lax.fori_loop(0, z.height // steps, body, (zero,) * z.side, unroll=4)
                    for a in range(z.side):
                        product_ref[z.side * a + b, at, :] = totals[a]

    def group(shape):
        return pl.BlockSpec(shape, lambda c: (0, begin + c, 0))

    operands = [columns, conv, x, *parts, *before]
    return pl.pallas_call(
        kernel,
        grid=(end - begin,),
        in_specs=[
            group((5, GROUP, LANES)), group((z.height, GROUP, z.wide)),
            group((z.height, GROUP, z.width)),
        ]
        + [group((z.bands, GROUP, p.shape[2])) for p in parts]
        + [pl.BlockSpec(memory_space=pl.ANY)] * len(before),
        out_specs=[group((z.height, GROUP, z.wide)), group((ntaps, GROUP, LANES))],
        out_shape=[
            jax.ShapeDtypeStruct((z.height, z.pad, z.wide), BF16),
            jax.ShapeDtypeStruct((ntaps, z.pad, LANES), F32),
        ],
        scratch_shapes=[
            pltpu.VMEM((z.height, GROUP, z.wide), F32),
            pltpu.VMEM((z.height + 2 * z.margin, GROUP, z.wide), F32),
        ],
        input_output_aliases={len(operands) - 2 + k: k for k in range(len(before))},
        compiler_params=params(),
        cost_estimate=cost(),
    )(*operands)


def conv_backward(z, taps, grad, cot, land):
    def kernel(taps_ref, grad_ref, cot_ref, land_ref, out_ref, source, result):
        zeros = jnp.zeros(source.shape[1:], F32)
        for k in range(z.margin):
            source[k] = zeros
            source[z.margin + z.height + k] = zeros

        def fill(h, carry):
            source[z.margin + h] = grad_ref[h].astype(F32)
            return carry

        lax.fori_loop(0, z.height, fill, 0, unroll=8)
        for part in range(GROUP // SUBL):
            at = slice(SUBL * part, SUBL * (part + 1))

            def put(h, tiles, carry):
                for j, tile in enumerate(tiles):
                    result[h, at, LANES * j : LANES * (j + 1)] = tile
                return carry

            @pl.when(pl.program_id(0) * GROUP + SUBL * part < z.chan)
            def _():
                convolve(z, 4, at, taps_ref, source, True, put, 0)

        def finish(h, carry):
            direct = cot_ref[h].astype(F32) * land_ref[h].astype(F32)
            out_ref[h] = (direct + result[h][:, : z.width]).astype(BF16)
            return carry

        lax.fori_loop(0, z.height, finish, 0, unroll=8)

    return pl.pallas_call(
        kernel,
        grid=(pl.cdiv(z.chan, GROUP),),
        in_specs=[
            group_lanes(taps.shape[0]), group_wide(z), group_rows(z),
            whole((z.height, 1, z.width)),
        ],
        out_specs=group_rows(z),
        out_shape=jax.ShapeDtypeStruct((z.height, z.chan, z.width), BF16),
        scratch_shapes=[
            pltpu.VMEM((z.height + 2 * z.margin, GROUP, z.wide), F32),
            pltpu.VMEM((z.height, GROUP, z.wide), F32),
        ],
        compiler_params=params(),
        cost_estimate=cost(),
    )(taps, grad, cot, land)


def mix_branch(z, branch, x, land):
    def kernel(x_ref, land_ref, branch_ref, out_ref):
        tiles = packed_tiles([branch_ref], lambda ref, lanes: ref[:, lanes].astype(F32))
        for band in range(PAIR):
            rows = unpack_rows(z, [tile[z.pad * band : z.pad * (band + 1)] for tile in tiles])
            for k, row in enumerate(rows):
                h = z.rows * band + k
                value = jnp.concatenate(row, axis=1)[:, : z.width]
                value = land_ref[h].astype(F32) * (x_ref[h].astype(F32) + value)
                out_ref[h] = value.astype(BF16)

    return pl.pallas_call(
        kernel,
        grid=(z.bands // PAIR,),
        in_specs=[pair_rows(z), pair_land(z), pair_packed(z, branch.shape[1])],
        out_specs=pair_rows(z),
        out_shape=jax.ShapeDtypeStruct((z.height, z.chan, z.width), BF16),
        compiler_params=params(),
        cost_estimate=cost(),
    )(x, land, branch)


def gelu_parts(h):
    span = 1.0 + (0.3275911 * math.sqrt(0.5)) * jnp.abs(h)
    t = pl.reciprocal(span, approx=True)
    t = t * (2.0 - span * t)
    bell = jnp.exp2((-0.5 / math.log(2.0)) * (h * h))
    poly = t * (
        0.5 * 0.254829592
        + t
        * (
            0.5 * -0.284496736
            + t * (0.5 * 1.421413741 + t * (0.5 * -1.453152027 + t * (0.5 * 1.061405429)))
        )
    )
    tail = poly * bell
    phi = jnp.where(h >= 0, 1.0 - tail, tail)
    return h * phi, phi + h * ((1.0 / math.sqrt(2.0 * math.pi)) * bell)


def pad_weight(z, matrix):
    groups, hidden = matrix.shape[0] // z.chan, matrix.shape[1]
    block = block_of(hidden, 640)
    rows = groups * z.pad

    def kernel(in_ref, out_ref, transposed_ref, wide):
        value = in_ref[...].astype(F32)
        zeros = jnp.zeros((z.pad - z.chan, block), F32)
        for k in range(groups):
            wide[z.pad * k : z.pad * (k + 1), :] = jnp.concatenate(
                [value[z.chan * k : z.chan * (k + 1), :], zeros], axis=0
            )
        padded = wide[...]
        out_ref[...] = padded.astype(BF16)
        transposed_ref[...] = padded.T.astype(BF16)

    return pl.pallas_call(
        kernel,
        grid=(hidden // block,),
        in_specs=[pl.BlockSpec((groups * z.chan, block), lambda f: (0, f))],
        out_specs=[
            pl.BlockSpec((rows, block), lambda f: (0, f)),
            pl.BlockSpec((block, rows), lambda f: (f, 0)),
        ],
        out_shape=[
            jax.ShapeDtypeStruct((rows, hidden), BF16),
            jax.ShapeDtypeStruct((hidden, rows), BF16),
        ],
        scratch_shapes=[pltpu.VMEM((rows, block), F32)],
        compiler_params=params(),
        cost_estimate=cost(),
    )(matrix)


def lane_block(rows, cells, part):
    return pl.BlockSpec((rows, cells), lambda *_: (0, part))


def row_step(rows, most):
    return max(n for n in range(16, most + 1, 16) if rows % n == 0)


def mlp(part, length, normed, out_grad, w_in_t, w_in, w_out, w_out_t, b_in, b_out, branch_all):
    packed, cells = normed.shape
    hidden = w_in_t.shape[0]
    block = block_of(hidden, 640)
    inner = row_step(block, 320)
    blocks = hidden // block
    pairs = block // inner // 2
    rows = row_step(packed, 416)
    outs = packed // rows

    def kernel(
        n_ref, g_ref, w_in_t_ref, w_in_ref, w_out_ref, w_out_t_ref, b_in_ref, b_out_ref, *rest
    ):
        (
            branch_ref, norm_ref, active_out, hidden_out,
            h_0, h_1, back_0, back_1, active, grads, sems,
        ) = rest[-11:]
        step = pl.program_id(0)

        def products(k, h, back):
            at = pl.ds(k * inner, inner)
            h[...] = (
                jnp.dot(w_in_t_ref[at, :], n_ref[...], preferred_element_type=F32) + b_in_ref[at, :]
            )
            back[...] = jnp.dot(w_out_ref[at, :], g_ref[:, :cells], preferred_element_type=F32)

        def gelu(k, h, back):
            at = pl.ds(pl.multiple_of(jnp.maximum(k, 0) * inner, inner), inner)
            value, slope = gelu_parts(h[...])
            active[at, :] = value.astype(BF16)
            grads[at, :] = (back[...] * slope).astype(BF16)

        @pl.when(step < blocks)
        def _():
            first = step * (2 * pairs)

            def body(i, carry):
                products(2 * i, h_0, back_0)
                gelu(first + 2 * i - 1, h_1, back_1)
                products(2 * i + 1, h_1, back_1)
                gelu(first + 2 * i, h_0, back_0)
                return carry

            lax.fori_loop(0, pairs, body, 0)

        copies = [
            pltpu.make_async_copy(active, active_out, sems.at[0]),
            pltpu.make_async_copy(grads, hidden_out, sems.at[1]),
        ]

        @pl.when(step == blocks)
        def _():
            gelu(2 * pairs * blocks - 1, h_1, back_1)
            for copy in copies:
                copy.start()

        @pl.when(step >= blocks)
        def _():
            branch = jnp.dot(w_out_t_ref[...], active[...], preferred_element_type=F32)
            branch_ref[:, :cells] = (branch + b_out_ref[...]).astype(BF16)
            norm = jnp.dot(w_in_ref[...], grads[...], preferred_element_type=F32)
            norm_ref[...] = norm.astype(BF16)

        @pl.when(step == blocks + outs - 1)
        def _():
            for copy in copies:
                copy.wait()

    def at_in(f):
        return jnp.minimum(f, blocks - 1)

    def at_out(f):
        return jnp.maximum(f - blocks, 0)

    tall_block = pl.BlockSpec((block, packed), lambda f: (at_in(f), 0))
    wide_block = pl.BlockSpec((rows, hidden), lambda f: (at_out(f), 0))
    anywhere = pl.BlockSpec(memory_space=pl.ANY)
    operands = [normed, out_grad, w_in_t, w_in, w_out, w_out_t, b_in, b_out]
    in_specs = [
        whole((packed, cells)), lane_block(packed, length, part),
        tall_block, wide_block, tall_block, wide_block,
        pl.BlockSpec((block, 1), lambda f: (at_in(f), 0)),
        pl.BlockSpec((rows, 1), lambda f: (at_out(f), 0)),
    ]
    aliases = {}
    if branch_all is not None:
        aliases = {len(operands): 0}
        operands.append(branch_all)
        in_specs.append(anywhere)
    buffer = pltpu.VMEM((inner, cells), F32)
    return pl.pallas_call(
        kernel,
        grid=(blocks + outs,),
        in_specs=in_specs,
        out_specs=[
            pl.BlockSpec((rows, length), lambda f: (at_out(f), part)),
            pl.BlockSpec((rows, cells), lambda f: (at_out(f), 0)),
            anywhere, anywhere,
        ],
        out_shape=[
            jax.ShapeDtypeStruct(out_grad.shape, BF16),
            jax.ShapeDtypeStruct((packed, cells), BF16),
            jax.ShapeDtypeStruct((hidden, cells), BF16),
            jax.ShapeDtypeStruct((hidden, cells), BF16),
        ],
        scratch_shapes=[buffer] * 4
        + [pltpu.VMEM((hidden, cells), BF16)] * 2
        + [pltpu.SemaphoreType.DMA((2,))],
        input_output_aliases=aliases,
        compiler_params=params(),
        cost_estimate=cost(),
    )(*operands)


def weight_grad(core, lefts, rights):
    rows, hidden = lefts[0][0].shape[0], rights[0].shape[0]
    half = rows // CORES
    block = block_of(hidden, 640)
    arrays = []
    for array, _ in lefts:
        if not any(array is known for known in arrays):
            arrays.append(array)
    which = [next(k for k, known in enumerate(arrays) if known is array) for array, _ in lefts]

    def kernel(core_ref, *refs):
        mine_ref, sent_ref, both = refs[-3:]
        total = None
        for k, (_, start), right in zip(which, lefts, refs[len(arrays) : -3]):
            part = lax.dot_general(
                refs[k][:, start : start + right.shape[1]], right[...],
                (((1,), (1,)), ((), ())), preferred_element_type=F32,
            )
            total = part if total is None else total + part
        both[0] = total[:half].astype(BF16)
        both[1] = total[half:].astype(BF16)
        mine_ref[...] = both[core_ref[0]]
        sent_ref[...] = both[1 - core_ref[0]]

    out = jax.ShapeDtypeStruct((half, hidden), BF16)
    return pl.pallas_call(
        kernel,
        grid=(hidden // block,),
        in_specs=[smem()] + [whole(array.shape) for array in arrays]
        + [pl.BlockSpec((block, right.shape[1]), lambda f: (f, 0)) for right in rights],
        out_specs=[pl.BlockSpec((half, block), lambda f: (0, f))] * 2,
        out_shape=[out, out],
        scratch_shapes=[pltpu.VMEM((CORES, half, block), BF16)],
        compiler_params=params(),
        cost_estimate=cost(),
    )(core[None], *arrays, *rights)


def unpad_rows(z, place, turn, pieces, before):
    groups, hidden = pieces[0].shape[0] // z.pad, pieces[0].shape[1]
    before = [] if before is None else [before]

    def kernel(place_ref, *refs):
        out_ref = refs[-1]

        def put(ref):
            value = ref[...].astype(F32)
            for k in range(groups):
                out_ref[z.chan * k : z.chan * (k + 1), :] = value[z.pad * k : z.pad * k + z.chan, :]

        for k in range(2):
            pl.when(pl.program_id(0) == k)(partial(put, refs[k]))

    return pl.pallas_call(
        kernel,
        grid_spec=pltpu.PrefetchScalarGridSpec(
            num_scalar_prefetch=1,
            grid=(2,),
            in_specs=[pl.BlockSpec(pieces[0].shape, lambda k, place_ref: (0, 0))] * 2
            + [pl.BlockSpec(memory_space=pl.ANY)] * len(before),
            out_specs=pl.BlockSpec(
                (groups * z.chan, hidden),
                lambda k, place_ref: (jnp.bitwise_xor(2 * k + turn, place_ref[0]), 0),
            ),
        ),
        out_shape=jax.ShapeDtypeStruct((4 * groups * z.chan, hidden), F32),
        input_output_aliases={3: 0} if before else {},
        compiler_params=params(),
        cost_estimate=cost(),
    )(place[None], *pieces, *before)


def exchange(value):
    return lax.all_to_all(value, CHAN, split_axis=0, concat_axis=0, tiled=True)


def after(value, *others):
    return lax.optimization_barrier((value, *others))[0]


def dp_sum(value):
    ways = lax.axis_size("dp")
    total = value
    for turn in range(1, ways):
        total = total + lax.ppermute(value, "dp", [(i, i ^ turn) for i in range(ways)])
    return total


def swap_cores(value):
    return lax.ppermute(value, "core", [(0, 1), (1, 0)])


class HalvingSum:
    def __init__(self, turns, mine, sent):
        place = lax.axis_index("dp")
        self.turns = turns
        self.bits = [jnp.bitwise_and(place // turn, 1) for turn in turns]
        self.core = lax.axis_index("core")
        self.mine, self.other = mine, swap_cores(sent)

    def meet(self, value, turn):
        ways = lax.axis_size("dp")
        return lax.ppermute(value, "dp", [(i, i ^ turn) for i in range(ways)])

    def pair(self, half):
        rows = self.mine.shape[0] // 2
        at = half * rows
        return lax.dynamic_slice_in_dim(self.mine, at, rows, 0).astype(
            F32
        ) + lax.dynamic_slice_in_dim(self.other, at, rows, 0).astype(F32)

    def first(self, ready):
        self.mine = after(self.mine, ready)
        self.sent = self.pair(1 - self.bits[0]).astype(BF16)
        self.arrived = self.meet(self.sent, self.turns[0])

    def second(self, ready):
        arrived = after(self.arrived, ready)
        total = self.pair(self.bits[0]) + arrived.astype(F32)
        rows = total.shape[0] // 2
        send = lax.dynamic_slice_in_dim(total, (1 - self.bits[1]) * rows, rows, 0).astype(BF16)
        self.kept = lax.dynamic_slice_in_dim(total, self.bits[1] * rows, rows, 0)
        self.sent = send
        self.arrived = self.meet(send, self.turns[1])

    def share(self, ready):
        return (self.kept + after(self.arrived, ready).astype(F32)).astype(BF16)

    def back_first(self, share):
        self.own = share
        self.arrived = self.meet(share, self.turns[1])

    def back_second(self, ready):
        other = after(self.arrived, ready)
        low = self.bits[1] == 0
        self.own = jnp.concatenate(
            [jnp.where(low, self.own, other), jnp.where(low, other, self.own)], axis=0
        )
        self.arrived = self.meet(self.own, self.turns[0])
        self.swapped = swap_cores(self.own)

    def begin(self, z):
        self.place = self.core * 2 + self.bits[0]
        self.result = unpad_rows(z, self.place, 0, [self.own, self.swapped], None)
        return self.result

    def finish(self, z, ready):
        other = after(self.arrived, ready)
        swapped = swap_cores(other)
        self.pieces = [self.own, other, self.swapped, swapped]
        return unpad_rows(z, self.place, 1, [other, swapped], self.result)

    def first_row(self, row):
        found = self.pieces[0][row]
        for k in range(1, 4):
            found = jnp.where(self.place == k, self.pieces[k][row], found)
        return found.astype(F32)


def per_device(
    x_in, cotangent, land, grid_res, dw_kernel, gain, shift, res_bias, w_in, b_in, w_out, b_out
):
    samples, height, columns, chan = x_in.shape
    groups = lax.axis_size("pair") * CORES
    first = (lax.axis_index("pair") * CORES + lax.axis_index("core")) * chan
    width = chan * groups
    ntaps = dw_kernel.shape[0]
    z = Sizes(chan, height, columns, groups, ntaps)
    pixels = float(samples * lax.axis_size("dp") * height * columns)
    part = (z.units + 1) // 2 * LANES
    lengths = [part, z.units * LANES - part]
    starts = [0, part]

    def own(values, axis=0):
        return lax.dynamic_slice_in_dim(values, first, chan, axis)

    def over_lanes(rows):
        rows = jnp.pad(rows, ((0, 0), (0, z.pad - chan)))
        return jnp.broadcast_to(rows[:, :, None], rows.shape + (LANES,))

    x = jnp.transpose(x_in[0], (0, 2, 1))
    cot = jnp.transpose(cotangent[0], (0, 2, 1))
    land3 = land[0][:, None, :]

    grad_packed, part_b_out = pack_out_grad(z, sum(lengths), cot, land3)
    grad_band = exchange(grad_packed)

    taps = over_lanes(own(dw_kernel, 1).astype(F32))
    conv, total, square = conv_forward(z, taps, after(x, grad_packed))
    total, square = lax.psum((total, square), "dp")
    mean = total / pixels
    var = square / pixels - mean * mean
    scale = lax.rsqrt(var + 1e-05)
    own_gain = own(gain)
    chooser = (grid_res[:, None] == jnp.arange(2, dtype=jnp.int32)[None, :]).astype(F32)
    sample_bias = jnp.sum(chooser[0][:, None] * own(res_bias, 1), axis=0)
    affine = over_lanes(jnp.stack([mean, own_gain * scale, own(shift) + sample_bias]))
    packed = pack_normed(z, lengths, conv, affine)

    w_in_p, w_in_t = pad_weight(z, after(w_in, packed[0]))
    w_out_t, w_out_p = pad_weight(z, after(w_out.T, packed[0]))
    b_out_p = jnp.pad(b_out.reshape(groups, chan), ((0, 0), (0, z.pad - chan))).reshape(-1, 1)
    weights = (w_in_t, w_in_p, w_out_p, w_out_t, b_in[:, None], b_out_p)

    normed = [exchange(after(packed[0], grad_band))]
    normed.append(exchange(after(packed[1], normed[0], w_in_t, w_out_p)))
    branch, norm1, active1, hidden1 = mlp(0, part, normed[0], grad_band, *weights, None)
    norm_parts = [exchange(after(norm1, normed[1]))]
    branch, norm2, active2, hidden2 = mlp(1, part, normed[1], grad_band, *weights, branch)
    norm_parts.append(exchange(after(norm2, norm_parts[0])))
    core = lax.axis_index("core")
    mine, sent_out = weight_grad(
        core, [(grad_band, start) for start in starts], [active1, after(active2, norm_parts[0])]
    )
    sum_out = HalvingSum((1, 2), mine, sent_out)
    mine, sent_in = weight_grad(
        core, [(value, 0) for value in normed], [hidden1, after(hidden2, sent_out)]
    )
    sum_in = HalvingSum((2, 1), mine, sent_in)
    branch = exchange(after(branch, norm_parts[1], sent_in))

    part_shift, part_gain = norm_sums(z, norm_parts, conv, over_lanes(jnp.stack([mean, scale])))
    small = jnp.concatenate(
        [part_shift[None], part_gain[None], chooser[0][:, None] * part_shift[None], part_b_out[None]],
        axis=0,
    )
    small = lax.psum(small, "dp")
    terms = over_lanes(
        jnp.stack([mean, scale, own_gain * scale, small[0] / pixels, small[1] / pixels])
    )
    sum_out.first(small)
    sum_in.first(small)
    terms = after(terms, sum_out.sent, sum_in.sent)
    calls = pl.cdiv(chan, GROUP)
    cuts = [0, min(2, calls), min(4, calls), calls]
    cuts = [cut for k, cut in enumerate(cuts) if k == 0 or cut > cuts[k - 1]]
    made = conv_gradient(z, cuts[0], cuts[1], terms, norm_parts, conv, x, ntaps, None)
    sum_out.second(made[1])
    sum_in.second(made[1])
    if len(cuts) > 2:
        made = conv_gradient(
            z, cuts[1], cuts[2], after(terms, sum_out.sent, sum_in.sent), norm_parts, conv, x, ntaps, made
        )
    shares = sum_out.share(made[1]), sum_in.share(made[1])
    if len(cuts) > 3:
        made = conv_gradient(
            z, cuts[2], cuts[3], after(terms, *shares), norm_parts, conv, x, ntaps, made
        )
    conv_grad, products = made
    shares = lax.psum(shares, "pair")
    g_kernel = dp_sum(jnp.sum(products, axis=2)[:, :chan])
    x_grad = conv_backward(z, taps, conv_grad, cot, land3)
    sum_out.back_first(after(shares[0], x_grad))
    sum_in.back_first(after(shares[1], x_grad))
    rows = jnp.concatenate([after(g_kernel, sum_out.own, sum_in.own), small], axis=0)
    gathered = lax.all_gather(rows, CHAN)
    placed = jnp.transpose(gathered, (1, 0, 2)).reshape(rows.shape[0], width)
    sum_out.back_second(gathered)
    sum_in.back_second(gathered)

    def as_output(value):
        value = jnp.transpose(after(value, sum_out.own, sum_in.own), (0, 2, 1))[None]
        return with_layout_constraint(value, Layout(major_to_minor=(0, 3, 1, 2)))

    mixed = as_output(mix_branch(z, branch, after(x, sum_out.own, sum_in.own), land3))
    x_grad = as_output(x_grad)
    early = sum_out.begin(z), sum_in.begin(z)
    g_w_out_t = sum_out.finish(z, (mixed, x_grad, early))
    g_w_in = sum_in.finish(z, (mixed, x_grad, early))

    return (
        mixed,
        x_grad,
        placed[:ntaps],
        placed[ntaps + 1],
        placed[ntaps],
        placed[ntaps + 2 : ntaps + 4],
        g_w_in,
        sum_in.first_row(chan),
        g_w_out_t.T,
        placed[ntaps + 4],
    )


def solution(mesh):
    shape = mesh.shape
    mesh = jax.sharding.Mesh(
        mesh.devices.reshape(shape["dp"], shape["chan"] // CORES, CORES), ("dp",) + CHAN
    )
    cells = P("dp", None, None, CHAN)
    return jax.shard_map(
        per_device,
        mesh=mesh,
        in_specs=(cells, cells, P("dp", None, None), P("dp")) + (P(),) * 8,
        out_specs=(cells, cells) + (P(),) * 8,
        check_vma=False,
    )
```

```python
from functools import partial
import math

import jax
import jax.numpy as jnp
from jax import lax
from jax.experimental import pallas as pl
from jax.experimental.layout import Layout, with_layout_constraint
from jax.experimental.pallas import tpu as pltpu
from jax.sharding import PartitionSpec as P

LANES = 128
SUBL = 8
VMEM_LIMIT = 56 * 1024 * 1024
CHAN = ("pair", "core")
CORES = 2
F32 = jnp.float32
BF16 = jnp.bfloat16


def round_up(value, step):
    return (value + step - 1) // step * step


def block_of(total, most):
    return max(size for size in range(1, most + 1) if total % size == 0)


class Sizes:
    def __init__(self, chan, height, width, bands, taps):
        self.chan, self.height, self.width, self.bands = chan, height, width, bands
        self.side = math.isqrt(taps)
        self.margin = self.side // 2
        self.rows = height // bands
        self.wide = round_up(width + 2 * self.margin, LANES)
        self.tiles = self.wide // LANES
        self.tail = width - (self.tiles - 1) * LANES
        self.pad = round_up(chan + 1, SUBL)
        self.packed_rows = bands * self.pad
        self.tail_units = round_up(self.rows * self.tail, LANES) // LANES
        self.units = self.rows * (self.tiles - 1) + self.tail_units


def params(semantics=("arbitrary",)):
    return pltpu.CompilerParams(dimension_semantics=semantics, vmem_limit_bytes=VMEM_LIMIT)


def roll_tiles(z, tiles, shift):
    jump, low = divmod(shift % z.wide, LANES)
    count = z.tiles
    if low == 0:
        return [tiles[(j - jump) % count] for j in range(count)]
    lane = lax.broadcasted_iota(jnp.int32, tiles[0].shape, 1)
    moved = [pltpu.roll(tile, low, 1) for tile in tiles]
    return [
        jnp.where(lane < low, moved[(j - jump - 1) % count], moved[(j - jump) % count])
        for j in range(count)
    ]


def wrap_tiles(z, tiles):
    last = tiles[-1]
    lane = lax.broadcasted_iota(jnp.int32, last.shape, 1)
    ahead = pltpu.roll(tiles[0], z.tail, 1)
    behind = pltpu.roll(last, LANES - z.tail, 1)
    last = jnp.where(lane < z.tail, last, jnp.where(lane < z.tail + z.margin, ahead, behind))
    return tiles[:-1] + [last]


def row_tiles(z, value):
    tiles = [value[:, LANES * j : LANES * (j + 1)] for j in range(z.tiles - 1)]
    tail = value[:, LANES * (z.tiles - 1) :]
    zeros = jnp.zeros((value.shape[0], LANES - z.tail), F32)
    return tiles + [jnp.concatenate([tail, zeros], axis=1)]


def pack_tails(z, tails):
    lane = lax.broadcasted_iota(jnp.int32, tails[0].shape, 1)
    tiles = []
    for t in range(z.tail_units):
        begin, tile = LANES * t, None
        for row, tail in enumerate(tails):
            low = z.tail * row - begin
            if low >= LANES or low + z.tail <= 0:
                continue
            moved = pltpu.roll(tail, low % LANES, 1) if low % LANES else tail
            tile = moved if tile is None else jnp.where(lane >= low, moved, tile)
        end = z.tail * z.rows - begin
        tiles.append(jnp.where(lane < end, tile, 0.0) if end < LANES else tile)
    return tiles


def unpack_tails(z, tiles):
    lane = lax.broadcasted_iota(jnp.int32, tiles[0].shape, 1)
    tails = []
    for row in range(z.rows):
        t, low = divmod(z.tail * row, LANES)
        tail = pltpu.roll(tiles[t], LANES - low, 1) if low else tiles[t]
        if LANES - low < z.tail:
            tail = jnp.where(lane < LANES - low, tail, pltpu.roll(tiles[t + 1], LANES - low, 1))
        tails.append(jnp.where(lane < z.tail, tail, 0.0))
    return tails


def pack_rows(z, rows):
    full = z.tiles - 1
    return [row[j] for row in rows for j in range(full)] + pack_tails(z, [row[full] for row in rows])


def unpack_rows(z, tiles):
    full = z.tiles - 1
    tails = unpack_tails(z, tiles[z.rows * full :])
    return [tiles[row * full : (row + 1) * full] + [tails[row]] for row in range(z.rows)]


def packed_tiles(refs, read):
    return [
        read(ref, slice(LANES * k, LANES * (k + 1)))
        for ref in refs
        for k in range(ref.shape[-1] // LANES)
    ]


def whole(shape):
    return pl.BlockSpec(shape, lambda *_: (0,) * len(shape))


def smem():
    return pl.BlockSpec(memory_space=pltpu.SMEM)


def cost():
    return pl.CostEstimate(flops=1000, bytes_accessed=1000, transcendentals=0)


PAIR = 2
GROUP = 16


def pair_rows(z):
    return pl.BlockSpec((PAIR * z.rows, z.pad, z.width), lambda g: (g, 0, 0))


def pair_wide(z):
    return pl.BlockSpec((PAIR * z.rows, z.pad, z.wide), lambda g: (g, 0, 0))


def pair_land(z):
    return pl.BlockSpec((PAIR * z.rows, 1, z.width), lambda g: (g, 0, 0))


def pair_packed(z, cells):
    return pl.BlockSpec((PAIR * z.pad, cells), lambda g: (g, 0))


def group_rows(z):
    return pl.BlockSpec((z.height, GROUP, z.width), lambda c: (0, c, 0))


def group_wide(z):
    return pl.BlockSpec((z.height, GROUP, z.wide), lambda c: (0, c, 0))


def group_lanes(count):
    return pl.BlockSpec((count, GROUP, LANES), lambda c: (0, c, 0))


def write_pair(z, refs, bands):
    tiles = [jnp.concatenate(both, axis=0).astype(BF16) for both in zip(*bands)]
    unit = 0
    for ref in refs:
        for k in range(ref.shape[1] // LANES):
            ref[:, LANES * k : LANES * (k + 1)] = tiles[unit]
            unit += 1


def pack_out_grad(z, cells, cot, land):
    def kernel(cot_ref, land_ref, out_ref, sum_ref):
        @pl.when(pl.program_id(0) == 0)
        def _():
            sum_ref[...] = jnp.zeros_like(sum_ref)

        channel = lax.broadcasted_iota(jnp.int32, (z.pad, z.width), 0)
        total = jnp.zeros((z.pad, LANES), F32)
        bands = []
        for band in range(PAIR):
            rows = []
            for row in range(z.rows * band, z.rows * (band + 1)):
                value = cot_ref[row].astype(F32) * land_ref[row].astype(F32)
                rows.append(row_tiles(z, jnp.where(channel < z.chan, value, 0.0)))
                total = total + sum(rows[-1])
            bands.append(pack_rows(z, rows))
        sum_ref[...] += total
        write_pair(z, [out_ref], bands)

    out, sums = pl.pallas_call(
        kernel,
        grid=(z.bands // PAIR,),
        in_specs=[pair_rows(z), pair_land(z)],
        out_specs=[pair_packed(z, cells), whole((z.pad, LANES))],
        out_shape=[
            jax.ShapeDtypeStruct((z.packed_rows, cells), BF16),
            jax.ShapeDtypeStruct((z.pad, LANES), F32),
        ],
        compiler_params=params(),
        cost_estimate=cost(),
    )(cot, land)
    return out, jnp.sum(sums, axis=1)[: z.chan]


def fill_rows(z, target, read, wrap):
    zeros = jnp.zeros(target.shape[1:], F32)
    for k in range(z.margin):
        target[k] = zeros
        target[z.margin + z.height + k] = zeros

    def body(h, carry):
        tiles = row_tiles(z, read(h))
        if wrap:
            tiles = wrap_tiles(z, tiles)
        for j, tile in enumerate(tiles):
            target[z.margin + h, :, LANES * j : LANES * (j + 1)] = tile
        return carry

    lax.fori_loop(0, z.height, body, 0, unroll=8)


def convolve(z, steps, at, taps_ref, source, flip, put, carry):
    span = steps + 2 * z.margin

    def body(block, carry):
        h0 = block * steps
        rows = [
            [source[h0 + m, at, LANES * j : LANES * (j + 1)] for j in range(z.tiles)]
            for m in range(span)
        ]
        sums = [None] * steps
        for b in range(z.side):
            weights = [taps_ref[z.side * a + b, at, :] for a in range(z.side)]
            for r in range(steps):
                part = None
                for a in range(z.side):
                    row = rows[r + 2 * z.margin - a] if flip else rows[r + a]
                    terms = [weights[a] * tile for tile in row]
                    part = terms if part is None else [p + t for p, t in zip(part, terms)]
                part = roll_tiles(z, part, b - z.margin if flip else z.margin - b)
                sums[r] = part if b == 0 else [s + p for s, p in zip(sums[r], part)]
        for r in range(steps):
            carry = put(h0 + r, sums[r], carry)
        return carry

    return lax.fori_loop(0, z.height // steps, body, carry, unroll=3)


def conv_forward(z, taps, x):
    def kernel(taps_ref, x_ref, conv_ref, sum_ref, square_ref, source):
        fill_rows(z, source, lambda h: x_ref[h].astype(F32), True)
        lane = lax.broadcasted_iota(jnp.int32, (SUBL, LANES), 1)
        for part in range(GROUP // SUBL):
            at = slice(SUBL * part, SUBL * (part + 1))

            def put(h, tiles, carry):
                for j, tile in enumerate(tiles):
                    conv_ref[h, at, LANES * j : LANES * (j + 1)] = tile
                tiles = tiles[:-1] + [jnp.where(lane < z.tail, tiles[-1], 0.0)]
                return carry[0] + sum(tiles), carry[1] + sum(t * t for t in tiles)

            @pl.when(pl.program_id(0) * GROUP + SUBL * part < z.chan)
            def _():
                zero = jnp.zeros((SUBL, LANES), F32)
                total, square = convolve(z, 4, at, taps_ref, source, False, put, (zero, zero))
                sum_ref[at, :] = total
                square_ref[at, :] = square

    lane_spec = pl.BlockSpec((GROUP, LANES), lambda c: (c, 0))
    lane_shape = jax.ShapeDtypeStruct((z.pad, LANES), F32)
    conv, total, square = pl.pallas_call(
        kernel,
        grid=(pl.cdiv(z.chan, GROUP),),
        in_specs=[group_lanes(taps.shape[0]), group_rows(z)],
        out_specs=[group_wide(z), lane_spec, lane_spec],
        out_shape=[
            jax.ShapeDtypeStruct((z.height, z.pad, z.wide), F32), lane_shape, lane_shape,
        ],
        scratch_shapes=[pltpu.VMEM((z.height + 2 * z.margin, GROUP, z.wide), F32)],
        compiler_params=params(),
        cost_estimate=cost(),
    )(taps, x)
    return conv, jnp.sum(total, axis=1)[: z.chan], jnp.sum(square, axis=1)[: z.chan]


def pack_normed(z, lengths, conv, columns):
    def kernel(columns_ref, conv_ref, *outs):
        channel = lax.broadcasted_iota(jnp.int32, (z.pad, LANES), 0)
        filler = jnp.where(channel == z.chan, 1.0, 0.0)
        mean, factor, offset = columns_ref[0], columns_ref[1], columns_ref[2]
        bands = []
        for band in range(PAIR):
            rows = []
            for row in range(z.rows * band, z.rows * (band + 1)):
                tiles = [conv_ref[row, :, LANES * j : LANES * (j + 1)] for j in range(z.tiles)]
                rows.append(
                    [
                        jnp.where(channel < z.chan, (tile - mean) * factor + offset, filler)
                        for tile in tiles
                    ]
                )
            bands.append(pack_rows(z, rows))
        write_pair(z, outs, bands)

    return pl.pallas_call(
        kernel,
        grid=(z.bands // PAIR,),
        in_specs=[whole(columns.shape), pair_wide(z)],
        out_specs=[pair_packed(z, n) for n in lengths],
        out_shape=[jax.ShapeDtypeStruct((z.packed_rows, n), BF16) for n in lengths],
        compiler_params=params(),
        cost_estimate=cost(),
    )(columns, conv)


def norm_sums(z, parts, conv, columns):
    count = len(parts)

    def kernel(columns_ref, conv_ref, *rest):
        ins, (shift_ref, gain_ref) = rest[:count], rest[count:]

        @pl.when(pl.program_id(0) == 0)
        def _():
            shift_ref[...] = jnp.zeros_like(shift_ref)
            gain_ref[...] = jnp.zeros_like(gain_ref)

        mean = columns_ref[0]
        tiles = packed_tiles(ins, lambda ref, lanes: ref[:, lanes].astype(F32))
        shift = jnp.zeros((z.pad, LANES), F32)
        gain = jnp.zeros((z.pad, LANES), F32)
        for band in range(PAIR):
            rows = unpack_rows(z, [tile[z.pad * band : z.pad * (band + 1)] for tile in tiles])
            for row, grads in enumerate(rows):
                for j, grad in enumerate(grads):
                    value = conv_ref[z.rows * band + row, :, LANES * j : LANES * (j + 1)]
                    shift = shift + grad
                    gain = gain + grad * (value - mean)
        shift_ref[...] += shift
        gain_ref[...] += gain * columns_ref[1]

    lane_shape = jax.ShapeDtypeStruct((z.pad, LANES), F32)
    shift, gain = pl.pallas_call(
        kernel,
        grid=(z.bands // PAIR,),
        in_specs=[whole(columns.shape), pair_wide(z)] + [pair_packed(z, p.shape[1]) for p in parts],
        out_specs=[whole((z.pad, LANES))] * 2,
        out_shape=[lane_shape, lane_shape],
        compiler_params=params(),
        cost_estimate=cost(),
    )(columns, conv, *parts)
    return jnp.sum(shift, axis=1)[: z.chan], jnp.sum(gain, axis=1)[: z.chan]


def conv_gradient(z, begin, end, columns, parts, conv, x, ntaps, before):
    count = len(parts)
    parts = [part.reshape(z.bands, z.pad, part.shape[1]) for part in parts]
    steps = 4
    before = [] if before is None else list(before)

    def kernel(columns_ref, conv_ref, x_ref, *rest):
        ins, (grad_ref, product_ref, grads, source) = rest[:count], rest[-4:]
        mean, scale, factor, shift, gain = (columns_ref[k] for k in range(5))

        def band_body(band, carry):
            tiles = packed_tiles(ins, lambda ref, lanes: ref[band, :, lanes].astype(F32))
            for row, values in enumerate(unpack_rows(z, tiles)):
                h = band * z.rows + row
                made = []
                for j, value in enumerate(values):
                    centred = (conv_ref[h, :, LANES * j : LANES * (j + 1)] - mean) * scale
                    made.append(factor * (value - (shift + centred * gain)))
                for j, tile in enumerate(wrap_tiles(z, made)):
                    at = slice(LANES * j, LANES * (j + 1))
                    grads[h, :, at] = tile
                    grad_ref[h, :, at] = tile.astype(BF16)
            return carry

        lax.fori_loop(0, z.bands, band_body, 0)
        fill_rows(z, source, lambda h: x_ref[h].astype(F32), False)
        for part in range(GROUP // SUBL):
            at = slice(SUBL * part, SUBL * (part + 1))

            @pl.when((begin + pl.program_id(0)) * GROUP + SUBL * part < z.chan)
            def _():
                for b in range(z.side):

                    def body(block, totals):
                        h0 = block * steps
                        rows = [
                            [source[h0 + m, at, LANES * j : LANES * (j + 1)] for j in range(z.tiles)]
                            for m in range(steps + 2 * z.margin)
                        ]
                        totals = list(totals)
                        for r in range(steps):
                            moved = roll_tiles(
                                z,
                                [grads[h0 + r, at, LANES * j : LANES * (j + 1)] for j in range(z.tiles)],
                                b - z.margin,
                            )
                            for a in range(z.side):
                                for m, tile in zip(moved, rows[r + a]):
                                    totals[a] = totals[a] + m * tile
                        return tuple(totals)

                    zero = jnp.zeros((SUBL, LANES), F32)
                    totals = lax.fori_loop(0, z.height // steps, body, (zero,) * z.side, unroll=6)
                    for a in range(z.side):
                        product_ref[z.side * a + b, at, :] = totals[a]

    def group(shape):
        return pl.BlockSpec(shape, lambda c: (0, begin + c, 0))

    operands = [columns, conv, x, *parts, *before]
    return pl.pallas_call(
        kernel,
        grid=(end - begin,),
        in_specs=[
            group((5, GROUP, LANES)), group((z.height, GROUP, z.wide)),
            group((z.height, GROUP, z.width)),
        ]
        + [group((z.bands, GROUP, p.shape[2])) for p in parts]
        + [pl.BlockSpec(memory_space=pl.ANY)] * len(before),
        out_specs=[group((z.height, GROUP, z.wide)), group((ntaps, GROUP, LANES))],
        out_shape=[
            jax.ShapeDtypeStruct((z.height, z.pad, z.wide), BF16),
            jax.ShapeDtypeStruct((ntaps, z.pad, LANES), F32),
        ],
        scratch_shapes=[
            pltpu.VMEM((z.height, GROUP, z.wide), F32),
            pltpu.VMEM((z.height + 2 * z.margin, GROUP, z.wide), F32),
        ],
        input_output_aliases={len(operands) - 2 + k: k for k in range(len(before))},
        compiler_params=params(),
        cost_estimate=cost(),
    )(*operands)


def conv_backward(z, taps, grad, cot, land):
    def kernel(taps_ref, grad_ref, cot_ref, land_ref, out_ref, source, result):
        zeros = jnp.zeros(source.shape[1:], F32)
        for k in range(z.margin):
            source[k] = zeros
            source[z.margin + z.height + k] = zeros

        def fill(h, carry):
            source[z.margin + h] = grad_ref[h].astype(F32)
            return carry

        lax.fori_loop(0, z.height, fill, 0, unroll=8)
        for part in range(GROUP // SUBL):
            at = slice(SUBL * part, SUBL * (part + 1))

            def put(h, tiles, carry):
                for j, tile in enumerate(tiles):
                    result[h, at, LANES * j : LANES * (j + 1)] = tile
                return carry

            @pl.when(pl.program_id(0) * GROUP + SUBL * part < z.chan)
            def _():
                convolve(z, 4, at, taps_ref, source, True, put, 0)

        def finish(h, carry):
            direct = cot_ref[h].astype(F32) * land_ref[h].astype(F32)
            out_ref[h] = (direct + result[h][:, : z.width]).astype(BF16)
            return carry

        lax.fori_loop(0, z.height, finish, 0, unroll=8)

    return pl.pallas_call(
        kernel,
        grid=(pl.cdiv(z.chan, GROUP),),
        in_specs=[
            group_lanes(taps.shape[0]), group_wide(z), group_rows(z),
            whole((z.height, 1, z.width)),
        ],
        out_specs=group_rows(z),
        out_shape=jax.ShapeDtypeStruct((z.height, z.chan, z.width), BF16),
        scratch_shapes=[
            pltpu.VMEM((z.height + 2 * z.margin, GROUP, z.wide), F32),
            pltpu.VMEM((z.height, GROUP, z.wide), F32),
        ],
        compiler_params=params(),
        cost_estimate=cost(),
    )(taps, grad, cot, land)


def mix_branch(z, branch, x, land):
    def kernel(x_ref, land_ref, branch_ref, out_ref):
        tiles = packed_tiles([branch_ref], lambda ref, lanes: ref[:, lanes].astype(F32))
        for band in range(PAIR):
            rows = unpack_rows(z, [tile[z.pad * band : z.pad * (band + 1)] for tile in tiles])
            for k, row in enumerate(rows):
                h = z.rows * band + k
                value = jnp.concatenate(row, axis=1)[:, : z.width]
                value = land_ref[h].astype(F32) * (x_ref[h].astype(F32) + value)
                out_ref[h] = value.astype(BF16)

    return pl.pallas_call(
        kernel,
        grid=(z.bands // PAIR,),
        in_specs=[pair_rows(z), pair_land(z), pair_packed(z, branch.shape[1])],
        out_specs=pair_rows(z),
        out_shape=jax.ShapeDtypeStruct((z.height, z.chan, z.width), BF16),
        compiler_params=params(),
        cost_estimate=cost(),
    )(x, land, branch)


def gelu_parts(h):
    span = 1.0 + (0.3275911 * math.sqrt(0.5)) * jnp.abs(h)
    t = pl.reciprocal(span, approx=True)
    t = t * (2.0 - span * t)
    bell = jnp.exp2((-0.5 / math.log(2.0)) * (h * h))
    poly = t * (
        0.5 * 0.254829592
        + t
        * (
            0.5 * -0.284496736
            + t * (0.5 * 1.421413741 + t * (0.5 * -1.453152027 + t * (0.5 * 1.061405429)))
        )
    )
    tail = poly * bell
    phi = jnp.where(h >= 0, 1.0 - tail, tail)
    return h * phi, phi + h * ((1.0 / math.sqrt(2.0 * math.pi)) * bell)


def pad_weight(z, matrix):
    groups, hidden = matrix.shape[0] // z.chan, matrix.shape[1]
    block = block_of(hidden, 640)
    rows = groups * z.pad

    def kernel(in_ref, out_ref, transposed_ref, wide):
        value = in_ref[...].astype(F32)
        zeros = jnp.zeros((z.pad - z.chan, block), F32)
        for k in range(groups):
            wide[z.pad * k : z.pad * (k + 1), :] = jnp.concatenate(
                [value[z.chan * k : z.chan * (k + 1), :], zeros], axis=0
            )
        padded = wide[...]
        out_ref[...] = padded.astype(BF16)
        transposed_ref[...] = padded.T.astype(BF16)

    return pl.pallas_call(
        kernel,
        grid=(hidden // block,),
        in_specs=[pl.BlockSpec((groups * z.chan, block), lambda f: (0, f))],
        out_specs=[
            pl.BlockSpec((rows, block), lambda f: (0, f)),
            pl.BlockSpec((block, rows), lambda f: (f, 0)),
        ],
        out_shape=[
            jax.ShapeDtypeStruct((rows, hidden), BF16),
            jax.ShapeDtypeStruct((hidden, rows), BF16),
        ],
        scratch_shapes=[pltpu.VMEM((rows, block), F32)],
        compiler_params=params(),
        cost_estimate=cost(),
    )(matrix)


def lane_block(rows, cells, part):
    return pl.BlockSpec((rows, cells), lambda *_: (0, part))


def row_step(rows, most):
    return max(n for n in range(16, most + 1, 16) if rows % n == 0)


def mlp(part, length, normed, out_grad, w_in_t, w_in, w_out, w_out_t, b_in, b_out, branch_all):
    packed, cells = normed.shape
    hidden = w_in_t.shape[0]
    block = block_of(hidden, 640)
    inner = row_step(block, 320)
    blocks = hidden // block
    pairs = block // inner // 2
    rows = row_step(packed, 416)
    outs = packed // rows

    def kernel(
        n_ref, g_ref, w_in_t_ref, w_in_ref, w_out_ref, w_out_t_ref, b_in_ref, b_out_ref, *rest
    ):
        (
            branch_ref, norm_ref, active_out, hidden_out,
            h_0, h_1, back_0, back_1, active, grads, sems,
        ) = rest[-11:]
        step = pl.program_id(0)

        def products(k, h, back):
            at = pl.ds(k * inner, inner)
            h[...] = (
                jnp.dot(w_in_t_ref[at, :], n_ref[...], preferred_element_type=F32) + b_in_ref[at, :]
            )
            back[...] = jnp.dot(w_out_ref[at, :], g_ref[:, :cells], preferred_element_type=F32)

        def gelu(k, h, back):
            at = pl.ds(pl.multiple_of(jnp.maximum(k, 0) * inner, inner), inner)
            value, slope = gelu_parts(h[...])
            active[at, :] = value.astype(BF16)
            grads[at, :] = (back[...] * slope).astype(BF16)

        @pl.when(step < blocks)
        def _():
            first = step * (2 * pairs)

            def body(i, carry):
                products(2 * i, h_0, back_0)
                gelu(first + 2 * i - 1, h_1, back_1)
                products(2 * i + 1, h_1, back_1)
                gelu(first + 2 * i, h_0, back_0)
                return carry

            lax.fori_loop(0, pairs, body, 0)

        copies = [
            pltpu.make_async_copy(active, active_out, sems.at[0]),
            pltpu.make_async_copy(grads, hidden_out, sems.at[1]),
        ]

        @pl.when(step == blocks)
        def _():
            gelu(2 * pairs * blocks - 1, h_1, back_1)
            for copy in copies:
                copy.start()

        @pl.when(step >= blocks)
        def _():
            branch = jnp.dot(w_out_t_ref[...], active[...], preferred_element_type=F32)
            branch_ref[:, :cells] = (branch + b_out_ref[...]).astype(BF16)
            norm = jnp.dot(w_in_ref[...], grads[...], preferred_element_type=F32)
            norm_ref[...] = norm.astype(BF16)

        @pl.when(step == blocks + outs - 1)
        def _():
            for copy in copies:
                copy.wait()

    def at_in(f):
        return jnp.minimum(f, blocks - 1)

    def at_out(f):
        return jnp.maximum(f - blocks, 0)

    tall_block = pl.BlockSpec((block, packed), lambda f: (at_in(f), 0))
    wide_block = pl.BlockSpec((rows, hidden), lambda f: (at_out(f), 0))
    anywhere = pl.BlockSpec(memory_space=pl.ANY)
    operands = [normed, out_grad, w_in_t, w_in, w_out, w_out_t, b_in, b_out]
    in_specs = [
        whole((packed, cells)), lane_block(packed, length, part),
        tall_block, wide_block, tall_block, wide_block,
        pl.BlockSpec((block, 1), lambda f: (at_in(f), 0)),
        pl.BlockSpec((rows, 1), lambda f: (at_out(f), 0)),
    ]
    aliases = {}
    if branch_all is not None:
        aliases = {len(operands): 0}
        operands.append(branch_all)
        in_specs.append(anywhere)
    buffer = pltpu.VMEM((inner, cells), F32)
    return pl.pallas_call(
        kernel,
        grid=(blocks + outs,),
        in_specs=in_specs,
        out_specs=[
            pl.BlockSpec((rows, length), lambda f: (at_out(f), part)),
            pl.BlockSpec((rows, cells), lambda f: (at_out(f), 0)),
            anywhere, anywhere,
        ],
        out_shape=[
            jax.ShapeDtypeStruct(out_grad.shape, BF16),
            jax.ShapeDtypeStruct((packed, cells), BF16),
            jax.ShapeDtypeStruct((hidden, cells), BF16),
            jax.ShapeDtypeStruct((hidden, cells), BF16),
        ],
        scratch_shapes=[buffer] * 4
        + [pltpu.VMEM((hidden, cells), BF16)] * 2
        + [pltpu.SemaphoreType.DMA((2,))],
        input_output_aliases=aliases,
        compiler_params=params(),
        cost_estimate=cost(),
    )(*operands)


def weight_grad(core, lefts, rights):
    rows, hidden = lefts[0][0].shape[0], rights[0].shape[0]
    half = rows // CORES
    block = block_of(hidden, 640)
    arrays = []
    for array, _ in lefts:
        if not any(array is known for known in arrays):
            arrays.append(array)
    which = [next(k for k, known in enumerate(arrays) if known is array) for array, _ in lefts]

    def kernel(core_ref, *refs):
        mine_ref, sent_ref, both = refs[-3:]
        total = None
        for k, (_, start), right in zip(which, lefts, refs[len(arrays) : -3]):
            part = lax.dot_general(
                refs[k][:, start : start + right.shape[1]], right[...],
                (((1,), (1,)), ((), ())), preferred_element_type=F32,
            )
            total = part if total is None else total + part
        both[0] = total[:half].astype(BF16)
        both[1] = total[half:].astype(BF16)
        mine_ref[...] = both[core_ref[0]]
        sent_ref[...] = both[1 - core_ref[0]]

    out = jax.ShapeDtypeStruct((half, hidden), BF16)
    return pl.pallas_call(
        kernel,
        grid=(hidden // block,),
        in_specs=[smem()] + [whole(array.shape) for array in arrays]
        + [pl.BlockSpec((block, right.shape[1]), lambda f: (f, 0)) for right in rights],
        out_specs=[pl.BlockSpec((half, block), lambda f: (0, f))] * 2,
        out_shape=[out, out],
        scratch_shapes=[pltpu.VMEM((CORES, half, block), BF16)],
        compiler_params=params(),
        cost_estimate=cost(),
    )(core[None], *arrays, *rights)


def unpad_rows(z, place, turn, pieces, before):
    groups, hidden = pieces[0].shape[0] // z.pad, pieces[0].shape[1]
    before = [] if before is None else [before]

    def kernel(place_ref, *refs):
        out_ref = refs[-1]

        def put(ref):
            value = ref[...].astype(F32)
            for k in range(groups):
                out_ref[z.chan * k : z.chan * (k + 1), :] = value[z.pad * k : z.pad * k + z.chan, :]

        for k in range(2):
            pl.when(pl.program_id(0) == k)(partial(put, refs[k]))

    return pl.pallas_call(
        kernel,
        grid_spec=pltpu.PrefetchScalarGridSpec(
            num_scalar_prefetch=1,
            grid=(2,),
            in_specs=[pl.BlockSpec(pieces[0].shape, lambda k, place_ref: (0, 0))] * 2
            + [pl.BlockSpec(memory_space=pl.ANY)] * len(before),
            out_specs=pl.BlockSpec(
                (groups * z.chan, hidden),
                lambda k, place_ref: (jnp.bitwise_xor(2 * k + turn, place_ref[0]), 0),
            ),
        ),
        out_shape=jax.ShapeDtypeStruct((4 * groups * z.chan, hidden), F32),
        input_output_aliases={3: 0} if before else {},
        compiler_params=params(),
        cost_estimate=cost(),
    )(place[None], *pieces, *before)


def exchange(value):
    return lax.all_to_all(value, CHAN, split_axis=0, concat_axis=0, tiled=True)


def after(value, *others):
    return lax.optimization_barrier((value, *others))[0]


def dp_sum(value):
    ways = lax.axis_size("dp")
    total = value
    for turn in range(1, ways):
        total = total + lax.ppermute(value, "dp", [(i, i ^ turn) for i in range(ways)])
    return total


def swap_cores(value):
    return lax.ppermute(value, "core", [(0, 1), (1, 0)])


class HalvingSum:
    def __init__(self, turns, mine, sent):
        place = lax.axis_index("dp")
        self.turns = turns
        self.bits = [jnp.bitwise_and(place // turn, 1) for turn in turns]
        self.core = lax.axis_index("core")
        self.mine, self.other = mine, swap_cores(sent)

    def meet(self, value, turn):
        ways = lax.axis_size("dp")
        return lax.ppermute(value, "dp", [(i, i ^ turn) for i in range(ways)])

    def pair(self, half):
        rows = self.mine.shape[0] // 2
        at = half * rows
        return lax.dynamic_slice_in_dim(self.mine, at, rows, 0).astype(
            F32
        ) + lax.dynamic_slice_in_dim(self.other, at, rows, 0).astype(F32)

    def first(self, ready):
        self.mine = after(self.mine, ready)
        self.sent = self.pair(1 - self.bits[0]).astype(BF16)
        self.arrived = self.meet(self.sent, self.turns[0])

    def second(self, ready):
        arrived = after(self.arrived, ready)
        total = self.pair(self.bits[0]) + arrived.astype(F32)
        rows = total.shape[0] // 2
        send = lax.dynamic_slice_in_dim(total, (1 - self.bits[1]) * rows, rows, 0).astype(BF16)
        self.kept = lax.dynamic_slice_in_dim(total, self.bits[1] * rows, rows, 0)
        self.sent = send
        self.arrived = self.meet(send, self.turns[1])

    def share(self, ready):
        return (self.kept + after(self.arrived, ready).astype(F32)).astype(BF16)

    def back_first(self, share):
        self.own = share
        self.arrived = self.meet(share, self.turns[1])

    def back_second(self, ready):
        other = after(self.arrived, ready)
        low = self.bits[1] == 0
        self.own = jnp.concatenate(
            [jnp.where(low, self.own, other), jnp.where(low, other, self.own)], axis=0
        )
        self.arrived = self.meet(self.own, self.turns[0])
        self.swapped = swap_cores(self.own)

    def begin(self, z):
        self.place = self.core * 2 + self.bits[0]
        self.result = unpad_rows(z, self.place, 0, [self.own, self.swapped], None)
        return self.result

    def finish(self, z, ready):
        other = after(self.arrived, ready)
        swapped = swap_cores(other)
        self.pieces = [self.own, other, self.swapped, swapped]
        return unpad_rows(z, self.place, 1, [other, swapped], self.result)

    def first_row(self, row):
        found = self.pieces[0][row]
        for k in range(1, 4):
            found = jnp.where(self.place == k, self.pieces[k][row], found)
        return found.astype(F32)


def per_device(
    x_in, cotangent, land, grid_res, dw_kernel, gain, shift, res_bias, w_in, b_in, w_out, b_out
):
    samples, height, columns, chan = x_in.shape
    groups = lax.axis_size("pair") * CORES
    first = (lax.axis_index("pair") * CORES + lax.axis_index("core")) * chan
    width = chan * groups
    ntaps = dw_kernel.shape[0]
    z = Sizes(chan, height, columns, groups, ntaps)
    pixels = float(samples * lax.axis_size("dp") * height * columns)
    part = (z.units + 1) // 2 * LANES
    lengths = [part, z.units * LANES - part]
    starts = [0, part]

    def own(values, axis=0):
        return lax.dynamic_slice_in_dim(values, first, chan, axis)

    def over_lanes(rows):
        rows = jnp.pad(rows, ((0, 0), (0, z.pad - chan)))
        return jnp.broadcast_to(rows[:, :, None], rows.shape + (LANES,))

    x = jnp.transpose(x_in[0], (0, 2, 1))
    cot = jnp.transpose(cotangent[0], (0, 2, 1))
    land3 = land[0][:, None, :]

    grad_packed, part_b_out = pack_out_grad(z, sum(lengths), cot, land3)
    grad_band = exchange(grad_packed)

    taps = over_lanes(own(dw_kernel, 1).astype(F32))
    conv, total, square = conv_forward(z, taps, after(x, grad_packed))
    total, square = lax.psum((total, square), "dp")
    mean = total / pixels
    var = square / pixels - mean * mean
    scale = lax.rsqrt(var + 1e-05)
    own_gain = own(gain)
    chooser = (grid_res[:, None] == jnp.arange(2, dtype=jnp.int32)[None, :]).astype(F32)
    sample_bias = jnp.sum(chooser[0][:, None] * own(res_bias, 1), axis=0)
    affine = over_lanes(jnp.stack([mean, own_gain * scale, own(shift) + sample_bias]))
    packed = pack_normed(z, lengths, conv, affine)

    w_in_p, w_in_t = pad_weight(z, after(w_in, packed[0]))
    w_out_t, w_out_p = pad_weight(z, after(w_out.T, packed[0]))
    b_out_p = jnp.pad(b_out.reshape(groups, chan), ((0, 0), (0, z.pad - chan))).reshape(-1, 1)
    weights = (w_in_t, w_in_p, w_out_p, w_out_t, b_in[:, None], b_out_p)

    normed = [exchange(after(packed[0], grad_band))]
    normed.append(exchange(after(packed[1], normed[0], w_in_t, w_out_p)))
    branch, norm1, active1, hidden1 = mlp(0, part, normed[0], grad_band, *weights, None)
    norm_parts = [exchange(after(norm1, normed[1]))]
    branch, norm2, active2, hidden2 = mlp(1, part, normed[1], grad_band, *weights, branch)
    norm_parts.append(exchange(after(norm2, norm_parts[0])))
    core = lax.axis_index("core")
    mine, sent_out = weight_grad(
        core, [(grad_band, start) for start in starts], [active1, after(active2, norm_parts[0])]
    )
    sum_out = HalvingSum((1, 2), mine, sent_out)
    mine, sent_in = weight_grad(
        core, [(value, 0) for value in normed], [hidden1, after(hidden2, sent_out)]
    )
    sum_in = HalvingSum((2, 1), mine, sent_in)
    branch = exchange(after(branch, norm_parts[1], sent_in))

    part_shift, part_gain = norm_sums(z, norm_parts, conv, over_lanes(jnp.stack([mean, scale])))
    small = jnp.concatenate(
        [part_shift[None], part_gain[None], chooser[0][:, None] * part_shift[None], part_b_out[None]],
        axis=0,
    )
    small = lax.psum(small, "dp")
    terms = over_lanes(
        jnp.stack([mean, scale, own_gain * scale, small[0] / pixels, small[1] / pixels])
    )
    sum_out.first(small)
    sum_in.first(small)
    terms = after(terms, sum_out.sent, sum_in.sent)
    calls = pl.cdiv(chan, GROUP)
    cuts = [0, min(2, calls), min(4, calls), calls]
    cuts = [cut for k, cut in enumerate(cuts) if k == 0 or cut > cuts[k - 1]]
    made = conv_gradient(z, cuts[0], cuts[1], terms, norm_parts, conv, x, ntaps, None)
    sum_out.second(made[1])
    sum_in.second(made[1])
    if len(cuts) > 2:
        made = conv_gradient(
            z, cuts[1], cuts[2], after(terms, sum_out.sent, sum_in.sent), norm_parts, conv, x, ntaps, made
        )
    shares = sum_out.share(made[1]), sum_in.share(made[1])
    if len(cuts) > 3:
        made = conv_gradient(
            z, cuts[2], cuts[3], after(terms, *shares, branch), norm_parts, conv, x, ntaps, made
        )
    conv_grad, products = made
    shares = lax.psum((after(shares[0], branch), after(shares[1], branch)), "pair")
    g_kernel = dp_sum(jnp.sum(products, axis=2)[:, :chan])
    x_grad = conv_backward(z, taps, conv_grad, cot, land3)
    sum_out.back_first(after(shares[0], x_grad, g_kernel))
    sum_in.back_first(after(shares[1], x_grad, g_kernel))
    rows = jnp.concatenate([after(g_kernel, sum_out.own, sum_in.own), small], axis=0)
    gathered = lax.all_gather(rows, CHAN)
    placed = jnp.transpose(gathered, (1, 0, 2)).reshape(rows.shape[0], width)
    sum_out.back_second(gathered)
    sum_in.back_second(gathered)

    def as_output(value):
        value = jnp.transpose(after(value, sum_out.own, sum_in.own), (0, 2, 1))[None]
        return with_layout_constraint(value, Layout(major_to_minor=(0, 3, 1, 2)))

    mixed = as_output(mix_branch(z, branch, after(x, sum_out.own, sum_in.own), land3))
    x_grad = as_output(x_grad)
    early = sum_out.begin(z), sum_in.begin(z)
    g_w_out_t = sum_out.finish(z, (mixed, x_grad, early))
    g_w_in = sum_in.finish(z, (mixed, x_grad, early))

    return (
        mixed,
        x_grad,
        placed[:ntaps],
        placed[ntaps + 1],
        placed[ntaps],
        placed[ntaps + 2 : ntaps + 4],
        g_w_in,
        sum_in.first_row(chan),
        g_w_out_t.T,
        placed[ntaps + 4],
    )


def solution(mesh):
    shape = mesh.shape
    mesh = jax.sharding.Mesh(
        mesh.devices.reshape(shape["dp"], shape["chan"] // CORES, CORES), ("dp",) + CHAN
    )
    cells = P("dp", None, None, CHAN)
    return jax.shard_map(
        per_device,
        mesh=mesh,
        in_specs=(cells, cells, P("dp", None, None), P("dp")) + (P(),) * 8,
        out_specs=(cells, cells) + (P(),) * 8,
        check_vma=False,
    )
```
